256 devices in a mesh: segment: 32 (over z_hi, x, core), tensor: 8 (over y, z_lo).
Axes of the slice: x: 4, y: 4, z: 8 (z_hi: 4, z_lo: 2; z = z_hi * 2 + z_lo), core: 2. Of those that a mesh axis runs over, the one named last changes fastest.
Arguments:
- queries: bfloat16 [32, 256, 8192], P('segment', None, 'tensor'), may hold values from -1280 to 1280
- grad_attended: bfloat16 [32, 256, 8192], P('segment', None, 'tensor'), may hold values from -6 to 6
- vision: bfloat16 [512, 8192], P('segment', 'tensor'), may hold values from -6 to 6
- key_weight: bfloat16 [32, 4096, 1024], P('segment', None, 'tensor'), may hold values from -1 to 1
- value_weight: bfloat16 [32, 4096, 1024], P('segment', None, 'tensor'), may hold values from -0.0625 to 0.0625
- tile_limit: int32 [512], replicated, may hold values from 1 to 4
Outputs:
- attended: bfloat16 [32, 256, 8192], P('segment', None, 'tensor')
- grad_queries: bfloat16 [32, 256, 8192], P('segment', None, 'tensor')
- grad_vision: float32 [512, 8192], P('segment', 'tensor')
The draws below stay inside these ranges and needn't reach their ends.
Inputs may be any that keep to these rules, and one draw needn't show every extreme that they name: Text token t sees image tokens 0 to tile_limit[t] * 128 - 1.
All inputs are finite; a program needn't handle non-finite values.
Results may differ from the reference program's by a relative error of at most 0.035.
The reference program's roundings to bfloat16 on the way count: a program that leaves them out, or rounds other values in their place, can miss the bound.
Values may be sent and summed in bfloat16 or wider, within the bound.
A program may use at most 128 MiB of HBM per device.

```python
import jax
import jax.numpy as jnp
from jax import lax

HEADS = 64
KV = 8
HD = 128
VW = 8192
TEXT_TOK = 256
TILES = 4
MB_TOK = 512
VIS = 512
SECTIONS = 32


def vision_field(key):
    noise = jax.random.normal(jax.random.fold_in(key, 101), (VIS, VW), jnp.float32)
    return jnp.clip(noise, -6.0, 6.0).astype(jnp.bfloat16)


def key_field(key):
    noise = jax.random.uniform(jax.random.fold_in(key, 202), (SECTIONS, VW // 2, KV * HD), jnp.float32, -1.0, 1.0)
    return (noise * (3.0 / VW) ** 0.5).astype(jnp.bfloat16)


def draw_vision(key, part):
    shared = vision_field(key)
    return shared


def draw_key_weight(key, part):
    shared = key_field(key)
    return shared


def draw_queries(key, part):
    key = jax.random.fold_in(key, 3)
    noise = jax.random.normal(jax.random.fold_in(key, 1), (SECTIONS, TEXT_TOK, HEADS * HD), jnp.float32)
    result = jnp.clip(2.0 * noise, -12.0, 12.0)
    return result.astype(jnp.bfloat16)


def with_ends(values, rng, least, top_value):
    place = [jax.random.randint(jax.random.fold_in(rng, axis), (), 0, length) for axis, length in enumerate(values.shape)]
    main_axis = values.shape.index(max(values.shape))
    neighbour = place[:main_axis] + [(place[main_axis] + 1) % values.shape[main_axis]] + place[main_axis + 1:]
    return values.at[tuple(place)].set(least).at[tuple(neighbour)].set(top_value)


def levels(rng, dims, split, least, largest):
    loudness, own = 1.0, jax.random.fold_in(rng, 6)
    for dim, blocks in split:
        draws = jnp.exp(jax.random.uniform(jax.random.fold_in(own, dim), (blocks,), jnp.float32, least / len(split), largest / len(split)))
        loudness = loudness * jnp.repeat(draws, dims[dim] // blocks).reshape([-1 if axis == dim else 1 for axis in range(len(dims))])
    return loudness


def normal_values(own_key, dims, width, most, cuts=(), kind=jnp.bfloat16):
    values = jax.random.normal(own_key, dims, jnp.float32) * width
    if len(cuts) > 0:
        values = levels(own_key, dims, cuts, -0.22, 0.18) * values
    return jnp.clip(values, min=-most, max=most).astype(kind)


def setup_inputs(seed: int = 0) -> dict:
    splits = jax.random.split(jax.random.key(seed), 7)
    return {
        "queries": draw_queries(jax.random.fold_in(splits[6], 71), 0),
        "grad_attended": normal_values(splits[1], (SECTIONS, TEXT_TOK, HEADS * HD), 1.0, 6.0, ((0, 32), (2, 8))),
        "vision": draw_vision(jax.random.fold_in(splits[6], 71), 0),
        "key_weight": draw_key_weight(jax.random.fold_in(splits[6], 71), 0),
        "value_weight": normal_values(splits[4], (SECTIONS, VW // 2, KV * HD), VW ** -0.5, 0.0625, ((0, 32), (2, 8))),
        "tile_limit": with_ends(jax.random.randint(splits[5], (MB_TOK,), 1, TILES + 1), jax.random.fold_in(splits[5], 1), 1, TILES).astype(jnp.int32),
    }


epsilon = 1e-05

def normalize(pre):
    return pre * lax.rsqrt(lax.optimization_barrier(jnp.mean(pre * pre, axis=-1, keepdims=True)) + epsilon)

def attend(query, grad_out, keys, values, limit, tile_tokens):
    score_scale = HD ** (-0.5)
    query_f = query.astype(jnp.float32)
    grad_f = grad_out.astype(jnp.float32)
    keys_f = keys.astype(jnp.float32)
    values_f = values.astype(jnp.float32)
    scores = jnp.einsum('rkgd,nkd->rkgn', query_f, keys_f) * score_scale
    positions = jnp.arange(keys.shape[0], dtype=jnp.int32)
    allowed = (positions[None, :] < (limit * tile_tokens)[:, None])[:, None, None, :]
    scores = jnp.where(allowed, scores, -1e+30)
    row_max = lax.optimization_barrier(jnp.max(scores, axis=-1, keepdims=True))
    shifted = jnp.exp(scores - row_max)
    probability = shifted / lax.optimization_barrier(jnp.sum(shifted, axis=-1, keepdims=True))
    prob_low = probability.astype(jnp.bfloat16)
    output = jnp.einsum('rkgn,nkd->rkgd', prob_low.astype(jnp.float32), values_f).astype(jnp.bfloat16)
    grad_prob = jnp.einsum('rkgd,nkd->rkgn', grad_f, values_f)
    delta = lax.optimization_barrier(jnp.sum(grad_f * output.astype(jnp.float32), axis=-1, keepdims=True))
    grad_score = (probability * (grad_prob - delta)).astype(jnp.bfloat16).astype(jnp.float32)
    grad_query = (jnp.einsum('rkgn,nkd->rkgd', grad_score, keys_f) * score_scale).astype(jnp.bfloat16)
    grad_keys = jnp.einsum('rkgn,rkgd->nkd', grad_score, query_f) * score_scale
    grad_values = jnp.einsum('rkgn,rkgd->nkd', prob_low.astype(jnp.float32), grad_f)
    return (output, grad_query, grad_keys, grad_values)

def reference(queries, grad_attended, vision, key_weight, value_weight, tile_limit):
    vis_total = vision.shape[0]
    tile_tokens = vis_total // TILES
    group = HEADS // KV
    half_rows = queries.shape[1]
    layer_count = queries.shape[0] // 2
    full_width = 2 * key_weight.shape[1]
    key_layers = key_weight.reshape(layer_count, full_width, KV * HD)
    value_layers = value_weight.reshape(layer_count, full_width, KV * HD)
    query_pairs = queries.reshape(layer_count, 2, half_rows, HEADS * HD)
    grad_pairs = grad_attended.reshape(layer_count, 2, half_rows, HEADS * HD)
    limits = tile_limit.reshape(2, half_rows)

    def segment_step(running, layer_inputs):
        query_pair, grad_pair, key_matrix, value_matrix = layer_inputs
        key_pre = jnp.dot(vision, key_matrix, preferred_element_type=jnp.float32).reshape(vis_total, KV, HD)
        value_pre = jnp.dot(vision, value_matrix, preferred_element_type=jnp.float32).reshape(vis_total, KV, HD)
        keys = normalize(key_pre).astype(jnp.bfloat16)
        values = value_pre.astype(jnp.bfloat16)
        pullback = jax.vjp(normalize, key_pre)[1]
        outputs = []
        query_grads = []
        for half in range(2):
            output, grad_query, grad_keys, grad_values = attend(query_pair[half].reshape(half_rows, KV, group, HD), grad_pair[half].reshape(half_rows, KV, group, HD), keys, values, limits[half], tile_tokens)
            grad_pre = pullback(grad_keys)[0]
            grad_pre = grad_pre.astype(jnp.bfloat16).reshape(vis_total, KV * HD)
            grad_vals = grad_values.astype(jnp.bfloat16).reshape(vis_total, KV * HD)
            term = jnp.dot(grad_pre, key_matrix.T, preferred_element_type=jnp.float32)
            term = term + jnp.dot(grad_vals, value_matrix.T, preferred_element_type=jnp.float32)
            running = running + term
            outputs.append(output.reshape(half_rows, HEADS * HD))
            query_grads.append(grad_query.reshape(half_rows, HEADS * HD))
        return (running, (jnp.stack(outputs), jnp.stack(query_grads)))
    start_sum = jnp.zeros((vis_total, vision.shape[1]), jnp.float32)
    grad_vision, stacked = lax.scan(segment_step, start_sum, (query_pairs, grad_pairs, key_layers, value_layers))
    return (stacked[0].reshape(queries.shape), stacked[1].reshape(queries.shape), grad_vision)
```

```python
import jax
import jax.numpy as jnp
from jax import lax
from jax.experimental import pallas as pl
from jax.experimental.pallas import tpu as pltpu
from jax.sharding import PartitionSpec as P

HD = 128
EPS = 1e-05
SCALE = HD ** (-0.5)
LOG2E = 1.4426950408889634
F32 = jnp.float32
BF16 = jnp.bfloat16
MESH = pl.DeviceIdType.MESH


def dot(a, b):
    return jnp.dot(a, b, preferred_element_type=F32)


def kernel(
    vis, wk, wv, q, do, lim, att_o, dq_o, gv_o,
    g, pb, w, wt, qt, dot_, bias, part, part_in, kv, kvt, dkv, dkv_in, acc,
    r1o, r1n, r1yo, r1yn, sx, sy, r2x, r2y, tx, ty, r3,
    ss1, rs1, ss2, rs2x, rs2y, ss3, rs3x, rs3y, ss4, rs4, lsem,
    ssr1, rsr1x, rsr1y, ssr2, rsr2x, rsr2y, ssr3, rsr3,
):
    seg, ten = lax.axis_index("segment"), lax.axis_index("tensor")
    zh, x, c = lax.div(seg, 8), lax.rem(lax.div(seg, 2), 4), lax.rem(seg, 2)
    y, zl = lax.div(ten, 2), lax.rem(ten, 2)
    z = zh * 2 + zl
    zi = zl * 4 + zh
    h, yp = lax.div(y, 2), lax.rem(y, 2)
    role = lax.rem(y + 4 - 2 * c, 4)
    home = c == h

    def dev(xx, yy, zz, cc):
        return (lax.div(zz, 2) * 8 + xx * 2 + cc, yy * 2 + lax.rem(zz, 2))

    def zind(zz):
        return lax.rem(zz, 2) * 4 + lax.div(zz, 2)

    def xo(d):
        return lax.rem(x + d + 4, 4)

    def yo(d):
        return lax.rem(y + d + 4, 4)

    def zo(d):
        return lax.rem(z + d + 8, 8)

    partner = dev(x, y, z, 1 - c)

    def rdma(src, dst, ss, rs, to):
        return pltpu.make_async_remote_copy(
            src_ref=src, dst_ref=dst, send_sem=ss, recv_sem=rs, device_id=to, device_id_type=MESH
        )

    def arrived(dst, rs):
        rdma(dst, dst, ss4.at[0], rs, partner).wait_recv()

    wcopies = [
        pltpu.make_async_copy(wk.at[0], w.at[:, pl.ds(0, HD)], lsem.at[0]),
        pltpu.make_async_copy(wv.at[0], w.at[:, pl.ds(HD, HD)], lsem.at[1]),
    ]
    for cp in wcopies:
        cp.start()

    barrier = pltpu.get_barrier_semaphore()
    greet = [dev(x, y, zo(d), cc) for d in range(1, 8) for cc in (0, 1)]
    greet += [dev(xo(d), y, z, c) for d in range(1, 4)]
    greet += [dev(x, yo(d), z, c) for d in range(1, 4)] + [partner]
    for other in greet:
        pl.semaphore_signal(barrier, inc=1, device_id=other, device_id_type=MESH)
    pl.semaphore_wait(barrier, len(greet))

    mine = (1 - c) * (x * 2 + yp) + c * (yp * 4 + x)

    def g1(d):
        return rdma(vis, g.at[c, mine, zi], ss1.at[d], rs1.at[c, zi], dev(x, y, zo(d), h))

    def g1_local():
        return pltpu.make_async_copy(vis, g.at[c, mine, zi], rs1.at[c, zi])

    for d in (4, 3, 5, 2, 6, 1, 7):
        g1(d).start()

    @pl.when(home)
    def _():
        g1_local().start()

    @pl.when(c == 1 - h)
    def _():
        g1(0).start()

    @pl.loop(0, 8)
    def _(n):
        lanes = pl.ds(pl.multiple_of(n * HD, HD), HD)
        qt[n] = q[0, :, lanes].astype(F32).T.astype(BF16)
        dot_[n] = do[0, :, lanes].astype(F32).T.astype(BF16)

    limit = (1 - c) * lim[0:1, :] + c * lim[1:2, :]
    for t in range(4):
        bias[t] = jnp.broadcast_to(jnp.where(t < limit, 0.0, -1e30), (16, 256))

    def g2x(d):
        blk = g.at[0, x * 2 + yp]
        return rdma(blk, blk, ss2.at[0, d], rs2x.at[yp], dev(x, yo(d), z, c))

    def g2y(d):
        blk = g.at[1, yp * 4 + x]
        return rdma(blk, blk, ss2.at[1, d], rs2y.at[x], dev(xo(d), y, z, c))

    @pl.when(home)
    def _():
        for zz in range(8):
            arrived(g.at[0, x * 2 + yp, zz], rs1.at[0, zz])
        for d in (2, 1, 3):
            g2x(d).start()
        for zz in range(8):
            arrived(g.at[1, yp * 4 + x, zz], rs1.at[1, zz])
        for d in (2, 1, 3):
            g2y(d).start()

    for cp in wcopies:
        cp.wait()

    @pl.loop(0, 16)
    def _(n):
        rows = pl.ds(pl.multiple_of(n * 256, 256), 256)
        wt[:, rows] = w[rows, :].astype(F32).T.astype(BF16)

    def g3x(d, half):
        blk = g.at[0, x * 2 + half]
        return rdma(blk, blk, ss3.at[0, d, half], rs3x.at[d, half], dev(xo(1 - 2 * d), y, z, c))

    def g3xf(d):
        blk = g.at[0, xo(2 * d - 1) * 2 + d]
        return rdma(blk, blk, ss3.at[0, d, 2], rs3x.at[d, 2], dev(xo(1 - 2 * d), y, z, c))

    def ywait_x(k):
        @pl.when(jnp.logical_not(jnp.logical_and(home, yp == k)))
        def _():
            arrived(g.at[0, x * 2 + k], rs2x.at[k])

    for k in range(2):
        ywait_x(k)
    for d, half in ((0, 0), (1, 1), (0, 1), (1, 0)):
        g3x(d, half).start()

    def half_y(k, j):
        return pl.ds(k * 4 + j * 2, 2)

    def g3y(k, j, d):
        blk = g.at[1, half_y(k, j)]
        return rdma(blk, blk, ss3.at[1, d, j], rs3y.at[k, j], dev(x, yo(1 - 2 * d), z, c))

    def g3y_role(r):
        if r == 0:
            return [g3y(0, 0, 0), g3y(0, 1, 1), g3y(0, 1, 0), g3y(0, 0, 1)]
        return [g3y(1, 0, 1), g3y(1, 1, 0), g3y(1, 1, 1), g3y(1, 0, 0)]

    def g3yf(r):
        k, j, d = ((1, 0, 1), (0, 0, 0), (1, 1, 0), (0, 1, 1))[r]
        blk = g.at[1, half_y(k, j)]
        return rdma(blk, blk, ss3.at[1, d, 2], rs3y.at[k, j], dev(x, yo(1 - 2 * d), z, c))

    for r in (0, 1):
        @pl.when(role == r)
        def _():
            for d in range(1, 4):
                arrived(g.at[1, r * 4 + xo(d)], rs2y.at[xo(d)])
            for cp in g3y_role(r):
                cp.start()

    arrived(g.at[0, xo(-1) * 2], rs3x.at[0, 0])
    g3xf(0).start()
    arrived(g.at[0, xo(1) * 2 + 1], rs3x.at[1, 1])
    g3xf(1).start()
    for r in range(4):
        @pl.when(role == r)
        def _():
            k, j, _d = ((1, 0, 1), (0, 0, 0), (1, 1, 0), (0, 1, 1))[r]
            arrived(g.at[1, half_y(k, j)], rs3y.at[k, j])
            g3yf(r).start()

    arrived(g.at[0, xo(-1) * 2 + 1], rs3x.at[0, 1])
    arrived(g.at[0, xo(1) * 2], rs3x.at[1, 0])
    arrived(g.at[0, xo(2) * 2], rs3x.at[0, 2])
    arrived(g.at[0, xo(2) * 2 + 1], rs3x.at[1, 2])
    for r in range(4):
        @pl.when(role == r)
        def _():
            first = ((1, 0), (0, 0), (1, 1), (0, 1))[r]
            for k in (0, 1):
                if r == k:
                    continue
                for j in (0, 1):
                    if (k, j) != first:
                        arrived(g.at[1, half_y(k, j)], rs3y.at[k, j])

    for p in range(2):
        total = jnp.zeros((256, 2 * HD), F32)
        for k in range(2):
            for l in range(2):
                if p == 0:
                    a = jnp.concatenate(
                        [g[0, xx * 2 + k, l * 4 : l * 4 + 4].reshape(64, 1024) for xx in range(4)], axis=0
                    )
                else:
                    a = g[1, k * 4 : k * 4 + 4, l * 4 : l * 4 + 4].reshape(256, 1024)
                base = (k * 2 + l) * 1024
                total += dot(a, w[base : base + 1024, :])
        part[p * 256 : (p + 1) * 256, :] = total

    swap = rdma(part, part_in, ss4.at[0], rs4.at[0], partner)
    swap.start()
    swap.wait()
    pre = part[...] + part_in[...]
    part[...] = pre
    kp = pre[:, :HD]
    inv = lax.rsqrt(jnp.mean(kp * kp, axis=-1, keepdims=True) + EPS)
    keys = kp * inv
    vals = pre[:, HD:]
    kv[0] = keys.astype(BF16)
    kv[1] = vals.astype(BF16)
    kvt[0] = keys.astype(BF16).astype(F32).T.astype(BF16)
    kvt[1] = vals.astype(BF16).astype(F32).T.astype(BF16)

    acc[...] = jnp.zeros_like(acc)

    @pl.loop(0, 8)
    def _(n):
        lanes = pl.ds(pl.multiple_of(n * HD, HD), HD)
        qn = q[0, :, lanes]
        don = do[0, :, lanes]
        dotn = dot_[n]
        s = dot(kv[0], qt[n]) * (SCALE * LOG2E)
        s = (s.reshape(8, 4, 16, 256) + bias[...][None]).reshape(512, 256)
        m = jnp.max(s, axis=0, keepdims=True)
        e = jnp.exp2(s - m)
        prob = e * (1.0 / jnp.sum(e, axis=0, keepdims=True))
        pb16 = prob.astype(BF16)
        at = dot(kvt[1], pb16).astype(BF16).astype(F32)
        dp = dot(kv[1], dotn)
        delta = jnp.sum(at * dotn.astype(F32), axis=0, keepdims=True)
        ds = (prob * (dp - delta)).astype(BF16)
        att_o[0, :, lanes] = at.T.astype(BF16)
        dqt = dot(kvt[0], ds) * SCALE
        dq_o[0, :, lanes] = dqt.T.astype(BF16)
        acc[0] += dot(ds, qn)
        acc[1] += dot(pb16, don)

    kp = part[:, :HD]
    inv = lax.rsqrt(jnp.mean(kp * kp, axis=-1, keepdims=True) + EPS)
    dk = acc[0] * SCALE
    dkp = inv * dk - kp * (inv * inv * inv * jnp.mean(kp * dk, axis=-1, keepdims=True))
    dkv[:, :HD] = dkp.astype(BF16)
    dkv[:, HD:] = acc[1].astype(BF16)
    swap2 = rdma(dkv, dkv_in, ss4.at[1], rs4.at[1], partner)
    swap2.start()
    swap2.wait()

    for k in range(2):
        for l in range(2):
            base = (k * 2 + l) * 1024
            for p in range(2):
                rows = slice(p * 256, (p + 1) * 256)
                wtb = wt[:, base : base + 1024]
                v = (dot(dkv[rows, :], wtb) + dot(dkv_in[rows, :], wtb)).astype(BF16)
                if p == 0:
                    for xx in range(4):
                        pb[0, xx * 2 + k, l * 4 : l * 4 + 4] = v[xx * 64 : (xx + 1) * 64].reshape(4, 16, 1024)
                else:
                    pb[1, k * 4 : k * 4 + 4, l * 4 : l * 4 + 4] = v.reshape(4, 4, 16, 1024)

    def r1x_opp(d):
        return rdma(pb.at[0, xo(2) * 2 + d], r1o.at[d], ssr1.at[0, d], rsr1x.at[0, d], dev(xo(1 - 2 * d), y, z, c))

    def r1x_free(d):
        return rdma(
            pb.at[0, xo(1 - 2 * d) * 2 + 1 - d], r1n.at[d, 1 - d], ssr1.at[0, 2 + d], rsr1x.at[1, d],
            dev(xo(1 - 2 * d), y, z, c),
        )

    def r1x_dep(d):
        return rdma(
            pb.at[0, xo(1 - 2 * d) * 2 + d], r1n.at[d, d], ssr1.at[0, 4 + d], rsr1x.at[2, d],
            dev(xo(1 - 2 * d), y, z, c),
        )

    y_opp = {2: ((1, 0, 0), (0, 0, 1)), 3: ((0, 1, 0), (1, 1, 1))}
    y_free = {0: (0, 1, 1), 1: (1, 0, 1), 2: (1, 1, 0), 3: (0, 0, 0)}
    y_dep = {0: (0, 1, 0), 1: (1, 0, 0), 2: (1, 1, 1), 3: (0, 0, 1)}

    def r1y_opp(r, i):
        d, k, j = y_opp[r][i]
        return rdma(pb.at[1, half_y(k, j)], r1yo, ssr1.at[1, i], rsr1y.at[0], dev(x, yo(1 - 2 * d), z, c))

    def r1y_free(r):
        d, k, j = y_free[r]
        side = 0 if r >= 2 else 1
        return rdma(
            pb.at[1, half_y(k, j)], r1yn.at[side, pl.ds(j * 2, 2)], ssr1.at[1, 2], rsr1y.at[1 + side * 2],
            dev(x, yo(1 - 2 * d), z, c),
        )

    def r1y_dep(r):
        d, k, j = y_dep[r]
        side = 0 if r >= 2 else 1
        return rdma(
            pb.at[1, half_y(k, j)], r1yn.at[side, pl.ds(j * 2, 2)], ssr1.at[1, 3], rsr1y.at[2 + side * 2],
            dev(x, yo(1 - 2 * d), z, c),
        )

    for d in range(2):
        r1x_opp(d).start()
    for r in (2, 3):
        @pl.when(role == r)
        def _():
            for i in range(2):
                r1y_opp(r, i).start()
    for d in range(2):
        r1x_free(d).start()
    for r in range(4):
        @pl.when(role == r)
        def _():
            r1y_free(r).start()

    def add_into(dst, src, n):
        @pl.loop(0, n)
        def _(i):
            dst(i)[...] = (dst(i)[...].astype(F32) + src(i)[...].astype(F32)).astype(BF16)

    for d in range(2):
        arrived(r1o.at[d], rsr1x.at[0, d])
        to = xo(1 - 2 * d) * 2 + d
        add_into(lambda i: pb.at[0, to, i], lambda i: r1o.at[d, i], 8)
        r1x_dep(d).start()
    arrived(r1yo, rsr1y.at[0])
    for r in range(4):
        @pl.when(role == r)
        def _():
            _d, k, j = y_dep[r]
            add_into(
                lambda i: pb.at[1, k * 4 + j * 2 + lax.div(i, 8), lax.rem(i, 8)],
                lambda i: r1yo.at[lax.div(i, 8), lax.rem(i, 8)],
                16,
            )
            r1y_dep(r).start()

    for d in range(2):
        arrived(r1n.at[d, 1 - d], rsr1x.at[1, d])
    for d in range(2):
        arrived(r1n.at[d, d], rsr1x.at[2, d])

    @pl.loop(0, 16)
    def _(i):
        k, b = lax.div(i, 8), lax.rem(i, 8)
        sx[k, b] = (pb[0, x * 2 + k, b].astype(F32) + r1n[0, k, b].astype(F32) + r1n[1, k, b].astype(F32)).astype(BF16)

    def r2x_to(k):
        return rdma(sx.at[k], r2x.at[y], ssr2.at[0, k], rsr2x.at[y], dev(x, 2 * c + k, z, c))

    def r2y_to(d):
        return rdma(sy.at[xo(d)], r2y.at[x], ssr2.at[1, d], rsr2y.at[x], dev(xo(d), y, z, c))

    for k in range(2):
        @pl.when(role != k)
        def _():
            r2x_to(k).start()

    @pl.when(home)
    def _():
        arrived(r1yn.at[0, pl.ds(0, 2)], rsr1y.at[1])
        arrived(r1yn.at[1, pl.ds(2, 2)], rsr1y.at[3])
        arrived(r1yn.at[0, pl.ds(2, 2)], rsr1y.at[2])
        arrived(r1yn.at[1, pl.ds(0, 2)], rsr1y.at[4])

        @pl.loop(0, 32)
        def _(i):
            k, b = lax.div(i, 8), lax.rem(i, 8)
            sy[k, b] = (
                pb[1, yp * 4 + k, b].astype(F32) + r1yn[0, k, b].astype(F32) + r1yn[1, k, b].astype(F32)
            ).astype(BF16)

        for d in (2, 1, 3):
            r2y_to(d).start()

        for d in range(1, 4):
            arrived(r2x.at[yo(d)], rsr2x.at[yo(d)])

        @pl.loop(0, 8)
        def _(b):
            v = sx[yp, b].astype(F32)
            for d in range(1, 4):
                v += r2x[yo(d), b].astype(F32)
            tx[b] = v.astype(BF16)

    def r3_to(t, cc, d):
        zz = zo(d)
        return rdma(t.at[zind(zz)], r3.at[zi], ssr3.at[cc, d], rsr3.at[zi], dev(x, y, zz, cc))

    def r3_all(t, cc, act):
        for d in (4, 3, 5, 2, 6, 1, 7):
            act(r3_to(t, cc, d))

        @pl.when(c != cc)
        def _():
            act(r3_to(t, cc, 0))

    def r3_local(t):
        return pltpu.make_async_copy(t.at[zi], r3.at[zi], rsr3.at[zi])

    def begin(cp):
        cp.start()

    @pl.when(home)
    def _():
        r3_all(tx, 0, begin)

        @pl.when(c == 0)
        def _():
            r3_local(tx).start()

        for d in range(1, 4):
            arrived(r2y.at[xo(d)], rsr2y.at[xo(d)])

        @pl.loop(0, 8)
        def _(b):
            v = sy[x, b].astype(F32)
            for d in range(1, 4):
                v += r2y[xo(d), b].astype(F32)
            ty[b] = v.astype(BF16)

        r3_all(ty, 1, begin)

        @pl.when(c == 1)
        def _():
            r3_local(ty).start()

    for b in range(8):
        arrived(r3.at[b], rsr3.at[b])
    total = r3[0].astype(F32)
    for b in range(1, 8):
        total += r3[b].astype(F32)
    gv_o[...] = total

    def sent(cp):
        cp.wait_send()

    for d in range(1, 8):
        sent(g1(d))

    @pl.when(c == 1 - h)
    def _():
        sent(g1(0))

    @pl.when(home)
    def _():
        for d in range(1, 4):
            sent(g2x(d))
            sent(g2y(d))
            sent(r2y_to(d))
        r3_all(tx, 0, sent)
        r3_all(ty, 1, sent)

    for d in range(2):
        for half in range(2):
            sent(g3x(d, half))
        sent(g3xf(d))
        sent(r1x_opp(d))
        sent(r1x_free(d))
        sent(r1x_dep(d))
    for r in range(4):
        @pl.when(role == r)
        def _():
            if r < 2:
                for cp in g3y_role(r):
                    sent(cp)
            else:
                for i in range(2):
                    sent(r1y_opp(r, i))
            sent(g3yf(r))
            sent(r1y_free(r))
            sent(r1y_dep(r))
    for k in range(2):
        @pl.when(role != k)
        def _():
            sent(r2x_to(k))


def on_device(queries, grad_attended, vision, key_weight, value_weight, tile_limit):
    vmem = pl.BlockSpec(memory_space=pltpu.VMEM)
    hbm = pl.BlockSpec(memory_space=pl.ANY)
    dma = pltpu.SemaphoreType.DMA
    return pl.pallas_call(
        kernel,
        out_shape=(
            jax.ShapeDtypeStruct(queries.shape, BF16),
            jax.ShapeDtypeStruct(queries.shape, BF16),
            jax.ShapeDtypeStruct(vision.shape, F32),
        ),
        in_specs=[vmem, hbm, hbm, vmem, vmem, vmem],
        out_specs=(vmem, vmem, vmem),
        scratch_shapes=[
            pltpu.VMEM((2, 8, 8, 16, 1024), BF16),
            pltpu.VMEM((2, 8, 8, 16, 1024), BF16),
            pltpu.VMEM((4096, 256), BF16),
            pltpu.VMEM((256, 4096), BF16),
            pltpu.VMEM((8, 128, 256), BF16),
            pltpu.VMEM((8, 128, 256), BF16),
            pltpu.VMEM((4, 16, 256), F32),
            pltpu.VMEM((512, 256), F32),
            pltpu.VMEM((512, 256), F32),
            pltpu.VMEM((2, 512, 128), BF16),
            pltpu.VMEM((2, 128, 512), BF16),
            pltpu.VMEM((512, 256), BF16),
            pltpu.VMEM((512, 256), BF16),
            pltpu.VMEM((2, 512, 128), F32),
            pltpu.VMEM((2, 8, 16, 1024), BF16),
            pltpu.VMEM((2, 2, 8, 16, 1024), BF16),
            pltpu.VMEM((2, 8, 16, 1024), BF16),
            pltpu.VMEM((2, 4, 8, 16, 1024), BF16),
            pltpu.VMEM((2, 8, 16, 1024), BF16),
            pltpu.VMEM((4, 8, 16, 1024), BF16),
            pltpu.VMEM((4, 8, 16, 1024), BF16),
            pltpu.VMEM((4, 8, 16, 1024), BF16),
            pltpu.VMEM((8, 16, 1024), BF16),
            pltpu.VMEM((8, 16, 1024), BF16),
            pltpu.VMEM((8, 16, 1024), BF16),
            dma((8,)), dma((2, 8)),
            dma((2, 4)), dma((2,)), dma((4,)),
            dma((2, 2, 3)), dma((2, 3)), dma((2, 2)),
            dma((2,)), dma((2,)), dma((2,)),
            dma((2, 6)), dma((3, 2)), dma((5,)),
            dma((2, 4)), dma((4,)), dma((4,)),
            dma((2, 8)), dma((8,)),
        ],
        compiler_params=pltpu.CompilerParams(
            collective_id=0, has_side_effects=True, vmem_limit_bytes=52 * 2**20
        ),
        cost_estimate=pl.CostEstimate(flops=6_000_000_000, bytes_accessed=6_000_000, transcendentals=1_000_000),
    )(vision, key_weight, value_weight, queries, grad_attended, tile_limit.reshape(2, 256))


def solution(mesh):
    return jax.shard_map(
        on_device,
        mesh=mesh,
        in_specs=(
            P("segment", None, "tensor"),
            P("segment", None, "tensor"),
            P("segment", "tensor"),
            P("segment", None, "tensor"),
            P("segment", None, "tensor"),
            P(),
        ),
        out_specs=(
            P("segment", None, "tensor"),
            P("segment", None, "tensor"),
            P("segment", "tensor"),
        ),
        check_vma=False,
    )
```

```python
import jax
import jax.numpy as jnp
from jax import lax
from jax.experimental import pallas as pl
from jax.experimental.pallas import tpu as pltpu
from jax.sharding import PartitionSpec as P

HD = 128
EPS = 1e-05
SCALE = HD ** (-0.5)
LOG2E = 1.4426950408889634
F32 = jnp.float32
BF16 = jnp.bfloat16
MESH = pl.DeviceIdType.MESH

ZW = 256
CW = (384, 384)
CO = (256, 640)
NC = len(CW)


def scratch():
    v, dma = pltpu.VMEM, pltpu.SemaphoreType.DMA
    s = {
        "q": v((256, 1024), BF16), "do": v((256, 1024), BF16),
        "w": v((4096, 256), BF16), "wt": v((256, 4096), BF16),
        "qt": v((8, 128, 256), BF16), "dot": v((8, 128, 256), BF16),
        "bias": v((4, 16, 256), F32),
        "part": v((512, 256), F32), "part_in": v((512, 256), F32),
        "kv": v((2, 512, 128), BF16), "kvt": v((2, 128, 512), BF16),
        "dkv": v((512, 256), BF16), "dkv_in": v((512, 256), BF16),
        "acc": v((2, 512, 128), F32),
        "gz": v((8, 2, 4, 2, 16, ZW), BF16), "pz": v((8, 2, 4, 2, 16, ZW), BF16),
        "rz1": v((2, 4, 2, 4, 2, 16, ZW), BF16), "rz2": v((16, 16, ZW), BF16),
    }
    for ch in range(NC):
        n = CW[ch]
        s |= {
            f"g{ch}": v((2, 8, 8, 16, n), BF16), f"pb{ch}": v((2, 8, 8, 16, n), BF16),
            f"r1o{ch}": v((2, 8, 16, n), BF16), f"r1n{ch}": v((2, 2, 8, 16, n), BF16),
            f"r1yo{ch}": v((2, 8, 16, n), BF16), f"r1yn{ch}": v((2, 4, 8, 16, n), BF16),
            f"sx{ch}": v((2, 8, 16, n), BF16), f"sy{ch}": v((4, 8, 16, n), BF16),
            f"r2x{ch}": v((4, 8, 16, n), BF16), f"r2y{ch}": v((4, 8, 16, n), BF16),
            f"tx{ch}": v((8, 16, n), BF16), f"ty{ch}": v((8, 16, n), BF16),
            f"r3{ch}": v((8, 16, n), BF16),
        }
    s |= {
        "lsem": dma((4,)),
        "ss1": dma((NC, 8)), "rs1": dma((NC, 2, 8)),
        "ss2": dma((NC, 2, 4)), "rs2x": dma((NC, 2)), "rs2y": dma((NC, 4)),
        "ss3": dma((NC, 2, 2, 3)), "rs3x": dma((NC, 2, 3)), "rs3y": dma((NC, 2, 2)),
        "ss4": dma((2,)), "rs4": dma((2,)),
        "ssr1": dma((NC, 2, 6)), "rsr1x": dma((NC, 3, 2)), "rsr1y": dma((NC, 5)),
        "ssr2": dma((NC, 2, 4)), "rsr2x": dma((NC, 4)), "rsr2y": dma((NC, 4)),
        "ssr3": dma((NC, 2, 8)), "rsr3": dma((NC, 8)),
        "ssz1": dma((4, 4)), "rsz1": dma((2, 4, 2)),
        "ssz3": dma((2, 4)), "rsz3": dma((2, 4)),
        "ssrz1": dma((2, 4)), "rsrz1": dma((2, 4)),
        "ssrz2": dma((16,)), "rsrz2": dma((16,)),
    }
    return s


NAMES = tuple(scratch())


def mm(a, b):
    return jnp.dot(a, b, preferred_element_type=F32)


def kernel(vis, wk, wv, q_in, do_in, lim, att_o, dq_o, gv_o, *rest):
    R = dict(zip(NAMES, rest, strict=True))
    q, do, w, wt = R["q"], R["do"], R["w"], R["wt"]
    gz, pz = R["gz"], R["pz"]
    G = [R[f"g{ch}"] for ch in range(NC)]
    PB = [R[f"pb{ch}"] for ch in range(NC)]

    seg, ten = lax.axis_index("segment"), lax.axis_index("tensor")
    zh, x, c = lax.div(seg, 8), lax.rem(lax.div(seg, 2), 4), lax.rem(seg, 2)
    y, zl = lax.div(ten, 2), lax.rem(ten, 2)
    z = zh * 2 + zl
    zi = zl * 4 + zh
    h, yp = lax.div(y, 2), lax.rem(y, 2)
    role = lax.rem(y + 4 - 2 * c, 4)
    home = c == h

    def dev(xx, yy, zz, cc):
        return (lax.div(zz, 2) * 8 + xx * 2 + cc, yy * 2 + lax.rem(zz, 2))

    def zind(zz):
        return lax.rem(zz, 2) * 4 + lax.div(zz, 2)

    def xo(d):
        return lax.rem(x + d + 4, 4)

    def yo(d):
        return lax.rem(y + d + 4, 4)

    def zo(d):
        return lax.rem(z + d + 8, 8)

    partner = dev(x, y, z, 1 - c)

    def rdma(src, dst, ss, rs, to):
        return pltpu.make_async_remote_copy(
            src_ref=src, dst_ref=dst, send_sem=ss, recv_sem=rs, device_id=to, device_id_type=MESH
        )

    def arrived(dst, rs):
        rdma(dst, dst, R["ss4"].at[0], rs, partner).wait_recv()

    def begin(cp):
        cp.start()

    def sent(cp):
        cp.wait_send()

    lsem = R["lsem"]
    qcopies = [
        pltpu.make_async_copy(q_in.at[0], q, lsem.at[0]),
        pltpu.make_async_copy(do_in.at[0], do, lsem.at[1]),
    ]
    wcopies = [
        pltpu.make_async_copy(wk.at[0], w.at[:, pl.ds(0, HD)], lsem.at[2]),
        pltpu.make_async_copy(wv.at[0], w.at[:, pl.ds(HD, HD)], lsem.at[3]),
    ]
    for cp in qcopies + wcopies:
        cp.start()

    barrier = pltpu.get_barrier_semaphore()
    greet = [dev(x, y, zo(d), cc) for d in range(1, 8) for cc in (0, 1)]
    greet += [dev(xo(d), yo(e), z, cc) for d in range(4) for e in range(4) for cc in (0, 1) if (d, e) != (0, 0)]
    greet += [partner]
    for other in greet:
        pl.semaphore_signal(barrier, inc=1, device_id=other, device_id_type=MESH)
    pl.semaphore_wait(barrier, len(greet))

    mine = (1 - c) * (x * 2 + yp) + c * (yp * 4 + x)

    def g1(ch, d):
        src = vis.at[:, pl.ds(CO[ch], CW[ch])]
        return rdma(src, G[ch].at[c, mine, zi], R["ss1"].at[ch, d], R["rs1"].at[ch, c, zi], dev(x, y, zo(d), h))

    def g1_local(ch):
        return pltpu.make_async_copy(
            vis.at[:, pl.ds(CO[ch], CW[ch])], G[ch].at[c, mine, zi], R["rs1"].at[ch, c, zi]
        )

    def g1_all(ch, act):
        for d in (4, 3, 5, 2, 6, 1, 7):
            act(g1(ch, d))

        @pl.when(c == 1 - h)
        def _():
            act(g1(ch, 0))

    def g1_own(ch):
        @pl.when(home)
        def _():
            g1_local(ch).start()

    def z1(d, e):
        return rdma(
            vis.at[:, pl.ds(0, ZW)], gz.at[zi, yp, x, c], R["ssz1"].at[d, e], R["rsz1"].at[yp, x, c],
            dev(xo(d), yo(e), z, h),
        )

    def z1_all(act):
        for d, e in ((2, 2), (2, 1), (2, 3), (1, 2), (3, 2), (1, 1), (1, 3), (3, 1), (3, 3), (2, 0), (0, 2), (1, 0), (3, 0), (0, 1), (0, 3)):
            act(z1(d, e))

        @pl.when(c == 1 - h)
        def _():
            act(z1(0, 0))

    g1_all(0, begin)
    g1_own(0)
    z1_all(begin)

    @pl.when(home)
    def _():
        pltpu.make_async_copy(vis.at[:, pl.ds(0, ZW)], gz.at[zi, yp, x, c], R["rsz1"].at[yp, x, c]).start()

    for ch in range(1, NC):
        g1_all(ch, begin)
        g1_own(ch)

    for cp in qcopies:
        cp.wait()
    qt, dot_, bias = R["qt"], R["dot"], R["bias"]

    @pl.loop(0, 8)
    def _(n):
        lanes = pl.ds(pl.multiple_of(n * HD, HD), HD)
        qt[n] = q[:, lanes].astype(F32).T.astype(BF16)
        dot_[n] = do[:, lanes].astype(F32).T.astype(BF16)

    def g2x(ch, d):
        blk = G[ch].at[0, x * 2 + yp]
        return rdma(blk, blk, R["ss2"].at[ch, 0, d], R["rs2x"].at[ch, yp], dev(x, yo(d), z, c))

    def g2y(ch, d):
        blk = G[ch].at[1, yp * 4 + x]
        return rdma(blk, blk, R["ss2"].at[ch, 1, d], R["rs2y"].at[ch, x], dev(xo(d), y, z, c))

    def step2(ch):
        @pl.when(home)
        def _():
            for zz in range(8):
                arrived(G[ch].at[0, x * 2 + yp, zz], R["rs1"].at[ch, 0, zz])
            for d in (2, 1, 3):
                g2x(ch, d).start()
            for zz in range(8):
                arrived(G[ch].at[1, yp * 4 + x, zz], R["rs1"].at[ch, 1, zz])
            for d in (2, 1, 3):
                g2y(ch, d).start()

    def z3(d, s):
        side = 1 - 2 * d
        if s < 3:
            blk = gz.at[zind(zo(-side * s))]
        else:
            blk = gz.at[zind(zo(-side * s)), d]
        return rdma(blk, blk, R["ssz3"].at[d, s], R["rsz3"].at[d, s], dev(x, y, zo(side), c))

    def z3_arrived(d, s):
        at = zind(zo(-(1 - 2 * d) * (s + 1)))
        arrived(gz.at[at] if s < 3 else gz.at[at, d], R["rsz3"].at[d, s])

    def zstep(s):
        for d in range(2):
            if s > 0:
                z3_arrived(d, s - 1)
            z3(d, s).start()

    def g3x(ch, d, half):
        blk = G[ch].at[0, x * 2 + half]
        return rdma(blk, blk, R["ss3"].at[ch, 0, d, half], R["rs3x"].at[ch, d, half], dev(xo(1 - 2 * d), y, z, c))

    def g3xf(ch, d):
        blk = G[ch].at[0, xo(2 * d - 1) * 2 + d]
        return rdma(blk, blk, R["ss3"].at[ch, 0, d, 2], R["rs3x"].at[ch, d, 2], dev(xo(1 - 2 * d), y, z, c))

    def half_y(k, j):
        return pl.ds(k * 4 + j * 2, 2)

    def g3y(ch, k, j, d):
        blk = G[ch].at[1, half_y(k, j)]
        return rdma(blk, blk, R["ss3"].at[ch, 1, d, j], R["rs3y"].at[ch, k, j], dev(x, yo(1 - 2 * d), z, c))

    def g3y_role(ch, r):
        order = ((0, 0, 0), (0, 1, 1), (0, 1, 0), (0, 0, 1)) if r == 0 else ((1, 0, 1), (1, 1, 0), (1, 1, 1), (1, 0, 0))
        return [g3y(ch, k, j, d) for k, j, d in order]

    passed = ((1, 0, 1), (0, 0, 0), (1, 1, 0), (0, 1, 1))

    def g3yf(ch, r):
        k, j, d = passed[r]
        blk = G[ch].at[1, half_y(k, j)]
        return rdma(blk, blk, R["ss3"].at[ch, 1, d, 2], R["rs3y"].at[ch, k, j], dev(x, yo(1 - 2 * d), z, c))

    def step3(ch):
        for k in range(2):
            @pl.when(role != k)
            def _():
                arrived(G[ch].at[0, x * 2 + k], R["rs2x"].at[ch, k])
        for d, half in ((0, 0), (1, 1), (0, 1), (1, 0)):
            g3x(ch, d, half).start()
        for r in (0, 1):
            @pl.when(role == r)
            def _():
                for d in range(1, 4):
                    arrived(G[ch].at[1, r * 4 + xo(d)], R["rs2y"].at[ch, xo(d)])
                for cp in g3y_role(ch, r):
                    cp.start()

    def forward3(ch):
        for d in range(2):
            arrived(G[ch].at[0, xo(2 * d - 1) * 2 + d], R["rs3x"].at[ch, d, d])
            g3xf(ch, d).start()
        for r in range(4):
            @pl.when(role == r)
            def _():
                k, j, _d = passed[r]
                arrived(G[ch].at[1, half_y(k, j)], R["rs3y"].at[ch, k, j])
                g3yf(ch, r).start()

    def rest3(ch):
        for d in range(2):
            arrived(G[ch].at[0, xo(2 * d - 1) * 2 + 1 - d], R["rs3x"].at[ch, d, 1 - d])
        for d in range(2):
            arrived(G[ch].at[0, xo(2) * 2 + d], R["rs3x"].at[ch, d, 2])
        for r in range(4):
            @pl.when(role == r)
            def _():
                for k in (0, 1):
                    if r == k:
                        continue
                    for j in (0, 1):
                        if (k, j) != passed[r][:2]:
                            arrived(G[ch].at[1, half_y(k, j)], R["rs3y"].at[ch, k, j])

    part, part_in = R["part"], R["part_in"]

    def project(ch):
        for p in range(2):
            rows = slice(p * 256, (p + 1) * 256)
            total = part[rows, :] if ch != 0 else jnp.zeros((256, 256), F32)
            for k in range(2):
                for l in range(2):
                    if p == 0:
                        a = jnp.concatenate(
                            [G[ch][0, xx * 2 + k, l * 4 : l * 4 + 4].reshape(64, CW[ch]) for xx in range(4)], axis=0
                        )
                    else:
                        a = G[ch][1, k * 4 : k * 4 + 4, l * 4 : l * 4 + 4].reshape(256, CW[ch])
                    base = (k * 2 + l) * 1024 + CO[ch]
                    total += mm(a, w[base : base + CW[ch], :])
            part[rows, :] = total

    def project_z():
        for p in range(2):
            rows = slice(p * 256, (p + 1) * 256)
            total = part[rows, :]
            for k in range(2):
                for l in range(2):
                    a = jnp.concatenate(
                        [gz[l * 4 : l * 4 + 4, k, xx, p].reshape(64, ZW) for xx in range(4)], axis=0
                    )
                    base = (k * 2 + l) * 1024
                    total += mm(a, w[base : base + ZW, :])
            part[rows, :] = total

    step2(0)
    for k in range(2):
        for xx in range(4):
            for cc in range(2):
                arrived(gz.at[zi, k, xx, cc], R["rsz1"].at[k, xx, cc])
    zstep(0)
    for ch in range(1, NC):
        step2(ch)

    for cp in wcopies:
        cp.wait()

    @pl.loop(0, 8)
    def _(n):
        rows = pl.ds(pl.multiple_of(n * 256, 256), 256)
        wt[:, rows] = w[rows, :].astype(F32).T.astype(BF16)

    step3(0)
    zstep(1)

    @pl.loop(8, 16)
    def _(n):
        rows = pl.ds(pl.multiple_of(n * 256, 256), 256)
        wt[:, rows] = w[rows, :].astype(F32).T.astype(BF16)

    for ch in range(1, NC):
        step3(ch)
    limit = (1 - c) * lim[0:1, :] + c * lim[1:2, :]
    for t in range(4):
        bias[t] = jnp.broadcast_to(jnp.where(t < limit, 0.0, -1e30), (16, 256))
    forward3(0)
    zstep(2)
    for ch in range(1, NC):
        forward3(ch)
    rest3(0)
    project(0)
    zstep(3)
    for d in range(2):
        z3_arrived(d, 3)
    project_z()
    for ch in range(1, NC):
        rest3(ch)
        project(ch)

    swap = rdma(part, part_in, R["ss4"].at[0], R["rs4"].at[0], partner)
    swap.start()
    swap.wait()
    kv, kvt, acc = R["kv"], R["kvt"], R["acc"]
    pre = part[...] + part_in[...]
    part[...] = pre
    kp = pre[:, :HD]
    inv = lax.rsqrt(jnp.mean(kp * kp, axis=-1, keepdims=True) + EPS)
    keys = (kp * inv).astype(BF16)
    vals = pre[:, HD:].astype(BF16)
    kv[0] = keys
    kv[1] = vals
    kvt[0] = keys.astype(F32).T.astype(BF16)
    kvt[1] = vals.astype(F32).T.astype(BF16)

    acc[...] = jnp.zeros_like(acc)

    @pl.loop(0, 8, unroll=2)
    def _(n):
        lanes = pl.ds(pl.multiple_of(n * HD, HD), HD)
        qn = q[:, lanes]
        don = do[:, lanes]
        dotn = dot_[n]
        s = mm(kv[0], qt[n]) * (SCALE * LOG2E)
        s = (s.reshape(8, 4, 16, 256) + bias[...][None]).reshape(512, 256)
        m = jnp.max(s, axis=0, keepdims=True)
        e = jnp.exp2(s - m)
        prob = e * (1.0 / jnp.sum(e, axis=0, keepdims=True))
        pb16 = prob.astype(BF16)
        at = mm(kvt[1], pb16).astype(BF16).astype(F32)
        dp = mm(kv[1], dotn)
        delta = jnp.sum(at * dotn.astype(F32), axis=0, keepdims=True)
        ds = (prob * (dp - delta)).astype(BF16)
        att_o[0, :, lanes] = at.T.astype(BF16)
        dqt = mm(kvt[0], ds) * SCALE
        dq_o[0, :, lanes] = dqt.T.astype(BF16)
        acc[0] += mm(ds, qn)
        acc[1] += mm(pb16, don)

    dkv, dkv_in = R["dkv"], R["dkv_in"]
    kp = part[:, :HD]
    inv = lax.rsqrt(jnp.mean(kp * kp, axis=-1, keepdims=True) + EPS)
    dk = acc[0] * SCALE
    dkp = inv * dk - kp * (inv * inv * inv * jnp.mean(kp * dk, axis=-1, keepdims=True))
    dkv[:, :HD] = dkp.astype(BF16)
    dkv[:, HD:] = acc[1].astype(BF16)
    swap2 = rdma(dkv, dkv_in, R["ss4"].at[1], R["rs4"].at[1], partner)
    swap2.start()
    swap2.wait()

    def back(p, base, n):
        rows = slice(p * 256, (p + 1) * 256)
        wtb = wt[:, base : base + n]
        return (mm(dkv[rows, :], wtb) + mm(dkv_in[rows, :], wtb)).astype(BF16)

    def back_z():
        for k in range(2):
            for l in range(2):
                for p in range(2):
                    v = back(p, (k * 2 + l) * 1024, ZW)
                    for xx in range(4):
                        pz[l * 4 : l * 4 + 4, k, xx, p] = v[xx * 64 : (xx + 1) * 64].reshape(4, 16, ZW)

    def back_chunk(ch):
        pb = PB[ch]
        for k in range(2):
            for l in range(2):
                for p in range(2):
                    v = back(p, (k * 2 + l) * 1024 + CO[ch], CW[ch])
                    if p == 0:
                        for xx in range(4):
                            pb[0, xx * 2 + k, l * 4 : l * 4 + 4] = v[xx * 64 : (xx + 1) * 64].reshape(4, 16, CW[ch])
                    else:
                        pb[1, k * 4 : k * 4 + 4, l * 4 : l * 4 + 4] = v.reshape(4, 4, 16, CW[ch])

    rz1, rz2 = R["rz1"], R["rz2"]

    def rz(d, s):
        side = 1 - 2 * d
        at = zind(zo(side * (4 - s)))
        src = pz.at[at, d] if s == 0 else pz.at[at]
        dst = rz1.at[d, 0, d] if s == 0 else rz1.at[d, s]
        return rdma(src, dst, R["ssrz1"].at[d, s], R["rsrz1"].at[d, s], dev(x, y, zo(side), c))

    def rz_arrived(d, s):
        arrived(rz1.at[d, 0, d] if s == 0 else rz1.at[d, s], R["rsrz1"].at[d, s])

    def rzstep(s):
        for d in range(2):
            if s > 0:
                rz_arrived(d, s - 1)
                at = zind(zo((1 - 2 * d) * (4 - s)))
                if s == 1:
                    pz[at, d] = (pz[at, d].astype(F32) + rz1[d, 0, d].astype(F32)).astype(BF16)
                else:
                    pz[at] = (pz[at].astype(F32) + rz1[d, s - 1].astype(F32)).astype(BF16)
            rz(d, s).start()

    def rz2_to(k, xx, cc):
        i = (yp * 4 + x) * 2 + cc
        return i

    def z2(d, k, cc):
        src = pz.at[zi, k, xo(d), cc]
        me = y * 4 + x
        return rdma(src, rz2.at[me], R["ssrz2"].at[(k * 4 + d) * 2 + cc], R["rsrz2"].at[me], dev(xo(d), 2 * c + k, z, cc))

    def z2_all(act):
        for d in (2, 1, 3):
            for k in range(2):
                for cc in range(2):
                    act(z2(d, k, cc))
        for k in range(2):
            for cc in range(2):
                if True:
                    @pl.when(jnp.logical_or(role != k, c != cc))
                    def _():
                        act(z2(0, k, cc))

    def z2_local():
        return pltpu.make_async_copy(pz.at[zi, yp, x, c], rz2.at[y * 4 + x], R["rsrz2"].at[y * 4 + x])

    def rz_sum():
        for d in range(2):
            rz_arrived(d, 3)
        pz[zi] = (pz[zi].astype(F32) + rz1[0, 3].astype(F32) + rz1[1, 3].astype(F32)).astype(BF16)
        z2_all(begin)

        @pl.when(home)
        def _():
            z2_local().start()

    def r1x_opp(ch, d):
        return rdma(
            PB[ch].at[0, xo(2) * 2 + d], R[f"r1o{ch}"].at[d], R["ssr1"].at[ch, 0, d], R["rsr1x"].at[ch, 0, d],
            dev(xo(1 - 2 * d), y, z, c),
        )

    def r1x_free(ch, d):
        return rdma(
            PB[ch].at[0, xo(1 - 2 * d) * 2 + 1 - d], R[f"r1n{ch}"].at[d, 1 - d], R["ssr1"].at[ch, 0, 2 + d],
            R["rsr1x"].at[ch, 1, d], dev(xo(1 - 2 * d), y, z, c),
        )

    def r1x_dep(ch, d):
        return rdma(
            PB[ch].at[0, xo(1 - 2 * d) * 2 + d], R[f"r1n{ch}"].at[d, d], R["ssr1"].at[ch, 0, 4 + d],
            R["rsr1x"].at[ch, 2, d], dev(xo(1 - 2 * d), y, z, c),
        )

    y_opp = {2: ((1, 0, 0), (0, 0, 1)), 3: ((0, 1, 0), (1, 1, 1))}
    y_free = {0: (0, 1, 1), 1: (1, 0, 1), 2: (1, 1, 0), 3: (0, 0, 0)}
    y_dep = {0: (0, 1, 0), 1: (1, 0, 0), 2: (1, 1, 1), 3: (0, 0, 1)}

    def r1y_opp(ch, r, i):
        d, k, j = y_opp[r][i]
        return rdma(
            PB[ch].at[1, half_y(k, j)], R[f"r1yo{ch}"], R["ssr1"].at[ch, 1, i], R["rsr1y"].at[ch, 0],
            dev(x, yo(1 - 2 * d), z, c),
        )

    def r1y_next(ch, r, dep):
        d, k, j = (y_dep if dep else y_free)[r]
        side = 0 if r >= 2 else 1
        return rdma(
            PB[ch].at[1, half_y(k, j)], R[f"r1yn{ch}"].at[side, pl.ds(j * 2, 2)], R["ssr1"].at[ch, 1, 2 + dep],
            R["rsr1y"].at[ch, 1 + dep + side * 2], dev(x, yo(1 - 2 * d), z, c),
        )

    def rs1(ch):
        for d in range(2):
            r1x_opp(ch, d).start()
        for r in (2, 3):
            @pl.when(role == r)
            def _():
                for i in range(2):
                    r1y_opp(ch, r, i).start()
        for d in range(2):
            r1x_free(ch, d).start()
        for r in range(4):
            @pl.when(role == r)
            def _():
                r1y_next(ch, r, 0).start()

    def rs1_dep(ch):
        pb, r1o, r1yo = PB[ch], R[f"r1o{ch}"], R[f"r1yo{ch}"]
        for d in range(2):
            arrived(r1o.at[d], R["rsr1x"].at[ch, 0, d])
            to = xo(1 - 2 * d) * 2 + d

            @pl.loop(0, 8, unroll=2)
            def _(i):
                pb[0, to, i] = (pb[0, to, i].astype(F32) + r1o[d, i].astype(F32)).astype(BF16)

            r1x_dep(ch, d).start()
        arrived(r1yo, R["rsr1y"].at[ch, 0])
        for r in range(4):
            @pl.when(role == r)
            def _():
                _d, k, j = y_dep[r]

                @pl.loop(0, 8)
                def _(i):
                    for xx in range(2):
                        at = k * 4 + j * 2 + xx
                        pb[1, at, i] = (pb[1, at, i].astype(F32) + r1yo[xx, i].astype(F32)).astype(BF16)

                r1y_next(ch, r, 1).start()

    def r2x_to(ch, k):
        return rdma(
            R[f"sx{ch}"].at[k], R[f"r2x{ch}"].at[y], R["ssr2"].at[ch, 0, k], R["rsr2x"].at[ch, y],
            dev(x, 2 * c + k, z, c),
        )

    def r2y_to(ch, d):
        return rdma(
            R[f"sy{ch}"].at[xo(d)], R[f"r2y{ch}"].at[x], R["ssr2"].at[ch, 1, d], R["rsr2y"].at[ch, x],
            dev(xo(d), y, z, c),
        )

    def rs2(ch):
        pb, r1n, r1yn, sx, sy = PB[ch], R[f"r1n{ch}"], R[f"r1yn{ch}"], R[f"sx{ch}"], R[f"sy{ch}"]
        for d in range(2):
            arrived(r1n.at[d, 1 - d], R["rsr1x"].at[ch, 1, d])
        for d in range(2):
            arrived(r1n.at[d, d], R["rsr1x"].at[ch, 2, d])

        @pl.loop(0, 8)
        def _(b):
            for k in range(2):
                sx[k, b] = (
                    pb[0, x * 2 + k, b].astype(F32) + r1n[0, k, b].astype(F32) + r1n[1, k, b].astype(F32)
                ).astype(BF16)

        for k in range(2):
            @pl.when(role != k)
            def _():
                r2x_to(ch, k).start()

        @pl.when(home)
        def _():
            arrived(r1yn.at[0, pl.ds(0, 2)], R["rsr1y"].at[ch, 1])
            arrived(r1yn.at[1, pl.ds(2, 2)], R["rsr1y"].at[ch, 3])
            arrived(r1yn.at[0, pl.ds(2, 2)], R["rsr1y"].at[ch, 2])
            arrived(r1yn.at[1, pl.ds(0, 2)], R["rsr1y"].at[ch, 4])

            @pl.loop(0, 8)
            def _(b):
                for k in range(4):
                    sy[k, b] = (
                        pb[1, yp * 4 + k, b].astype(F32) + r1yn[0, k, b].astype(F32) + r1yn[1, k, b].astype(F32)
                    ).astype(BF16)

            for d in (2, 1, 3):
                r2y_to(ch, d).start()

    def r3_to(ch, cc, d):
        t = R[f"ty{ch}" if cc else f"tx{ch}"]
        zz = zo(d)
        return rdma(t.at[zind(zz)], R[f"r3{ch}"].at[zi], R["ssr3"].at[ch, cc, d], R["rsr3"].at[ch, zi], dev(x, y, zz, cc))

    def r3_all(ch, cc, act):
        for d in (4, 3, 5, 2, 6, 1, 7):
            act(r3_to(ch, cc, d))

        @pl.when(c != cc)
        def _():
            act(r3_to(ch, cc, 0))

    def r3_own(ch, cc):
        t = R[f"ty{ch}" if cc else f"tx{ch}"]

        @pl.when(c == cc)
        def _():
            pltpu.make_async_copy(t.at[zi], R[f"r3{ch}"].at[zi], R["rsr3"].at[ch, zi]).start()

    def rs3(ch):
        sx, sy, r2x, r2y, tx, ty = (R[f"{n}{ch}"] for n in ("sx", "sy", "r2x", "r2y", "tx", "ty"))

        @pl.when(home)
        def _():
            for d in range(1, 4):
                arrived(r2x.at[yo(d)], R["rsr2x"].at[ch, yo(d)])

            @pl.loop(0, 8, unroll=2)
            def _(b):
                v = sx[yp, b].astype(F32)
                for d in range(1, 4):
                    v += r2x[yo(d), b].astype(F32)
                tx[b] = v.astype(BF16)

            r3_all(ch, 0, begin)
            r3_own(ch, 0)
            for d in range(1, 4):
                arrived(r2y.at[xo(d)], R["rsr2y"].at[ch, xo(d)])

            @pl.loop(0, 8, unroll=2)
            def _(b):
                v = sy[x, b].astype(F32)
                for d in range(1, 4):
                    v += r2y[xo(d), b].astype(F32)
                ty[b] = v.astype(BF16)

            r3_all(ch, 1, begin)
            r3_own(ch, 1)

    def finish(ch):
        r3 = R[f"r3{ch}"]
        for b in range(8):
            arrived(r3.at[b], R["rsr3"].at[ch, b])
        total = r3[0].astype(F32)
        for b in range(1, 8):
            total += r3[b].astype(F32)
        gv_o[:, CO[ch] : CO[ch] + CW[ch]] = total

    back_z()
    rzstep(0)
    for ch in range(NC):
        back_chunk(ch)
        rs1(ch)
    rs1_dep(0)
    rzstep(1)
    for ch in range(1, NC):
        rs1_dep(ch)
    rs2(0)
    rzstep(2)
    for ch in range(1, NC):
        rs2(ch)
    rs3(0)
    rzstep(3)
    for ch in range(1, NC):
        rs3(ch)
    rz_sum()
    for ch in range(NC):
        finish(ch)
    for i in range(16):
        arrived(rz2.at[i], R["rsrz2"].at[i])
    total = rz2[0].astype(F32)
    for i in range(1, 16):
        total += rz2[i].astype(F32)
    gv_o[:, :ZW] = total

    z1_all(sent)
    z2_all(sent)
    for d in range(2):
        for s in range(4):
            sent(z3(d, s))
            sent(rz(d, s))
    for ch in range(NC):
        g1_all(ch, sent)

        @pl.when(home)
        def _():
            for d in range(1, 4):
                sent(g2x(ch, d))
                sent(g2y(ch, d))
                sent(r2y_to(ch, d))
            for cc in range(2):
                r3_all(ch, cc, sent)

        for d in range(2):
            for half in range(2):
                sent(g3x(ch, d, half))
            sent(g3xf(ch, d))
            sent(r1x_opp(ch, d))
            sent(r1x_free(ch, d))
            sent(r1x_dep(ch, d))
        for r in range(4):
            @pl.when(role == r)
            def _():
                if r < 2:
                    for cp in g3y_role(ch, r):
                        sent(cp)
                else:
                    for i in range(2):
                        sent(r1y_opp(ch, r, i))
                sent(g3yf(ch, r))
                sent(r1y_next(ch, r, 0))
                sent(r1y_next(ch, r, 1))
        for k in range(2):
            @pl.when(role != k)
            def _():
                sent(r2x_to(ch, k))


def on_device(queries, grad_attended, vision, key_weight, value_weight, tile_limit):
    vmem = pl.BlockSpec(memory_space=pltpu.VMEM)
    hbm = pl.BlockSpec(memory_space=pl.ANY)
    return pl.pallas_call(
        kernel,
        out_shape=(
            jax.ShapeDtypeStruct(queries.shape, BF16),
            jax.ShapeDtypeStruct(queries.shape, BF16),
            jax.ShapeDtypeStruct(vision.shape, F32),
        ),
        in_specs=[hbm, hbm, hbm, hbm, hbm, vmem],
        out_specs=(vmem, vmem, vmem),
        scratch_shapes=list(scratch().values()),
        compiler_params=pltpu.CompilerParams(
            collective_id=0, has_side_effects=True, vmem_limit_bytes=56 * 2**20
        ),
        cost_estimate=pl.CostEstimate(flops=6_000_000_000, bytes_accessed=6_000_000, transcendentals=1_000_000),
    )(vision, key_weight, value_weight, queries, grad_attended, tile_limit.reshape(2, 256))


def solution(mesh):
    return jax.shard_map(
        on_device,
        mesh=mesh,
        in_specs=(
            P("segment", None, "tensor"),
            P("segment", None, "tensor"),
            P("segment", "tensor"),
            P("segment", None, "tensor"),
            P("segment", None, "tensor"),
            P(),
        ),
        out_specs=(
            P("segment", None, "tensor"),
            P("segment", None, "tensor"),
            P("segment", "tensor"),
        ),
        check_vma=False,
    )
```

```python
import jax
import jax.numpy as jnp
from jax import lax
from jax.experimental import pallas as pl
from jax.experimental.pallas import tpu as pltpu
from jax.sharding import PartitionSpec as P

HD = 128
EPS = 1e-05
SCALE = HD ** (-0.5)
LOG2E = 1.4426950408889634
F32 = jnp.float32
BF16 = jnp.bfloat16
MESH = pl.DeviceIdType.MESH

ZW, XW, YW = 256, 384, 384
XO, YO = ZW, ZW + XW


def scratch():
    v, dma = pltpu.VMEM, pltpu.SemaphoreType.DMA
    s = {
        "q": v((8, 256, 128), BF16), "do": v((8, 256, 128), BF16),
        "w": v((4096, 256), BF16), "wt": v((256, 4096), BF16),
        "qt": v((8, 128, 256), BF16), "dot": v((8, 128, 256), BF16),
        "bias": v((4, 16, 256), F32),
        "part": v((512, 256), F32), "part_in": v((512, 256), F32),
        "kv": v((2, 512, 128), BF16), "kvt": v((2, 128, 512), BF16),
        "probs": v((512, 2048), BF16), "dsc": v((512, 2048), BF16), "at": v((8, 128, 256), BF16),
        "dkv": v((512, 256), BF16), "dkv_in": v((512, 256), BF16),
        "att_v": v((256, 1024), BF16), "dq_v": v((256, 1024), BF16), "gv_v": v((16, 1024), F32),
        "gz": v((2, 8, 2, 4, 16, ZW), BF16), "pz": v((2, 8, 2, 4, 16, ZW), BF16),
        "rz1": v((2, 2, 4, 2, 4, 16, ZW), BF16), "rzy": v((2, 4, 4, 16, ZW), BF16),
        "tz": v((2, 4, 16, ZW), BF16), "rzx": v((4, 16, ZW), BF16),
        "gx": v((2, 8, 8, 16, XW), BF16), "gy": v((2, 8, 8, 16, YW), BF16),
        "px": v((2, 8, 8, 16, XW), BF16), "py": v((2, 8, 8, 16, YW), BF16),
        "r1o": v((2, 2, 8, 16, XW), BF16), "r1n": v((2, 2, 2, 8, 16, XW), BF16),
        "r1yo": v((2, 2, 8, 16, YW), BF16), "r1yn": v((2, 2, 4, 8, 16, YW), BF16),
        "sx": v((2, 2, 8, 16, XW), BF16), "sy": v((2, 4, 8, 16, YW), BF16),
        "r2x": v((2, 4, 8, 16, XW), BF16), "r2y": v((2, 4, 8, 16, YW), BF16),
        "tx": v((2, 8, 16, XW), BF16), "ty": v((2, 8, 16, YW), BF16),
        "r3x": v((8, 16, XW), BF16), "r3y": v((8, 16, YW), BF16),
        "lsem": dma((8,)), "osem": dma((3,)),
        "ss1": dma((2, 8)), "rs1": dma((2, 2, 8)),
        "ss2": dma((2, 2, 4)), "rs2x": dma((2, 2)), "rs2y": dma((2, 4)),
        "ss3": dma((2, 2, 2, 3)), "rs3x": dma((2, 2, 3)), "rs3y": dma((2, 2, 2)),
        "ss4": dma((4,)), "rs4": dma((4,)),
        "ssr1": dma((2, 2, 6)), "rsr1x": dma((2, 3, 2)), "rsr1y": dma((2, 5)),
        "ssr2": dma((2, 2, 4)), "rsr2x": dma((2, 4)), "rsr2y": dma((2, 4)),
        "ssr3": dma((2, 2, 8)), "rsr3": dma((2, 8)),
        "ssz1": dma((4,)), "rsz1": dma((2, 4)), "ssz2": dma((2, 4)), "rsz2": dma((2, 2)),
        "ssz3": dma((2, 2, 4)), "rsz3": dma((2, 2, 4)),
        "ssrz1": dma((2, 2, 4)), "rsrz1": dma((2, 2, 4)),
        "ssrz2": dma((2, 2)), "rsrz2": dma((2, 4)), "ssrz3": dma((2, 4)), "rsrz3": dma((4,)),
    }
    return s


NAMES = tuple(scratch())


def mm(a, b):
    return jnp.dot(a, b, preferred_element_type=F32)


def kernel(vis, wk, wv, q_in, do_in, lim, att_o, dq_o, gv_o, *rest):
    R = dict(zip(NAMES, rest, strict=True))
    q, do, w, wt = R["q"], R["do"], R["w"], R["wt"]
    gx, gy, gz, px, py, pz = (R[n] for n in ("gx", "gy", "gz", "px", "py", "pz"))

    seg, ten = lax.axis_index("segment"), lax.axis_index("tensor")
    zh, x, c = lax.div(seg, 8), lax.rem(lax.div(seg, 2), 4), lax.rem(seg, 2)
    y, zl = lax.div(ten, 2), lax.rem(ten, 2)
    z = zh * 2 + zl
    zi = zl * 4 + zh
    h, yp = lax.div(y, 2), lax.rem(y, 2)
    role = lax.rem(y + 4 - 2 * c, 4)
    home = c == h

    def dev(xx, yy, zz, cc):
        return (lax.div(zz, 2) * 8 + xx * 2 + cc, yy * 2 + lax.rem(zz, 2))

    def zind(zz):
        return lax.rem(zz, 2) * 4 + lax.div(zz, 2)

    def xo(d):
        return lax.rem(x + d + 4, 4)

    def yo(d):
        return lax.rem(y + d + 4, 4)

    def zo(d):
        return lax.rem(z + d + 8, 8)

    partner = dev(x, y, z, 1 - c)

    def rdma(src, dst, ss, rs, to):
        return pltpu.make_async_remote_copy(
            src_ref=src, dst_ref=dst, send_sem=ss, recv_sem=rs, device_id=to, device_id_type=MESH
        )

    def arrived(dst, rs):
        rdma(dst, dst, R["ss4"].at[0], rs, partner).wait_recv()

    def begin(cp):
        cp.start()

    def sent(cp):
        cp.wait_send()

    lsem = R["lsem"]
    wcopies = [
        pltpu.make_async_copy(wk.at[0], w.at[:, pl.ds(0, HD)], lsem.at[0]),
        pltpu.make_async_copy(wv.at[0], w.at[:, pl.ds(HD, HD)], lsem.at[1]),
    ]

    barrier = pltpu.get_barrier_semaphore()
    greet = [dev(x, y, zo(d), cc) for d in range(1, 8) for cc in (0, 1)]
    greet += [dev(xo(d), y, z, cc) for d in range(1, 4) for cc in (0, 1)]
    greet += [dev(x, yo(d), z, c) for d in range(1, 4)] + [partner]
    for other in greet:
        pl.semaphore_signal(barrier, inc=1, device_id=other, device_id_type=MESH)
    for cp in wcopies:
        cp.start()
    loads = [
        pltpu.make_async_copy(q_in.at[0], R["att_v"], lsem.at[2]),
        pltpu.make_async_copy(do_in.at[0], R["dq_v"], lsem.at[3]),
    ]
    for cp in loads:
        cp.start()
    pl.semaphore_wait(barrier, len(greet))

    def z1(d):
        return rdma(vis.at[:, pl.ds(0, ZW)], gz.at[c, zi, yp, x], R["ssz1"].at[d], R["rsz1"].at[c, x], dev(xo(d), y, z, h))

    def z1_all(act):
        for d in (2, 1, 3):
            act(z1(d))

        @pl.when(c == 1 - h)
        def _():
            act(z1(0))

    def g1(route, d):
        src, dst = (
            (vis.at[:, pl.ds(XO, XW)], gx.at[c, x * 2 + yp, zi]),
            (vis.at[:, pl.ds(YO, YW)], gy.at[c, yp * 4 + x, zi]),
        )[route]
        return rdma(src, dst, R["ss1"].at[route, d], R["rs1"].at[c, route, zi], dev(x, y, zo(d), h))

    def g1_all(route, act):
        for d in (4, 3, 5, 2, 6, 1, 7):
            act(g1(route, d))

        @pl.when(c == 1 - h)
        def _():
            act(g1(route, 0))

    z1_all(begin)
    for route in range(2):
        g1_all(route, begin)

    @pl.when(home)
    def _():
        pltpu.make_async_copy(vis.at[:, pl.ds(0, ZW)], gz.at[c, zi, yp, x], R["rsz1"].at[c, x]).start()
        pltpu.make_async_copy(vis.at[:, pl.ds(XO, XW)], gx.at[c, x * 2 + yp, zi], R["rs1"].at[c, 0, zi]).start()
        pltpu.make_async_copy(vis.at[:, pl.ds(YO, YW)], gy.at[c, yp * 4 + x, zi], R["rs1"].at[c, 1, zi]).start()

    for cp in loads:
        cp.wait()
    qt, dot_, bias = R["qt"], R["dot"], R["bias"]

    @pl.loop(0, 8)
    def _(n):
        lanes = pl.ds(pl.multiple_of(n * HD, HD), HD)
        qn = R["att_v"][:, lanes]
        dn = R["dq_v"][:, lanes]
        q[n] = qn
        do[n] = dn
        qt[n] = qn.astype(F32).T.astype(BF16)
        dot_[n] = dn.astype(F32).T.astype(BF16)

    def z2(r, d):
        blk = gz.at[r, zi, yp]
        return rdma(blk, blk, R["ssz2"].at[r, d], R["rsz2"].at[r, yp], dev(x, yo(d), z, c))

    @pl.when(home)
    def _():
        for r in range(2):
            for xx in range(4):
                arrived(gz.at[r, zi, yp, xx], R["rsz1"].at[r, xx])
            for d in (2, 1, 3):
                z2(r, d).start()

    def g2x(r, d):
        blk = gx.at[r, x * 2 + yp]
        return rdma(blk, blk, R["ss2"].at[r, 0, d], R["rs2x"].at[r, yp], dev(x, yo(d), z, c))

    def g2y(r, d):
        blk = gy.at[r, yp * 4 + x]
        return rdma(blk, blk, R["ss2"].at[r, 1, d], R["rs2y"].at[r, x], dev(xo(d), y, z, c))

    def step2(r):
        @pl.when(home)
        def _():
            for zz in range(8):
                arrived(gx.at[r, x * 2 + yp, zz], R["rs1"].at[r, 0, zz])
            for d in (2, 1, 3):
                g2x(r, d).start()
            for zz in range(8):
                arrived(gy.at[r, yp * 4 + x, zz], R["rs1"].at[r, 1, zz])
            for d in (2, 1, 3):
                g2y(r, d).start()

    def z3(r, d, s):
        side = 1 - 2 * d
        at = zind(zo(-side * s))
        blk = gz.at[r, at] if s < 3 else gz.at[r, at, d]
        return rdma(blk, blk, R["ssz3"].at[r, d, s], R["rsz3"].at[r, d, s], dev(x, y, zo(side), c))

    def z3_arrived(r, d, s):
        at = zind(zo(-(1 - 2 * d) * (s + 1)))
        arrived(gz.at[r, at] if s < 3 else gz.at[r, at, d], R["rsz3"].at[r, d, s])

    def zstep(r, s):
        if s == 0:
            for k in range(2):
                @pl.when(role != k)
                def _():
                    arrived(gz.at[r, zi, k], R["rsz2"].at[r, k])
        for d in range(2):
            if s > 0:
                z3_arrived(r, d, s - 1)
            z3(r, d, s).start()

    def g3x(r, d, half):
        blk = gx.at[r, x * 2 + half]
        return rdma(blk, blk, R["ss3"].at[r, 0, d, half], R["rs3x"].at[r, d, half], dev(xo(1 - 2 * d), y, z, c))

    def g3xf(r, d):
        blk = gx.at[r, xo(2 * d - 1) * 2 + d]
        return rdma(blk, blk, R["ss3"].at[r, 0, d, 2], R["rs3x"].at[r, d, 2], dev(xo(1 - 2 * d), y, z, c))

    def half_y(k, j):
        return pl.ds(k * 4 + j * 2, 2)

    def g3y(r, k, j, d):
        blk = gy.at[r, half_y(k, j)]
        return rdma(blk, blk, R["ss3"].at[r, 1, d, j], R["rs3y"].at[r, k, j], dev(x, yo(1 - 2 * d), z, c))

    def g3y_role(r, o):
        order = ((0, 0, 0), (0, 1, 1), (0, 1, 0), (0, 0, 1)) if o == 0 else ((1, 0, 1), (1, 1, 0), (1, 1, 1), (1, 0, 0))
        return [g3y(r, k, j, d) for k, j, d in order]

    passed = ((1, 0, 1), (0, 0, 0), (1, 1, 0), (0, 1, 1))

    def g3yf(r, o):
        k, j, d = passed[o]
        blk = gy.at[r, half_y(k, j)]
        return rdma(blk, blk, R["ss3"].at[r, 1, d, 2], R["rs3y"].at[r, k, j], dev(x, yo(1 - 2 * d), z, c))

    def step3(r):
        for k in range(2):
            @pl.when(role != k)
            def _():
                arrived(gx.at[r, x * 2 + k], R["rs2x"].at[r, k])
        for d, half in ((0, 0), (1, 1), (0, 1), (1, 0)):
            g3x(r, d, half).start()
        for o in (0, 1):
            @pl.when(role == o)
            def _():
                for d in range(1, 4):
                    arrived(gy.at[r, o * 4 + xo(d)], R["rs2y"].at[r, xo(d)])
                for cp in g3y_role(r, o):
                    cp.start()

    def forward3(r):
        for d in range(2):
            arrived(gx.at[r, xo(2 * d - 1) * 2 + d], R["rs3x"].at[r, d, d])
            g3xf(r, d).start()
        for o in range(4):
            @pl.when(role == o)
            def _():
                k, j, _d = passed[o]
                arrived(gy.at[r, half_y(k, j)], R["rs3y"].at[r, k, j])
                g3yf(r, o).start()

    def rest3(r):
        for d in range(2):
            arrived(gx.at[r, xo(2 * d - 1) * 2 + 1 - d], R["rs3x"].at[r, d, 1 - d])
        for d in range(2):
            arrived(gx.at[r, xo(2) * 2 + d], R["rs3x"].at[r, d, 2])
        for o in range(4):
            @pl.when(role == o)
            def _():
                for k in (0, 1):
                    if o == k:
                        continue
                    for j in (0, 1):
                        if (k, j) != passed[o][:2]:
                            arrived(gy.at[r, half_y(k, j)], R["rs3y"].at[r, k, j])

    part, part_in = R["part"], R["part_in"]
    ROWS = (slice(0, 256), slice(256, 512))

    def project(r, route):
        total = part[ROWS[r], :] if route else jnp.zeros((256, 256), F32)
        for k in range(2):
            for l in range(2):
                base = (k * 2 + l) * 1024
                zs = slice(l * 4, l * 4 + 4)
                if route == 0:
                    a = jnp.concatenate([gz[r, zs, k, xx].reshape(64, ZW) for xx in range(4)], axis=0)
                    total += mm(a, w[base : base + ZW, :])
                elif route == 1:
                    a = jnp.concatenate([gx[r, xx * 2 + k, zs].reshape(64, XW) for xx in range(4)], axis=0)
                    total += mm(a, w[base + XO : base + XO + XW, :])
                else:
                    a = gy[r, k * 4 : k * 4 + 4, zs].reshape(256, YW)
                    total += mm(a, w[base + YO : base + YO + YW, :])
        part[ROWS[r], :] = total

    def swap(r):
        rows = pl.ds(r * 256, 256)
        return rdma(part.at[rows], part_in.at[rows], R["ss4"].at[r], R["rs4"].at[r], partner)

    kv, kvt = R["kv"], R["kvt"]

    def keys_values(r):
        rows = ROWS[r]
        pre = part[rows, :] + part_in[rows, :]
        part_in[rows, :] = pre
        kp = pre[:, :HD]
        inv = lax.rsqrt(jnp.mean(kp * kp, axis=-1, keepdims=True) + EPS)
        keys = (kp * inv).astype(BF16)
        vals = pre[:, HD:].astype(BF16)
        kv[0, rows] = keys
        kv[1, rows] = vals
        kvt[0, :, rows] = keys.astype(F32).T.astype(BF16)
        kvt[1, :, rows] = vals.astype(F32).T.astype(BF16)

    def transpose_weights(lo, hi):
        @pl.loop(lo, hi)
        def _(n):
            rows = pl.ds(pl.multiple_of(n * 256, 256), 256)
            wt[:, rows] = w[rows, :].astype(F32).T.astype(BF16)

    step2(0)
    step2(1)
    zstep(0, 0)
    zstep(1, 0)
    for cp in wcopies:
        cp.wait()
    step3(0)
    transpose_weights(0, 8)
    zstep(0, 1)
    zstep(1, 1)
    step3(1)
    transpose_weights(8, 16)
    limits = lim[...].reshape(1, 512)
    limit = (1 - c) * limits[:, :256] + c * limits[:, 256:]
    for t in range(4):
        bias[t] = jnp.broadcast_to(jnp.where(t < limit, 0.0, -1e30), (16, 256))
    forward3(0)
    zstep(0, 2)
    zstep(1, 2)
    zstep(0, 3)
    zstep(1, 3)
    for d in range(2):
        z3_arrived(0, d, 3)
    project(0, 0)
    forward3(1)
    rest3(0)
    project(0, 1)
    project(0, 2)
    swap(0).start()
    for d in range(2):
        z3_arrived(1, d, 3)
    project(1, 0)
    swap(0).wait()
    keys_values(0)
    rest3(1)
    project(1, 1)
    project(1, 2)
    swap(1).start()
    swap(1).wait()
    keys_values(1)

    probs, dsc, at_ = R["probs"], R["dsc"], R["at"]

    @pl.loop(0, 8, unroll=4)
    def _(n):
        lanes = pl.ds(pl.multiple_of(n * 256, 256), 256)
        dotn = dot_[n]
        s = mm(kv[0], qt[n]) * (SCALE * LOG2E)
        s = (s.reshape(8, 4, 16, 256) + bias[...][None]).reshape(512, 256)
        m = jnp.max(s, axis=0, keepdims=True)
        e = jnp.exp2(s - m)
        prob = e * (1.0 / jnp.sum(e, axis=0, keepdims=True))
        pb16 = prob.astype(BF16)
        probs[:, lanes] = pb16
        at = mm(kvt[1], pb16).astype(BF16)
        at_[n] = at
        dp = mm(kv[1], dotn)
        delta = jnp.sum(at.astype(F32) * dotn.astype(F32), axis=0, keepdims=True)
        dsc[:, lanes] = (prob * (dp - delta)).astype(BF16)

    dkv, dkv_in = R["dkv"], R["dkv_in"]

    def key_grads(r):
        rows = ROWS[r]
        kp = part_in[rows, :HD]
        inv = lax.rsqrt(jnp.mean(kp * kp, axis=-1, keepdims=True) + EPS)
        dk = mm(dsc[rows, :], q[...].reshape(2048, HD)) * SCALE
        dv = mm(probs[rows, :], do[...].reshape(2048, HD))
        dkp = inv * dk - kp * (inv * inv * inv * jnp.mean(kp * dk, axis=-1, keepdims=True))
        dkv[rows, :HD] = dkp.astype(BF16)
        dkv[rows, HD:] = dv.astype(BF16)

    def swap2(r):
        rows = pl.ds(r * 256, 256)
        return rdma(dkv.at[rows], dkv_in.at[rows], R["ss4"].at[2 + r], R["rs4"].at[2 + r], partner)

    def heads_out(lo, hi):
        @pl.loop(lo, hi, unroll=2)
        def _(n):
            lanes = pl.ds(pl.multiple_of(n * HD, HD), HD)
            dqt = mm(kvt[0], dsc[:, pl.ds(pl.multiple_of(n * 256, 256), 256)]) * SCALE
            R["dq_v"][:, lanes] = dqt.T.astype(BF16)
            R["att_v"][:, lanes] = at_[n].astype(F32).T.astype(BF16)

    def back(r, route):
        for k in range(2):
            for l in range(2):
                base = (k * 2 + l) * 1024 + (0, XO, YO)[route]
                n = (ZW, XW, YW)[route]
                zs = slice(l * 4, l * 4 + 4)
                wtb = wt[:, base : base + n]
                v = (mm(dkv[ROWS[r], :], wtb) + mm(dkv_in[ROWS[r], :], wtb)).astype(BF16)
                if route == 2:
                    py[r, k * 4 : k * 4 + 4, zs] = v.reshape(4, 4, 16, YW)
                    continue
                for xx in range(4):
                    b = v[xx * 64 : (xx + 1) * 64].reshape(4, 16, n)
                    if route == 0:
                        pz[r, zs, k, xx] = b
                    else:
                        px[r, xx * 2 + k, zs] = b

    rz1 = R["rz1"]

    def rz(r, d, s):
        side = 1 - 2 * d
        at = zind(zo(side * (4 - s)))
        src = pz.at[r, at, d] if s == 0 else pz.at[r, at]
        dst = rz1.at[r, d, 0, d] if s == 0 else rz1.at[r, d, s]
        return rdma(src, dst, R["ssrz1"].at[r, d, s], R["rsrz1"].at[r, d, s], dev(x, y, zo(side), c))

    def rz_arrived(r, d, s):
        arrived(rz1.at[r, d, 0, d] if s == 0 else rz1.at[r, d, s], R["rsrz1"].at[r, d, s])

    def rzstep(r, s):
        for d in range(2):
            if s > 0:
                rz_arrived(r, d, s - 1)
                at = zind(zo((1 - 2 * d) * (4 - s)))
                if s == 1:
                    pz[r, at, d] = (pz[r, at, d].astype(F32) + rz1[r, d, 0, d].astype(F32)).astype(BF16)
                else:
                    pz[r, at] = (pz[r, at].astype(F32) + rz1[r, d, s - 1].astype(F32)).astype(BF16)
            rz(r, d, s).start()

    def rzy_to(r, k):
        return rdma(
            pz.at[r, zi, k], R["rzy"].at[r, y], R["ssrz2"].at[r, k], R["rsrz2"].at[r, y], dev(x, 2 * c + k, z, c)
        )

    def rz_sum(r):
        for d in range(2):
            rz_arrived(r, d, 3)
        pz[r, zi] = (pz[r, zi].astype(F32) + rz1[r, 0, 3].astype(F32) + rz1[r, 1, 3].astype(F32)).astype(BF16)
        for k in range(2):
            @pl.when(role != k)
            def _():
                rzy_to(r, k).start()

    def rzx_to(r, d):
        return rdma(
            R["tz"].at[r, xo(d)], R["rzx"].at[x], R["ssrz3"].at[r, d], R["rsrz3"].at[x], dev(xo(d), y, z, r)
        )

    def rzx_all(r, act):
        for d in (2, 1, 3):
            act(rzx_to(r, d))

        @pl.when(c != r)
        def _():
            act(rzx_to(r, 0))

    def rz_rows(r):
        @pl.when(home)
        def _():
            v = pz[r, zi, yp].astype(F32)
            for d in range(1, 4):
                arrived(R["rzy"].at[r, yo(d)], R["rsrz2"].at[r, yo(d)])
                v += R["rzy"][r, yo(d)].astype(F32)
            R["tz"][r] = v.astype(BF16)
            rzx_all(r, begin)

            @pl.when(c == r)
            def _():
                pltpu.make_async_copy(R["tz"].at[r, x], R["rzx"].at[x], R["rsrz3"].at[x]).start()

    def r1x_opp(r, d):
        return rdma(
            px.at[r, xo(2) * 2 + d], R["r1o"].at[r, d], R["ssr1"].at[r, 0, d], R["rsr1x"].at[r, 0, d],
            dev(xo(1 - 2 * d), y, z, c),
        )

    def r1x_free(r, d):
        return rdma(
            px.at[r, xo(1 - 2 * d) * 2 + 1 - d], R["r1n"].at[r, d, 1 - d], R["ssr1"].at[r, 0, 2 + d],
            R["rsr1x"].at[r, 1, d], dev(xo(1 - 2 * d), y, z, c),
        )

    def r1x_dep(r, d):
        return rdma(
            px.at[r, xo(1 - 2 * d) * 2 + d], R["r1n"].at[r, d, d], R["ssr1"].at[r, 0, 4 + d],
            R["rsr1x"].at[r, 2, d], dev(xo(1 - 2 * d), y, z, c),
        )

    y_opp = {2: ((1, 0, 0), (0, 0, 1)), 3: ((0, 1, 0), (1, 1, 1))}
    y_free = {0: (0, 1, 1), 1: (1, 0, 1), 2: (1, 1, 0), 3: (0, 0, 0)}
    y_dep = {0: (0, 1, 0), 1: (1, 0, 0), 2: (1, 1, 1), 3: (0, 0, 1)}

    def r1y_opp(r, o, i):
        d, k, j = y_opp[o][i]
        return rdma(
            py.at[r, half_y(k, j)], R["r1yo"].at[r], R["ssr1"].at[r, 1, i], R["rsr1y"].at[r, 0],
            dev(x, yo(1 - 2 * d), z, c),
        )

    def r1y_next(r, o, dep):
        d, k, j = (y_dep if dep else y_free)[o]
        side = 0 if o >= 2 else 1
        return rdma(
            py.at[r, half_y(k, j)], R["r1yn"].at[r, side, pl.ds(j * 2, 2)], R["ssr1"].at[r, 1, 2 + dep],
            R["rsr1y"].at[r, 1 + dep + side * 2], dev(x, yo(1 - 2 * d), z, c),
        )

    def rs1x(r):
        for d in range(2):
            r1x_opp(r, d).start()
        for d in range(2):
            r1x_free(r, d).start()

    def rs1y(r):
        for o in (2, 3):
            @pl.when(role == o)
            def _():
                for i in range(2):
                    r1y_opp(r, o, i).start()
        for o in range(4):
            @pl.when(role == o)
            def _():
                r1y_next(r, o, 0).start()

    def rs1_dep(r):
        r1o, r1yo = R["r1o"], R["r1yo"]
        for d in range(2):
            arrived(r1o.at[r, d], R["rsr1x"].at[r, 0, d])
            to = xo(1 - 2 * d) * 2 + d

            @pl.loop(0, 8, unroll=2)
            def _(i):
                px[r, to, i] = (px[r, to, i].astype(F32) + r1o[r, d, i].astype(F32)).astype(BF16)

            r1x_dep(r, d).start()
        arrived(r1yo.at[r], R["rsr1y"].at[r, 0])
        for o in range(4):
            @pl.when(role == o)
            def _():
                _d, k, j = y_dep[o]

                @pl.loop(0, 8)
                def _(i):
                    for xx in range(2):
                        at = k * 4 + j * 2 + xx
                        py[r, at, i] = (py[r, at, i].astype(F32) + r1yo[r, xx, i].astype(F32)).astype(BF16)

                r1y_next(r, o, 1).start()

    sx, sy, r2x, r2y, tx, ty = (R[n] for n in ("sx", "sy", "r2x", "r2y", "tx", "ty"))

    def r2x_to(r, k):
        return rdma(
            sx.at[r, k], r2x.at[r, y], R["ssr2"].at[r, 0, k], R["rsr2x"].at[r, y], dev(x, 2 * c + k, z, c)
        )

    def r2y_to(r, d):
        return rdma(
            sy.at[r, xo(d)], r2y.at[r, x], R["ssr2"].at[r, 1, d], R["rsr2y"].at[r, x], dev(xo(d), y, z, c)
        )

    def rs2(r):
        r1n, r1yn = R["r1n"], R["r1yn"]
        for d in range(2):
            arrived(r1n.at[r, d, 1 - d], R["rsr1x"].at[r, 1, d])
        for d in range(2):
            arrived(r1n.at[r, d, d], R["rsr1x"].at[r, 2, d])

        @pl.loop(0, 8)
        def _(b):
            for k in range(2):
                sx[r, k, b] = (
                    px[r, x * 2 + k, b].astype(F32) + r1n[r, 0, k, b].astype(F32) + r1n[r, 1, k, b].astype(F32)
                ).astype(BF16)

        for k in range(2):
            @pl.when(role != k)
            def _():
                r2x_to(r, k).start()

        @pl.when(home)
        def _():
            arrived(r1yn.at[r, 0, pl.ds(0, 2)], R["rsr1y"].at[r, 1])
            arrived(r1yn.at[r, 1, pl.ds(2, 2)], R["rsr1y"].at[r, 3])
            arrived(r1yn.at[r, 0, pl.ds(2, 2)], R["rsr1y"].at[r, 2])
            arrived(r1yn.at[r, 1, pl.ds(0, 2)], R["rsr1y"].at[r, 4])

            @pl.loop(0, 8)
            def _(b):
                for k in range(4):
                    sy[r, k, b] = (
                        py[r, yp * 4 + k, b].astype(F32) + r1yn[r, 0, k, b].astype(F32) + r1yn[r, 1, k, b].astype(F32)
                    ).astype(BF16)

            for d in (2, 1, 3):
                r2y_to(r, d).start()

    def r3_to(r, route, d):
        t, dst = ((tx, R["r3x"]), (ty, R["r3y"]))[route]
        zz = zo(d)
        return rdma(
            t.at[r, zind(zz)], dst.at[zi], R["ssr3"].at[r, route, d], R["rsr3"].at[route, zi], dev(x, y, zz, r)
        )

    def r3_all(r, route, act):
        for d in (4, 3, 5, 2, 6, 1, 7):
            act(r3_to(r, route, d))

        @pl.when(c != r)
        def _():
            act(r3_to(r, route, 0))

    def r3_own(r, route):
        t, dst = ((tx, R["r3x"]), (ty, R["r3y"]))[route]

        @pl.when(c == r)
        def _():
            pltpu.make_async_copy(t.at[r, zi], dst.at[zi], R["rsr3"].at[route, zi]).start()

    def rs3(r):
        @pl.when(home)
        def _():
            for d in range(1, 4):
                arrived(r2x.at[r, yo(d)], R["rsr2x"].at[r, yo(d)])

            @pl.loop(0, 8, unroll=2)
            def _(b):
                v = sx[r, yp, b].astype(F32)
                for d in range(1, 4):
                    v += r2x[r, yo(d), b].astype(F32)
                tx[r, b] = v.astype(BF16)

            r3_all(r, 0, begin)
            r3_own(r, 0)
            for d in range(1, 4):
                arrived(r2y.at[r, xo(d)], R["rsr2y"].at[r, xo(d)])

            @pl.loop(0, 8, unroll=2)
            def _(b):
                v = sy[r, x, b].astype(F32)
                for d in range(1, 4):
                    v += r2y[r, xo(d), b].astype(F32)
                ty[r, b] = v.astype(BF16)

            r3_all(r, 1, begin)
            r3_own(r, 1)

    def finish(route):
        src, n, o = ((R["r3x"], XW, XO), (R["r3y"], YW, YO))[route]
        for b in range(8):
            arrived(src.at[b], R["rsr3"].at[route, b])
        total = src[0].astype(F32)
        for b in range(1, 8):
            total += src[b].astype(F32)
        R["gv_v"][:, o : o + n] = total

    def finish_z():
        for b in range(4):
            arrived(R["rzx"].at[b], R["rsrz3"].at[b])
        total = R["rzx"][0].astype(F32)
        for b in range(1, 4):
            total += R["rzx"][b].astype(F32)
        R["gv_v"][:, :ZW] = total

    outs = [
        pltpu.make_async_copy(R["att_v"], att_o.at[0], R["osem"].at[0]),
        pltpu.make_async_copy(R["dq_v"], dq_o.at[0], R["osem"].at[1]),
        pltpu.make_async_copy(R["gv_v"], gv_o, R["osem"].at[2]),
    ]

    key_grads(0)
    swap2(0).start()
    key_grads(1)
    swap2(1).start()
    swap2(0).wait()
    for r in range(2):
        if r == 1:
            swap2(1).wait()
        back(r, 0)
        for d in range(2):
            rz(r, d, 0).start()
        back(r, 1)
        rs1x(r)
        back(r, 2)
        rs1y(r)
    heads_out(0, 4)
    rs1_dep(0)
    rzstep(0, 1)
    rzstep(1, 1)
    heads_out(4, 8)
    for cp in outs[:2]:
        cp.start()
    rs1_dep(1)
    rzstep(0, 2)
    rzstep(1, 2)
    rs2(0)
    rzstep(0, 3)
    rzstep(1, 3)
    rs2(1)
    rs3(0)
    rz_sum(0)
    rz_sum(1)
    rz_rows(0)
    rz_rows(1)
    rs3(1)
    finish_z()
    finish(0)
    finish(1)
    outs[2].start()

    z1_all(sent)
    for route in range(2):
        g1_all(route, sent)
    for r in range(2):
        @pl.when(home)
        def _():
            for d in range(1, 4):
                sent(z2(r, d))
                sent(g2x(r, d))
                sent(g2y(r, d))
                sent(r2y_to(r, d))
            for route in range(2):
                r3_all(r, route, sent)
            rzx_all(r, sent)

        for d in range(2):
            for s in range(4):
                sent(z3(r, d, s))
                sent(rz(r, d, s))
            for half in range(2):
                sent(g3x(r, d, half))
            sent(g3xf(r, d))
            sent(r1x_opp(r, d))
            sent(r1x_free(r, d))
            sent(r1x_dep(r, d))
        for o in range(4):
            @pl.when(role == o)
            def _():
                if o < 2:
                    for cp in g3y_role(r, o):
                        sent(cp)
                else:
                    for i in range(2):
                        sent(r1y_opp(r, o, i))
                sent(g3yf(r, o))
                sent(r1y_next(r, o, 0))
                sent(r1y_next(r, o, 1))
        for k in range(2):
            @pl.when(role != k)
            def _():
                sent(r2x_to(r, k))
                sent(rzy_to(r, k))
    for cp in outs:
        cp.wait()


def copy_out(a, b, d, ao, bo, do, av, bv, dv, sems):
    moves = ((a, av, ao), (b, bv, bo), (d, dv, do))
    loads = [pltpu.make_async_copy(s, v, sems.at[0, i]) for i, (s, v, _) in enumerate(moves)]
    stores = [pltpu.make_async_copy(v, t, sems.at[1, i]) for i, (_, v, t) in enumerate(moves)]
    for cp in loads:
        cp.start()
    for load, store in zip(loads, stores):
        load.wait()
        store.start()
    for cp in stores:
        cp.wait()


def on_device(queries, grad_attended, vision, key_weight, value_weight, tile_limit):
    vmem = pl.BlockSpec(memory_space=pltpu.VMEM)
    hbm = pl.BlockSpec(memory_space=pl.ANY)
    shapes = (
        jax.ShapeDtypeStruct(queries.shape, BF16),
        jax.ShapeDtypeStruct(queries.shape, BF16),
        jax.ShapeDtypeStruct(vision.shape, F32),
    )
    outs = pl.pallas_call(
        kernel,
        out_shape=shapes,
        in_specs=[hbm, hbm, hbm, hbm, hbm, vmem],
        out_specs=(hbm, hbm, hbm),
        scratch_shapes=list(scratch().values()),
        compiler_params=pltpu.CompilerParams(
            collective_id=0, has_side_effects=True, vmem_limit_bytes=60 * 2**20
        ),
        cost_estimate=pl.CostEstimate(flops=6_000_000_000, bytes_accessed=6_000_000, transcendentals=1_000_000),
    )(vision, key_weight, value_weight, queries, grad_attended, tile_limit)
    return pl.pallas_call(
        copy_out,
        out_shape=shapes,
        in_specs=[hbm, hbm, hbm],
        out_specs=(hbm, hbm, hbm),
        scratch_shapes=[pltpu.VMEM(s.shape, s.dtype) for s in shapes] + [pltpu.SemaphoreType.DMA((2, 3))],
    )(*outs)


def solution(mesh):
    return jax.shard_map(
        on_device,
        mesh=mesh,
        in_specs=(
            P("segment", None, "tensor"),
            P("segment", None, "tensor"),
            P("segment", "tensor"),
            P("segment", None, "tensor"),
            P("segment", None, "tensor"),
            P(),
        ),
        out_specs=(
            P("segment", None, "tensor"),
            P("segment", None, "tensor"),
            P("segment", "tensor"),
        ),
        check_vma=False,
    )
```

```python
import jax
import jax.numpy as jnp
from jax import lax
from jax.experimental import pallas as pl
from jax.experimental.pallas import tpu as pltpu
from jax.sharding import PartitionSpec as P

HD = 128
EPS = 1e-05
SCALE = HD ** (-0.5)
LOG2E = 1.4426950408889634
F32 = jnp.float32
BF16 = jnp.bfloat16
MESH = pl.DeviceIdType.MESH

ZW, XW, YW = 256, 384, 384
XO, YO = ZW, ZW + XW


def scratch():
    v, dma = pltpu.VMEM, pltpu.SemaphoreType.DMA
    s = {
        "q": v((8, 256, 128), BF16), "do": v((8, 256, 128), BF16),
        "w": v((4096, 256), BF16), "wt": v((256, 4096), BF16),
        "qt": v((8, 128, 256), BF16), "dot": v((8, 128, 256), BF16),
        "bias": v((4, 16, 256), F32),
        "part": v((512, 256), F32), "part_in": v((512, 256), F32),
        "kv": v((2, 512, 128), BF16), "kvt": v((2, 128, 512), BF16),
        "probs": v((512, 2048), BF16), "dsc": v((512, 2048), BF16), "at": v((8, 128, 256), BF16),
        "dkv": v((512, 256), BF16), "dkv_in": v((512, 256), BF16),
        "att_v": v((256, 1024), BF16), "dq_v": v((256, 1024), BF16), "gv_v": v((16, 1024), F32),
        "gz": v((2, 8, 2, 4, 16, ZW), BF16), "pz": v((2, 8, 2, 4, 16, ZW), BF16),
        "rz1": v((2, 2, 4, 2, 4, 16, ZW), BF16), "rzy": v((2, 4, 4, 16, ZW), BF16),
        "tz": v((2, 4, 16, ZW), BF16), "rzx": v((4, 16, ZW), BF16),
        "gx": v((2, 8, 8, 16, XW), BF16), "gy": v((2, 8, 8, 16, YW), BF16),
        "px": v((2, 8, 8, 16, XW), BF16), "py": v((2, 8, 8, 16, YW), BF16),
        "r1o": v((2, 2, 8, 16, XW), BF16), "r1n": v((2, 2, 2, 8, 16, XW), BF16),
        "r1yo": v((2, 2, 8, 16, YW), BF16), "r1yn": v((2, 2, 4, 8, 16, YW), BF16),
        "sx": v((2, 2, 8, 16, XW), BF16), "sy": v((2, 4, 8, 16, YW), BF16),
        "r2x": v((2, 4, 8, 16, XW), BF16), "r2y": v((2, 4, 8, 16, YW), BF16),
        "tx": v((2, 8, 16, XW), BF16), "ty": v((2, 8, 16, YW), BF16),
        "r3x": v((8, 16, XW), BF16), "r3y": v((8, 16, YW), BF16),
        "lsem": dma((4,)), "osem": dma((3,)), "ss4": dma((4,)), "rs4": dma((4,)),
        "ssz1": dma((1,)), "ss1": dma((2,)), "ssz2": dma((2,)), "ss2": dma((2, 2)), "ss3": dma((2, 2)),
        "ssz3": dma((2,)), "ssrz1": dma((2,)), "ssr1": dma((2, 2)), "ssr2": dma((2, 2)), "ssr3": dma((2, 2)),
        "ssrz2": dma((2,)), "ssrz3": dma((2,)),
        "rsz1": dma((2,)), "rs1": dma((2, 2)), "rsz2": dma((2,)), "rs2x": dma((2,)), "rs2y": dma((2,)),
        "rs3x": dma((2, 3)), "rs3y": dma((2, 2)), "rsz3": dma((2, 7)),
        "rsrz1": dma((2, 7)), "rsr1x": dma((2, 3)), "rsr1y": dma((2, 2)), "rsr2x": dma((2,)), "rsr2y": dma((2,)),
        "rsr3": dma((2,)), "rsrz2": dma((2,)), "rsrz3": dma((1,)),
    }
    return s


NAMES = tuple(scratch())


def mm(a, b):
    return jnp.dot(a, b, preferred_element_type=F32)


def kernel(vis, wk, wv, q_in, do_in, lim, att_o, dq_o, gv_o, *rest):
    R = dict(zip(NAMES, rest, strict=True))
    q, do, w, wt = R["q"], R["do"], R["w"], R["wt"]
    gx, gy, gz, px, py, pz = (R[n] for n in ("gx", "gy", "gz", "px", "py", "pz"))

    seg, ten = lax.axis_index("segment"), lax.axis_index("tensor")
    zh, x, c = lax.div(seg, 8), lax.rem(lax.div(seg, 2), 4), lax.rem(seg, 2)
    y, zl = lax.div(ten, 2), lax.rem(ten, 2)
    z = zh * 2 + zl
    zi = zl * 4 + zh
    h, yp = lax.div(y, 2), lax.rem(y, 2)
    role = lax.rem(y + 4 - 2 * c, 4)
    home = c == h

    def dev(xx, yy, zz, cc):
        return (lax.div(zz, 2) * 8 + xx * 2 + cc, yy * 2 + lax.rem(zz, 2))

    def zind(zz):
        return lax.rem(zz, 2) * 4 + lax.div(zz, 2)

    def xo(d):
        return lax.rem(x + d + 4, 4)

    def yo(d):
        return lax.rem(y + d + 4, 4)

    def zo(d):
        return lax.rem(z + d + 8, 8)

    partner = dev(x, y, z, 1 - c)

    def rdma(src, dst, ss, rs, to):
        return pltpu.make_async_remote_copy(
            src_ref=src, dst_ref=dst, send_sem=ss, recv_sem=rs, device_id=to, device_id_type=MESH
        )

    def arrived(dst, rs):
        rdma(dst, dst, R["ss4"].at[0], rs, partner).wait_recv()

    def begin(cp):
        cp.start()

    def sent(ref, ss):
        rdma(ref, ref, ss, R["rs4"].at[0], partner).wait_send()

    lsem = R["lsem"]
    wcopies = [
        pltpu.make_async_copy(wk.at[0], w.at[:, pl.ds(0, HD)], lsem.at[0]),
        pltpu.make_async_copy(wv.at[0], w.at[:, pl.ds(HD, HD)], lsem.at[1]),
    ]

    barrier = pltpu.get_barrier_semaphore()
    greet = [dev(x, y, zo(d), cc) for d in range(1, 8) for cc in (0, 1)]
    greet += [dev(xo(d), y, z, cc) for d in range(1, 4) for cc in (0, 1)]
    greet += [dev(x, yo(d), z, c) for d in range(1, 4)] + [partner]
    for other in greet:
        pl.semaphore_signal(barrier, inc=1, device_id=other, device_id_type=MESH)
    for cp in wcopies:
        cp.start()
    loads = [
        pltpu.make_async_copy(q_in.at[0], R["att_v"], lsem.at[2]),
        pltpu.make_async_copy(do_in.at[0], R["dq_v"], lsem.at[3]),
    ]
    for cp in loads:
        cp.start()
    pl.semaphore_wait(barrier, len(greet))

    def z1(d):
        return rdma(vis.at[:, pl.ds(0, ZW)], gz.at[c, zi, yp, x], R["ssz1"].at[0], R["rsz1"].at[c], dev(xo(d), y, z, h))

    def z1_all(act):
        for d in (2, 1, 3):
            act(z1(d))

        @pl.when(c == 1 - h)
        def _():
            act(z1(0))

    def g1(route, d):
        src, dst = (
            (vis.at[:, pl.ds(XO, XW)], gx.at[c, x * 2 + yp, zi]),
            (vis.at[:, pl.ds(YO, YW)], gy.at[c, yp * 4 + x, zi]),
        )[route]
        return rdma(src, dst, R["ss1"].at[route], R["rs1"].at[c, route], dev(x, y, zo(d), h))

    def g1_all(route, act):
        for d in (4, 3, 5, 2, 6, 1, 7):
            act(g1(route, d))

        @pl.when(c == 1 - h)
        def _():
            act(g1(route, 0))

    z1_all(begin)
    for route in range(2):
        g1_all(route, begin)

    @pl.when(home)
    def _():
        pltpu.make_async_copy(vis.at[:, pl.ds(0, ZW)], gz.at[c, zi, yp, x], R["rsz1"].at[c]).start()
        pltpu.make_async_copy(vis.at[:, pl.ds(XO, XW)], gx.at[c, x * 2 + yp, zi], R["rs1"].at[c, 0]).start()
        pltpu.make_async_copy(vis.at[:, pl.ds(YO, YW)], gy.at[c, yp * 4 + x, zi], R["rs1"].at[c, 1]).start()

    for cp in loads:
        cp.wait()
    qt, dot_, bias = R["qt"], R["dot"], R["bias"]

    @pl.loop(0, 8)
    def _(n):
        lanes = pl.ds(pl.multiple_of(n * HD, HD), HD)
        qn = R["att_v"][:, lanes]
        dn = R["dq_v"][:, lanes]
        q[n] = qn
        do[n] = dn
        qt[n] = qn.astype(F32).T.astype(BF16)
        dot_[n] = dn.astype(F32).T.astype(BF16)

    def z2(r, d):
        blk = gz.at[r, zi, yp]
        return rdma(blk, blk, R["ssz2"].at[r], R["rsz2"].at[r], dev(x, yo(d), z, c))

    @pl.when(home)
    def _():
        for r in range(2):
            arrived(gz.at[r, zi, yp], R["rsz1"].at[r])
            for d in (2, 1, 3):
                z2(r, d).start()

    def g2x(r, d):
        blk = gx.at[r, x * 2 + yp]
        return rdma(blk, blk, R["ss2"].at[r, 0], R["rs2x"].at[r], dev(x, yo(d), z, c))

    def g2y(r, d):
        blk = gy.at[r, yp * 4 + x]
        return rdma(blk, blk, R["ss2"].at[r, 1], R["rs2y"].at[r], dev(xo(d), y, z, c))

    def step2x(r):
        @pl.when(home)
        def _():
            arrived(gx.at[r, x * 2 + yp], R["rs1"].at[r, 0])
            for d in (2, 1, 3):
                g2x(r, d).start()

    def step2y(r):
        @pl.when(home)
        def _():
            arrived(gy.at[r, yp * 4 + x], R["rs1"].at[r, 1])
            for d in (2, 1, 3):
                g2y(r, d).start()

    def by_home(few, many):
        @pl.when(home)
        def _():
            few()

        @pl.when(c == 1 - h)
        def _():
            many()

    def z3(r, d, s):
        side = 1 - 2 * d
        at = zind(zo(-side * s))
        blk = gz.at[r, at] if s < 3 else gz.at[r, at, d]
        return rdma(blk, blk, R["ssz3"].at[r], R["rsz3"].at[r, s * 2 + d if s < 3 else 6], dev(x, y, zo(side), c))

    def z3_arrived(r, d, s):
        arrived(gz.at[r, zind(zo(-(1 - 2 * d) * (s + 1)))], R["rsz3"].at[r, s * 2 + d])

    def z3_last(r):
        arrived(gz.at[r, zind(zo(4))], R["rsz3"].at[r, 6])

    def zstep(r, s):
        if s == 0:
            by_home(
                lambda: arrived(gz.at[r, zi, 1 - yp], R["rsz2"].at[r]),
                lambda: arrived(gz.at[r, zi], R["rsz2"].at[r]),
            )
        for d in range(2):
            if s > 0:
                z3_arrived(r, d, s - 1)
            z3(r, d, s).start()

    def g3x(r, d, half):
        blk = gx.at[r, x * 2 + half]
        return rdma(blk, blk, R["ss3"].at[r, 0], R["rs3x"].at[r, d if half == d else 2], dev(xo(1 - 2 * d), y, z, c))

    def g3xf(r, d):
        blk = gx.at[r, xo(2 * d - 1) * 2 + d]
        return rdma(blk, blk, R["ss3"].at[r, 0], R["rs3x"].at[r, 2], dev(xo(1 - 2 * d), y, z, c))

    def half_y(k, j):
        return pl.ds(k * 4 + j * 2, 2)

    passed = ((1, 0, 1), (0, 0, 0), (1, 1, 0), (0, 1, 1))

    def g3y(r, o, k, j, d):
        blk = gy.at[r, half_y(k, j)]
        first = passed[(o + 1 - 2 * d) % 4][:2] == (k, j)
        return rdma(blk, blk, R["ss3"].at[r, 1], R["rs3y"].at[r, 0 if first else 1], dev(x, yo(1 - 2 * d), z, c))

    def g3y_role(r, o):
        order = ((0, 0, 0), (0, 1, 1), (0, 1, 0), (0, 0, 1)) if o == 0 else ((1, 0, 1), (1, 1, 0), (1, 1, 1), (1, 0, 0))
        return [g3y(r, o, k, j, d) for k, j, d in order]

    def g3yf(r, o):
        k, j, d = passed[o]
        return g3y(r, o, k, j, d)

    def step3x(r):
        by_home(
            lambda: arrived(gx.at[r, x * 2 + 1 - yp], R["rs2x"].at[r]),
            lambda: arrived(gx.at[r, pl.ds(x * 2, 2)], R["rs2x"].at[r]),
        )
        for d, half in ((0, 0), (1, 1), (0, 1), (1, 0)):
            g3x(r, d, half).start()

    def step3y(r):
        for o in (0, 1):
            @pl.when(role == o)
            def _():
                arrived(gy.at[r, pl.ds(o * 4, 3)], R["rs2y"].at[r])
                for cp in g3y_role(r, o):
                    cp.start()

    def forward3x(r):
        for d in range(2):
            arrived(gx.at[r, xo(2 * d - 1) * 2 + d], R["rs3x"].at[r, d])
            g3xf(r, d).start()

    def forward3y(r):
        for o in range(4):
            @pl.when(role == o)
            def _():
                arrived(gy.at[r, half_y(*passed[o][:2])], R["rs3y"].at[r, 0])
                g3yf(r, o).start()

    def rest3x(r):
        arrived(gx.at[r, pl.ds(0, 4)], R["rs3x"].at[r, 2])

    def rest3y(r):
        by_home(
            lambda: arrived(gy.at[r, pl.ds(0, 2)], R["rs3y"].at[r, 1]),
            lambda: arrived(gy.at[r, pl.ds(0, 6)], R["rs3y"].at[r, 1]),
        )

    part, part_in = R["part"], R["part_in"]
    ROWS = (slice(0, 256), slice(256, 512))

    def project(r, route):
        total = part[ROWS[r], :] if route != (1, 0)[r] else jnp.zeros((256, 256), F32)
        for k in range(2):
            for l in range(2):
                base = (k * 2 + l) * 1024
                zs = slice(l * 4, l * 4 + 4)
                if route == 0:
                    a = jnp.concatenate([gz[r, zs, k, xx].reshape(64, ZW) for xx in range(4)], axis=0)
                    total += mm(a, w[base : base + ZW, :])
                elif route == 1:
                    a = jnp.concatenate([gx[r, xx * 2 + k, zs].reshape(64, XW) for xx in range(4)], axis=0)
                    total += mm(a, w[base + XO : base + XO + XW, :])
                else:
                    a = gy[r, k * 4 : k * 4 + 4, zs].reshape(256, YW)
                    total += mm(a, w[base + YO : base + YO + YW, :])
        part[ROWS[r], :] = total

    def swap(r):
        rows = pl.ds(r * 256, 256)
        return rdma(part.at[rows], part_in.at[rows], R["ss4"].at[r], R["rs4"].at[r], partner)

    kv, kvt = R["kv"], R["kvt"]

    def keys_values(r):
        rows = ROWS[r]
        pre = part[rows, :] + part_in[rows, :]
        part_in[rows, :] = pre
        kp = pre[:, :HD]
        inv = lax.rsqrt(jnp.mean(kp * kp, axis=-1, keepdims=True) + EPS)
        keys = (kp * inv).astype(BF16)
        vals = pre[:, HD:].astype(BF16)
        kv[0, rows] = keys
        kv[1, rows] = vals
        kvt[0, :, rows] = keys.astype(F32).T.astype(BF16)
        kvt[1, :, rows] = vals.astype(F32).T.astype(BF16)

    def transpose_weights(lo, hi):
        @pl.loop(lo, hi)
        def _(n):
            rows = pl.ds(pl.multiple_of(n * 256, 256), 256)
            wt[:, rows] = w[rows, :].astype(F32).T.astype(BF16)

    step2x(0)
    step2x(1)
    step2y(0)
    step2y(1)
    zstep(0, 0)
    zstep(1, 0)
    for cp in wcopies:
        cp.wait()
    step3x(0)
    step3y(0)
    step3x(1)
    step3y(1)
    transpose_weights(0, 8)
    zstep(0, 1)
    zstep(1, 1)
    transpose_weights(8, 16)
    limits = lim[...].reshape(1, 512)
    limit = (1 - c) * limits[:, :256] + c * limits[:, 256:]
    for t in range(4):
        bias[t] = jnp.broadcast_to(jnp.where(t < limit, 0.0, -1e30), (16, 256))
    forward3x(0)
    forward3y(0)
    zstep(0, 2)
    zstep(1, 2)
    forward3x(1)
    forward3y(1)
    zstep(0, 3)
    zstep(1, 3)
    rest3x(0)
    project(0, 1)
    rest3y(0)
    project(0, 2)
    z3_last(0)
    project(0, 0)
    swap(0).start()
    z3_last(1)
    project(1, 0)
    swap(0).wait()
    keys_values(0)
    rest3x(1)
    project(1, 1)
    rest3y(1)
    project(1, 2)
    swap(1).start()
    swap(1).wait()
    keys_values(1)

    probs, dsc, at_ = R["probs"], R["dsc"], R["at"]

    @pl.loop(0, 8, unroll=4)
    def _(n):
        lanes = pl.ds(pl.multiple_of(n * 256, 256), 256)
        dotn = dot_[n]
        s = mm(kv[0], qt[n]) * (SCALE * LOG2E)
        s = (s.reshape(8, 4, 16, 256) + bias[...][None]).reshape(512, 256)
        m = jnp.max(s, axis=0, keepdims=True)
        e = jnp.exp2(s - m)
        prob = e * (1.0 / jnp.sum(e, axis=0, keepdims=True))
        pb16 = prob.astype(BF16)
        probs[:, lanes] = pb16
        at = mm(kvt[1], pb16).astype(BF16)
        at_[n] = at
        dp = mm(kv[1], dotn)
        delta = jnp.sum(at.astype(F32) * dotn.astype(F32), axis=0, keepdims=True)
        dsc[:, lanes] = (prob * (dp - delta)).astype(BF16)

    dkv, dkv_in = R["dkv"], R["dkv_in"]

    def key_grads(r):
        rows = ROWS[r]
        kp = part_in[rows, :HD]
        inv = lax.rsqrt(jnp.mean(kp * kp, axis=-1, keepdims=True) + EPS)
        dk = mm(dsc[rows, :], q[...].reshape(2048, HD)) * SCALE
        dv = mm(probs[rows, :], do[...].reshape(2048, HD))
        dkp = inv * dk - kp * (inv * inv * inv * jnp.mean(kp * dk, axis=-1, keepdims=True))
        dkv[rows, :HD] = dkp.astype(BF16)
        dkv[rows, HD:] = dv.astype(BF16)

    def swap2(r):
        rows = pl.ds(r * 256, 256)
        return rdma(dkv.at[rows], dkv_in.at[rows], R["ss4"].at[2 + r], R["rs4"].at[2 + r], partner)

    def heads_out(lo, hi):
        @pl.loop(lo, hi, unroll=2)
        def _(n):
            lanes = pl.ds(pl.multiple_of(n * HD, HD), HD)
            dqt = mm(kvt[0], dsc[:, pl.ds(pl.multiple_of(n * 256, 256), 256)]) * SCALE
            R["dq_v"][:, lanes] = dqt.T.astype(BF16)
            R["att_v"][:, lanes] = at_[n].astype(F32).T.astype(BF16)

    def back(r, route):
        for k in range(2):
            for l in range(2):
                base = (k * 2 + l) * 1024 + (0, XO, YO)[route]
                n = (ZW, XW, YW)[route]
                zs = slice(l * 4, l * 4 + 4)
                wtb = wt[:, base : base + n]
                v = (mm(dkv[ROWS[r], :], wtb) + mm(dkv_in[ROWS[r], :], wtb)).astype(BF16)
                if route == 2:
                    py[r, k * 4 : k * 4 + 4, zs] = v.reshape(4, 4, 16, YW)
                    continue
                for xx in range(4):
                    b = v[xx * 64 : (xx + 1) * 64].reshape(4, 16, n)
                    if route == 0:
                        pz[r, zs, k, xx] = b
                    else:
                        px[r, xx * 2 + k, zs] = b

    rz1 = R["rz1"]

    def rz(r, d, s):
        side = 1 - 2 * d
        at = zind(zo(side * (4 - s)))
        src = pz.at[r, at, d] if s == 0 else pz.at[r, at]
        dst = rz1.at[r, d, 0, d] if s == 0 else rz1.at[r, d, s]
        return rdma(src, dst, R["ssrz1"].at[r], R["rsrz1"].at[r, s * 2 + d if s < 3 else 6], dev(x, y, zo(side), c))

    def rz_arrived(r, d, s):
        arrived(rz1.at[r, d, 0, d] if s == 0 else rz1.at[r, d, s], R["rsrz1"].at[r, s * 2 + d])

    def rzstep(r, s):
        for d in range(2):
            if s > 0:
                rz_arrived(r, d, s - 1)
                at = zind(zo((1 - 2 * d) * (4 - s)))
                if s == 1:
                    pz[r, at, d] = (pz[r, at, d].astype(F32) + rz1[r, d, 0, d].astype(F32)).astype(BF16)
                else:
                    pz[r, at] = (pz[r, at].astype(F32) + rz1[r, d, s - 1].astype(F32)).astype(BF16)
            rz(r, d, s).start()

    def rzy_to(r, k):
        return rdma(
            pz.at[r, zi, k], R["rzy"].at[r, y], R["ssrz2"].at[r], R["rsrz2"].at[r], dev(x, 2 * c + k, z, c)
        )

    def rz_sum(r):
        arrived(rz1.at[r, 0, pl.ds(2, 2)], R["rsrz1"].at[r, 6])
        pz[r, zi] = (pz[r, zi].astype(F32) + rz1[r, 0, 3].astype(F32) + rz1[r, 1, 3].astype(F32)).astype(BF16)
        for k in range(2):
            @pl.when(role != k)
            def _():
                rzy_to(r, k).start()

    def rzx_to(r, d):
        return rdma(
            R["tz"].at[r, xo(d)], R["rzx"].at[x], R["ssrz3"].at[r], R["rsrz3"].at[0], dev(xo(d), y, z, r)
        )

    def rzx_all(r, act):
        for d in (2, 1, 3):
            act(rzx_to(r, d))

        @pl.when(c != r)
        def _():
            act(rzx_to(r, 0))

    def rz_rows(r):
        @pl.when(home)
        def _():
            arrived(R["rzy"].at[r, pl.ds(0, 3)], R["rsrz2"].at[r])
            v = pz[r, zi, yp].astype(F32)
            for d in range(1, 4):
                v += R["rzy"][r, yo(d)].astype(F32)
            R["tz"][r] = v.astype(BF16)
            rzx_all(r, begin)

            @pl.when(c == r)
            def _():
                pltpu.make_async_copy(R["tz"].at[r, x], R["rzx"].at[x], R["rsrz3"].at[0]).start()

    def r1x_opp(r, d):
        return rdma(
            px.at[r, xo(2) * 2 + d], R["r1o"].at[r, d], R["ssr1"].at[r, 0], R["rsr1x"].at[r, d],
            dev(xo(1 - 2 * d), y, z, c),
        )

    def r1x_free(r, d):
        return rdma(
            px.at[r, xo(1 - 2 * d) * 2 + 1 - d], R["r1n"].at[r, d, 1 - d], R["ssr1"].at[r, 0],
            R["rsr1x"].at[r, 2], dev(xo(1 - 2 * d), y, z, c),
        )

    def r1x_dep(r, d):
        return rdma(
            px.at[r, xo(1 - 2 * d) * 2 + d], R["r1n"].at[r, d, d], R["ssr1"].at[r, 0],
            R["rsr1x"].at[r, 2], dev(xo(1 - 2 * d), y, z, c),
        )

    y_opp = {2: ((1, 0, 0), (0, 0, 1)), 3: ((0, 1, 0), (1, 1, 1))}
    y_free = {0: (0, 1, 1), 1: (1, 0, 1), 2: (1, 1, 0), 3: (0, 0, 0)}
    y_dep = {0: (0, 1, 0), 1: (1, 0, 0), 2: (1, 1, 1), 3: (0, 0, 1)}

    def r1y_opp(r, o, i):
        d, k, j = y_opp[o][i]
        return rdma(
            py.at[r, half_y(k, j)], R["r1yo"].at[r], R["ssr1"].at[r, 1], R["rsr1y"].at[r, 0],
            dev(x, yo(1 - 2 * d), z, c),
        )

    def r1y_next(r, o, dep):
        d, k, j = (y_dep if dep else y_free)[o]
        side = 0 if o >= 2 else 1
        return rdma(
            py.at[r, half_y(k, j)], R["r1yn"].at[r, side, pl.ds(j * 2, 2)], R["ssr1"].at[r, 1],
            R["rsr1y"].at[r, 1], dev(x, yo(1 - 2 * d), z, c),
        )

    def opp_x(r):
        for d in range(2):
            r1x_opp(r, d).start()

    def free_x(r):
        for d in range(2):
            r1x_free(r, d).start()

    def opp_y(r):
        for o in (2, 3):
            @pl.when(role == o)
            def _():
                for i in range(2):
                    r1y_opp(r, o, i).start()

    def free_y(r):
        for o in range(4):
            @pl.when(role == o)
            def _():
                r1y_next(r, o, 0).start()

    r1o, r1yo, r1n, r1yn = (R[n] for n in ("r1o", "r1yo", "r1n", "r1yn"))

    def dep_x(r):
        for d in range(2):
            arrived(r1o.at[r, d], R["rsr1x"].at[r, d])
            to = xo(1 - 2 * d) * 2 + d

            @pl.loop(0, 8, unroll=2)
            def _(i):
                px[r, to, i] = (px[r, to, i].astype(F32) + r1o[r, d, i].astype(F32)).astype(BF16)

            r1x_dep(r, d).start()
    def dep_y(r):
        arrived(r1yo.at[r], R["rsr1y"].at[r, 0])
        for o in range(4):
            @pl.when(role == o)
            def _():
                _d, k, j = y_dep[o]

                @pl.loop(0, 8)
                def _(i):
                    for xx in range(2):
                        at = k * 4 + j * 2 + xx
                        py[r, at, i] = (py[r, at, i].astype(F32) + r1yo[r, xx, i].astype(F32)).astype(BF16)

                r1y_next(r, o, 1).start()

    sx, sy, r2x, r2y, tx, ty = (R[n] for n in ("sx", "sy", "r2x", "r2y", "tx", "ty"))

    def r2x_to(r, k):
        return rdma(
            sx.at[r, k], r2x.at[r, y], R["ssr2"].at[r, 0], R["rsr2x"].at[r], dev(x, 2 * c + k, z, c)
        )

    def r2y_to(r, d):
        return rdma(
            sy.at[r, xo(d)], r2y.at[r, x], R["ssr2"].at[r, 1], R["rsr2y"].at[r], dev(xo(d), y, z, c)
        )

    def rs2x(r):
        arrived(r1n.at[r], R["rsr1x"].at[r, 2])

        @pl.loop(0, 8)
        def _(b):
            for k in range(2):
                sx[r, k, b] = (
                    px[r, x * 2 + k, b].astype(F32) + r1n[r, 0, k, b].astype(F32) + r1n[r, 1, k, b].astype(F32)
                ).astype(BF16)

        for k in range(2):
            @pl.when(role != k)
            def _():
                r2x_to(r, k).start()

    def rs2y(r):
        @pl.when(home)
        def _():
            arrived(r1yn.at[r], R["rsr1y"].at[r, 1])

            @pl.loop(0, 8)
            def _(b):
                for k in range(4):
                    sy[r, k, b] = (
                        py[r, yp * 4 + k, b].astype(F32) + r1yn[r, 0, k, b].astype(F32) + r1yn[r, 1, k, b].astype(F32)
                    ).astype(BF16)

            for d in (2, 1, 3):
                r2y_to(r, d).start()

    def r3_to(r, route, d):
        t, dst = ((tx, R["r3x"]), (ty, R["r3y"]))[route]
        zz = zo(d)
        return rdma(
            t.at[r, zind(zz)], dst.at[zi], R["ssr3"].at[r, route], R["rsr3"].at[route], dev(x, y, zz, r)
        )

    def r3_all(r, route, act):
        for d in (4, 3, 5, 2, 6, 1, 7):
            act(r3_to(r, route, d))

        @pl.when(c != r)
        def _():
            act(r3_to(r, route, 0))

    def r3_own(r, route):
        t, dst = ((tx, R["r3x"]), (ty, R["r3y"]))[route]

        @pl.when(c == r)
        def _():
            pltpu.make_async_copy(t.at[r, zi], dst.at[zi], R["rsr3"].at[route]).start()

    def rs3x(r):
        @pl.when(home)
        def _():
            arrived(r2x.at[r, pl.ds(0, 3)], R["rsr2x"].at[r])

            @pl.loop(0, 8, unroll=2)
            def _(b):
                v = sx[r, yp, b].astype(F32)
                for d in range(1, 4):
                    v += r2x[r, yo(d), b].astype(F32)
                tx[r, b] = v.astype(BF16)

            r3_all(r, 0, begin)
            r3_own(r, 0)

    def rs3y(r):
        @pl.when(home)
        def _():
            arrived(r2y.at[r, pl.ds(0, 3)], R["rsr2y"].at[r])

            @pl.loop(0, 8, unroll=2)
            def _(b):
                v = sy[r, x, b].astype(F32)
                for d in range(1, 4):
                    v += r2y[r, xo(d), b].astype(F32)
                ty[r, b] = v.astype(BF16)

            r3_all(r, 1, begin)
            r3_own(r, 1)

    def finish(route):
        src, n, o = ((R["r3x"], XW, XO), (R["r3y"], YW, YO))[route]
        arrived(src, R["rsr3"].at[route])
        total = src[0].astype(F32)
        for b in range(1, 8):
            total += src[b].astype(F32)
        R["gv_v"][:, o : o + n] = total

    def finish_z():
        arrived(R["rzx"], R["rsrz3"].at[0])
        total = R["rzx"][0].astype(F32)
        for b in range(1, 4):
            total += R["rzx"][b].astype(F32)
        R["gv_v"][:, :ZW] = total

    outs = [
        pltpu.make_async_copy(R["att_v"], att_o.at[0], R["osem"].at[0]),
        pltpu.make_async_copy(R["dq_v"], dq_o.at[0], R["osem"].at[1]),
        pltpu.make_async_copy(R["gv_v"], gv_o, R["osem"].at[2]),
    ]

    key_grads(0)
    swap2(0).start()
    key_grads(1)
    swap2(1).start()
    swap2(0).wait()
    back(0, 0)
    for d in range(2):
        rz(0, d, 0).start()
    back(0, 1)
    opp_x(0)
    free_x(0)
    back(0, 2)
    opp_y(0)
    free_y(0)
    swap2(1).wait()
    back(1, 0)
    for d in range(2):
        rz(1, d, 0).start()
    back(1, 1)
    opp_x(1)
    free_x(1)
    back(1, 2)
    opp_y(1)
    free_y(1)
    heads_out(0, 4)
    dep_x(0)
    dep_y(0)
    rzstep(0, 1)
    rzstep(1, 1)
    heads_out(4, 8)
    for cp in outs[:2]:
        cp.start()
    dep_x(1)
    dep_y(1)
    rzstep(0, 2)
    rzstep(1, 2)
    rs2x(0)
    rs2y(0)
    rzstep(0, 3)
    rzstep(1, 3)
    rs2x(1)
    rs2y(1)
    rs3x(0)
    rs3y(0)
    rz_sum(0)
    rz_sum(1)
    rz_rows(0)
    rz_rows(1)
    rs3x(1)
    rs3y(1)
    finish_z()
    finish(0)
    finish(1)
    outs[2].start()

    by_home(
        lambda: sent(gz.at[0, 0, 0, pl.ds(0, 3)], R["ssz1"].at[0]),
        lambda: sent(gz.at[0, 0, 0], R["ssz1"].at[0]),
    )
    for i, ref in enumerate((gx, gy)):
        by_home(
            lambda: sent(ref.at[0, 0, pl.ds(0, 7)], R["ss1"].at[i]),
            lambda: sent(ref.at[0, 0], R["ss1"].at[i]),
        )
    for r in range(2):
        sent(gz.at[r, pl.ds(0, 7)], R["ssz3"].at[r])
        sent(pz.at[r, pl.ds(0, 7)], R["ssrz1"].at[r])
        sent(gx.at[r, pl.ds(0, 6)], R["ss3"].at[r, 0])
        sent(px.at[r, pl.ds(0, 6)], R["ssr1"].at[r, 0])

        @pl.when(home)
        def _():
            sent(R["rzy"].at[r, pl.ds(0, 3)], R["ssz2"].at[r])
            sent(gx.at[r, pl.ds(0, 3)], R["ss2"].at[r, 0])
            sent(gy.at[r, pl.ds(0, 3)], R["ss2"].at[r, 1])
            sent(sy.at[r, pl.ds(0, 3)], R["ssr2"].at[r, 1])
            sent(gy.at[:, pl.ds(0, 5)], R["ss3"].at[r, 1])

            @pl.when(c == r)
            def _():
                sent(tx.at[r, pl.ds(0, 7)], R["ssr3"].at[r, 0])
                sent(ty.at[r, pl.ds(0, 7)], R["ssr3"].at[r, 1])
                sent(R["tz"].at[r, pl.ds(0, 3)], R["ssrz3"].at[r])

            @pl.when(c != r)
            def _():
                sent(tx.at[r], R["ssr3"].at[r, 0])
                sent(ty.at[r], R["ssr3"].at[r, 1])
                sent(R["tz"].at[r], R["ssrz3"].at[r])

        by_home(
            lambda: sent(py.at[r, pl.ds(0, 4)], R["ssr1"].at[r, 1]),
            lambda: sent(py.at[r], R["ssr1"].at[r, 1]),
        )
        by_home(
            lambda: sent(sx.at[r, 0], R["ssr2"].at[r, 0]),
            lambda: sent(sx.at[r], R["ssr2"].at[r, 0]),
        )
        by_home(
            lambda: sent(pz.at[r, 0, 0], R["ssrz2"].at[r]),
            lambda: sent(pz.at[r, 0], R["ssrz2"].at[r]),
        )

        @pl.when(c == 1 - h)
        def _():
            sent(gy.at[r, pl.ds(0, 2)], R["ss3"].at[r, 1])

    for cp in outs:
        cp.wait()


def copy_out(a, b, d, ao, bo, do, av, bv, dv, sems):
    moves = ((a, av, ao), (b, bv, bo), (d, dv, do))
    loads = [pltpu.make_async_copy(s, v, sems.at[0, i]) for i, (s, v, _) in enumerate(moves)]
    stores = [pltpu.make_async_copy(v, t, sems.at[1, i]) for i, (_, v, t) in enumerate(moves)]
    for cp in loads:
        cp.start()
    for load, store in zip(loads, stores):
        load.wait()
        store.start()
    for cp in stores:
        cp.wait()


def on_device(queries, grad_attended, vision, key_weight, value_weight, tile_limit):
    vmem = pl.BlockSpec(memory_space=pltpu.VMEM)
    hbm = pl.BlockSpec(memory_space=pl.ANY)
    shapes = (
        jax.ShapeDtypeStruct(queries.shape, BF16),
        jax.ShapeDtypeStruct(queries.shape, BF16),
        jax.ShapeDtypeStruct(vision.shape, F32),
    )
    outs = pl.pallas_call(
        kernel,
        out_shape=shapes,
        in_specs=[hbm, hbm, hbm, hbm, hbm, vmem],
        out_specs=(hbm, hbm, hbm),
        scratch_shapes=list(scratch().values()),
        compiler_params=pltpu.CompilerParams(
            collective_id=0, has_side_effects=True, vmem_limit_bytes=60 * 2**20
        ),
        cost_estimate=pl.CostEstimate(flops=6_000_000_000, bytes_accessed=6_000_000, transcendentals=1_000_000),
    )(vision, key_weight, value_weight, queries, grad_attended, tile_limit)
    return pl.pallas_call(
        copy_out,
        out_shape=shapes,
        in_specs=[hbm, hbm, hbm],
        out_specs=(hbm, hbm, hbm),
        scratch_shapes=[pltpu.VMEM(s.shape, s.dtype) for s in shapes] + [pltpu.SemaphoreType.DMA((2, 3))],
    )(*outs)


def solution(mesh):
    return jax.shard_map(
        on_device,
        mesh=mesh,
        in_specs=(
            P("segment", None, "tensor"),
            P("segment", None, "tensor"),
            P("segment", "tensor"),
            P("segment", None, "tensor"),
            P("segment", None, "tensor"),
            P(),
        ),
        out_specs=(
            P("segment", None, "tensor"),
            P("segment", None, "tensor"),
            P("segment", "tensor"),
        ),
        check_vma=False,
    )
```

```python
import jax
import jax.numpy as jnp
from jax import lax
from jax.experimental import pallas as pl
from jax.experimental.pallas import tpu as pltpu
from jax.sharding import PartitionSpec as P

HD = 128
EPS = 1e-05
SCALE = HD ** (-0.5)
LOG2E = 1.4426950408889634
F32 = jnp.float32
BF16 = jnp.bfloat16
MESH = pl.DeviceIdType.MESH

ZW, XW, YW = 256, 384, 384
XO, YO = ZW, ZW + XW


def scratch():
    v, dma = pltpu.VMEM, pltpu.SemaphoreType.DMA
    s = {
        "vis": v((16, 1024), BF16),
        "q": v((8, 256, 128), BF16), "do": v((8, 256, 128), BF16),
        "w": v((4096, 256), BF16), "wt": v((256, 4096), BF16),
        "qt": v((8, 128, 256), BF16), "dot": v((8, 128, 256), BF16),
        "bias": v((4, 16, 256), F32),
        "part": v((512, 256), F32), "part_in": v((512, 256), F32),
        "kv": v((2, 512, 128), BF16), "kvt": v((2, 128, 512), BF16),
        "probs": v((512, 2048), BF16), "dsc": v((512, 2048), BF16), "at": v((8, 128, 256), BF16),
        "dkv": v((512, 256), BF16), "dkv_in": v((512, 256), BF16),
        "att_v": v((256, 1024), BF16), "dq_v": v((256, 1024), BF16), "gv_v": v((16, 1024), F32),
        "gz": v((2, 8, 2, 4, 16, ZW), BF16), "pz": v((2, 8, 2, 4, 16, ZW), BF16),
        "rz1": v((2, 2, 4, 2, 4, 16, ZW), BF16), "rzy": v((2, 4, 4, 16, ZW), BF16),
        "tz": v((2, 4, 16, ZW), BF16), "rzx": v((4, 16, ZW), BF16),
        "gx": v((2, 8, 8, 16, XW), BF16), "gy": v((2, 8, 8, 16, YW), BF16),
        "px": v((2, 8, 8, 16, XW), BF16), "py": v((2, 8, 8, 16, YW), BF16),
        "r1o": v((2, 2, 8, 16, XW), BF16), "r1n": v((2, 2, 2, 8, 16, XW), BF16),
        "r1yo": v((2, 2, 8, 16, YW), BF16), "r1yn": v((2, 2, 4, 8, 16, YW), BF16),
        "sx": v((2, 2, 8, 16, XW), BF16), "sy": v((2, 4, 8, 16, YW), BF16),
        "r2x": v((2, 4, 8, 16, XW), BF16), "r2y": v((2, 4, 8, 16, YW), BF16),
        "tx": v((2, 8, 16, XW), BF16), "ty": v((2, 8, 16, YW), BF16),
        "r3x": v((8, 16, XW), BF16), "r3y": v((8, 16, YW), BF16),
        "lsem": dma((5,)), "osem": dma((3,)), "ss4": dma((4,)), "rs4": dma((4,)),
        "ssz1": dma((1,)), "ss1": dma((2,)), "ssz2": dma((2,)), "ss2": dma((2, 2)), "ss3": dma((2, 2)),
        "ssz3": dma((2,)), "ssrz1": dma((2,)), "ssr1": dma((2, 2)), "ssr2": dma((2, 2)), "ssr3": dma((2, 2)),
        "ssrz2": dma((2,)), "ssrz3": dma((2,)),
        "rsz1": dma((2,)), "rs1": dma((2, 2)), "rsz2": dma((2,)), "rs2x": dma((2,)), "rs2y": dma((2,)),
        "rs3x": dma((2, 3)), "rs3y": dma((2, 2)), "rsz3": dma((2, 7)),
        "rsrz1": dma((2, 7)), "rsr1x": dma((2, 3)), "rsr1y": dma((2, 2)), "rsr2x": dma((2,)), "rsr2y": dma((2,)),
        "rsr3": dma((2,)), "rsrz2": dma((2,)), "rsrz3": dma((1,)),
    }
    return s


NAMES = tuple(scratch())


def mm(a, b):
    return jnp.dot(a, b, preferred_element_type=F32)


def kernel(vis_in, wk, wv, q_in, do_in, lim, att_o, dq_o, gv_o, *rest):
    R = dict(zip(NAMES, rest, strict=True))
    vis, q, do, w, wt = R["vis"], R["q"], R["do"], R["w"], R["wt"]
    gx, gy, gz, px, py, pz = (R[n] for n in ("gx", "gy", "gz", "px", "py", "pz"))

    seg, ten = lax.axis_index("segment"), lax.axis_index("tensor")
    zh, x, c = lax.div(seg, 8), lax.rem(lax.div(seg, 2), 4), lax.rem(seg, 2)
    y, zl = lax.div(ten, 2), lax.rem(ten, 2)
    z = zh * 2 + zl
    zi = zl * 4 + zh
    h, yp = lax.div(y, 2), lax.rem(y, 2)
    role = lax.rem(y + 4 - 2 * c, 4)
    home = c == h

    def dev(xx, yy, zz, cc):
        return (lax.div(zz, 2) * 8 + xx * 2 + cc, yy * 2 + lax.rem(zz, 2))

    def zind(zz):
        return lax.rem(zz, 2) * 4 + lax.div(zz, 2)

    def xo(d):
        return lax.rem(x + d + 4, 4)

    def yo(d):
        return lax.rem(y + d + 4, 4)

    def zo(d):
        return lax.rem(z + d + 8, 8)

    partner = dev(x, y, z, 1 - c)

    def rdma(src, dst, ss, rs, to):
        return pltpu.make_async_remote_copy(
            src_ref=src, dst_ref=dst, send_sem=ss, recv_sem=rs, device_id=to, device_id_type=MESH
        )

    def arrived(dst, rs):
        rdma(dst, dst, R["ss4"].at[0], rs, partner).wait_recv()

    def begin(cp):
        cp.start()

    def sent(ref, ss):
        rdma(ref, ref, ss, R["rs4"].at[0], partner).wait_send()

    lsem = R["lsem"]
    wcopies = [
        pltpu.make_async_copy(wk.at[0], w.at[:, pl.ds(0, HD)], lsem.at[0]),
        pltpu.make_async_copy(wv.at[0], w.at[:, pl.ds(HD, HD)], lsem.at[1]),
    ]

    barrier = pltpu.get_barrier_semaphore()
    greet = [dev(x, y, zo(d), cc) for d in range(1, 8) for cc in (0, 1)]
    greet += [dev(xo(d), y, z, cc) for d in range(1, 4) for cc in (0, 1)]
    greet += [dev(x, yo(d), z, c) for d in range(1, 4)] + [partner]
    shard = pltpu.make_async_copy(vis_in, vis, lsem.at[4])
    shard.start()
    for other in greet:
        pl.semaphore_signal(barrier, inc=1, device_id=other, device_id_type=MESH)
    for cp in wcopies:
        cp.start()
    loads = [
        pltpu.make_async_copy(q_in.at[0], R["att_v"], lsem.at[2]),
        pltpu.make_async_copy(do_in.at[0], R["dq_v"], lsem.at[3]),
    ]
    for cp in loads:
        cp.start()
    shard.wait()
    pl.semaphore_wait(barrier, len(greet))

    def z1(d):
        return rdma(vis.at[:, pl.ds(0, ZW)], gz.at[c, zi, yp, x], R["ssz1"].at[0], R["rsz1"].at[c], dev(xo(d), y, z, h))

    def z1_all(act):
        for d in (2, 1, 3):
            act(z1(d))

        @pl.when(c == 1 - h)
        def _():
            act(z1(0))

    def g1(route, d):
        src, dst = (
            (vis.at[:, pl.ds(XO, XW)], gx.at[c, x * 2 + yp, zi]),
            (vis.at[:, pl.ds(YO, YW)], gy.at[c, yp * 4 + x, zi]),
        )[route]
        return rdma(src, dst, R["ss1"].at[route], R["rs1"].at[c, route], dev(x, y, zo(d), h))

    def g1_all(route, act):
        for d in (4, 3, 5, 2, 6, 1, 7):
            act(g1(route, d))

        @pl.when(c == 1 - h)
        def _():
            act(g1(route, 0))

    z1_all(begin)
    for route in range(2):
        g1_all(route, begin)

    @pl.when(home)
    def _():
        pltpu.make_async_copy(vis.at[:, pl.ds(0, ZW)], gz.at[c, zi, yp, x], R["rsz1"].at[c]).start()
        pltpu.make_async_copy(vis.at[:, pl.ds(XO, XW)], gx.at[c, x * 2 + yp, zi], R["rs1"].at[c, 0]).start()
        pltpu.make_async_copy(vis.at[:, pl.ds(YO, YW)], gy.at[c, yp * 4 + x, zi], R["rs1"].at[c, 1]).start()

    for cp in loads:
        cp.wait()
    qt, dot_, bias = R["qt"], R["dot"], R["bias"]

    @pl.loop(0, 8)
    def _(n):
        lanes = pl.ds(pl.multiple_of(n * HD, HD), HD)
        qn = R["att_v"][:, lanes]
        dn = R["dq_v"][:, lanes]
        q[n] = qn
        do[n] = dn
        qt[n] = qn.astype(F32).T.astype(BF16)
        dot_[n] = dn.astype(F32).T.astype(BF16)

    def z2(r, d):
        blk = gz.at[r, zi, yp]
        return rdma(blk, blk, R["ssz2"].at[r], R["rsz2"].at[r], dev(x, yo(d), z, c))

    @pl.when(home)
    def _():
        for r in range(2):
            arrived(gz.at[r, zi, yp], R["rsz1"].at[r])
            for d in (2, 1, 3):
                z2(r, d).start()

    def g2x(r, d):
        blk = gx.at[r, x * 2 + yp]
        return rdma(blk, blk, R["ss2"].at[r, 0], R["rs2x"].at[r], dev(x, yo(d), z, c))

    def g2y(r, d):
        blk = gy.at[r, yp * 4 + x]
        return rdma(blk, blk, R["ss2"].at[r, 1], R["rs2y"].at[r], dev(xo(d), y, z, c))

    def step2x(r):
        @pl.when(home)
        def _():
            arrived(gx.at[r, x * 2 + yp], R["rs1"].at[r, 0])
            for d in (2, 1, 3):
                g2x(r, d).start()

    def step2y(r):
        @pl.when(home)
        def _():
            arrived(gy.at[r, yp * 4 + x], R["rs1"].at[r, 1])
            for d in (2, 1, 3):
                g2y(r, d).start()

    def by_home(few, many):
        @pl.when(home)
        def _():
            few()

        @pl.when(c == 1 - h)
        def _():
            many()

    def z3(r, d, s):
        side = 1 - 2 * d
        at = zind(zo(-side * s))
        blk = gz.at[r, at] if s < 3 else gz.at[r, at, d]
        return rdma(blk, blk, R["ssz3"].at[r], R["rsz3"].at[r, s * 2 + d if s < 3 else 6], dev(x, y, zo(side), c))

    def z3_arrived(r, d, s):
        arrived(gz.at[r, zind(zo(-(1 - 2 * d) * (s + 1)))], R["rsz3"].at[r, s * 2 + d])

    def z3_last(r):
        arrived(gz.at[r, zind(zo(4))], R["rsz3"].at[r, 6])

    def zstep(r, s):
        if s == 0:
            by_home(
                lambda: arrived(gz.at[r, zi, 1 - yp], R["rsz2"].at[r]),
                lambda: arrived(gz.at[r, zi], R["rsz2"].at[r]),
            )
        for d in range(2):
            if s > 0:
                z3_arrived(r, d, s - 1)
            z3(r, d, s).start()

    def g3x(r, d, half):
        blk = gx.at[r, x * 2 + half]
        return rdma(blk, blk, R["ss3"].at[r, 0], R["rs3x"].at[r, d if half == d else 2], dev(xo(1 - 2 * d), y, z, c))

    def g3xf(r, d):
        blk = gx.at[r, xo(2 * d - 1) * 2 + d]
        return rdma(blk, blk, R["ss3"].at[r, 0], R["rs3x"].at[r, 2], dev(xo(1 - 2 * d), y, z, c))

    def half_y(k, j):
        return pl.ds(k * 4 + j * 2, 2)

    passed = ((1, 0, 1), (0, 0, 0), (1, 1, 0), (0, 1, 1))

    def g3y(r, o, k, j, d):
        blk = gy.at[r, half_y(k, j)]
        first = passed[(o + 1 - 2 * d) % 4][:2] == (k, j)
        return rdma(blk, blk, R["ss3"].at[r, 1], R["rs3y"].at[r, 0 if first else 1], dev(x, yo(1 - 2 * d), z, c))

    def g3y_role(r, o):
        order = ((0, 0, 0), (0, 1, 1), (0, 1, 0), (0, 0, 1)) if o == 0 else ((1, 0, 1), (1, 1, 0), (1, 1, 1), (1, 0, 0))
        return [g3y(r, o, k, j, d) for k, j, d in order]

    def g3yf(r, o):
        k, j, d = passed[o]
        return g3y(r, o, k, j, d)

    def step3x(r):
        by_home(
            lambda: arrived(gx.at[r, x * 2 + 1 - yp], R["rs2x"].at[r]),
            lambda: arrived(gx.at[r, pl.ds(x * 2, 2)], R["rs2x"].at[r]),
        )
        for d, half in ((0, 0), (1, 1), (0, 1), (1, 0)):
            g3x(r, d, half).start()

    def step3y(r):
        for o in (0, 1):
            @pl.when(role == o)
            def _():
                arrived(gy.at[r, pl.ds(o * 4, 3)], R["rs2y"].at[r])
                for cp in g3y_role(r, o):
                    cp.start()

    def forward3x(r):
        for d in range(2):
            arrived(gx.at[r, xo(2 * d - 1) * 2 + d], R["rs3x"].at[r, d])
            g3xf(r, d).start()

    def forward3y(r):
        for o in range(4):
            @pl.when(role == o)
            def _():
                arrived(gy.at[r, half_y(*passed[o][:2])], R["rs3y"].at[r, 0])
                g3yf(r, o).start()

    def rest3x(r):
        arrived(gx.at[r, pl.ds(0, 4)], R["rs3x"].at[r, 2])

    def rest3y(r):
        by_home(
            lambda: arrived(gy.at[r, pl.ds(0, 2)], R["rs3y"].at[r, 1]),
            lambda: arrived(gy.at[r, pl.ds(0, 6)], R["rs3y"].at[r, 1]),
        )

    part, part_in = R["part"], R["part_in"]
    ROWS = (slice(0, 256), slice(256, 512))

    def project(r, route):
        total = part[ROWS[r], :] if route != (1, 0)[r] else jnp.zeros((256, 256), F32)
        for k in range(2):
            for l in range(2):
                base = (k * 2 + l) * 1024
                zs = slice(l * 4, l * 4 + 4)
                if route == 0:
                    a = jnp.concatenate([gz[r, zs, k, xx].reshape(64, ZW) for xx in range(4)], axis=0)
                    total += mm(a, w[base : base + ZW, :])
                elif route == 1:
                    a = jnp.concatenate([gx[r, xx * 2 + k, zs].reshape(64, XW) for xx in range(4)], axis=0)
                    total += mm(a, w[base + XO : base + XO + XW, :])
                else:
                    a = gy[r, k * 4 : k * 4 + 4, zs].reshape(256, YW)
                    total += mm(a, w[base + YO : base + YO + YW, :])
        part[ROWS[r], :] = total

    def swap(r):
        rows = pl.ds(r * 256, 256)
        return rdma(part.at[rows], part_in.at[rows], R["ss4"].at[r], R["rs4"].at[r], partner)

    kv, kvt = R["kv"], R["kvt"]

    def keys_values(r):
        rows = ROWS[r]
        pre = part[rows, :] + part_in[rows, :]
        part_in[rows, :] = pre
        kp = pre[:, :HD]
        inv = lax.rsqrt(jnp.mean(kp * kp, axis=-1, keepdims=True) + EPS)
        keys = (kp * inv).astype(BF16)
        vals = pre[:, HD:].astype(BF16)
        kv[0, rows] = keys
        kv[1, rows] = vals
        kvt[0, :, rows] = keys.astype(F32).T.astype(BF16)
        kvt[1, :, rows] = vals.astype(F32).T.astype(BF16)

    def transpose_weights(lo, hi):
        @pl.loop(lo, hi)
        def _(n):
            rows = pl.ds(pl.multiple_of(n * 256, 256), 256)
            wt[:, rows] = w[rows, :].astype(F32).T.astype(BF16)

    step2x(0)
    step2x(1)
    step2y(0)
    step2y(1)
    zstep(0, 0)
    zstep(1, 0)
    for cp in wcopies:
        cp.wait()
    step3x(0)
    step3y(0)
    step3x(1)
    step3y(1)
    transpose_weights(0, 8)
    zstep(0, 1)
    zstep(1, 1)
    transpose_weights(8, 16)
    limits = lim[...].reshape(1, 512)
    limit = (1 - c) * limits[:, :256] + c * limits[:, 256:]
    for t in range(4):
        bias[t] = jnp.broadcast_to(jnp.where(t < limit, 0.0, -1e30), (16, 256))
    forward3x(0)
    forward3y(0)
    zstep(0, 2)
    zstep(1, 2)
    forward3x(1)
    forward3y(1)
    zstep(0, 3)
    zstep(1, 3)
    rest3x(0)
    project(0, 1)
    rest3y(0)
    project(0, 2)
    z3_last(0)
    project(0, 0)
    swap(0).start()
    z3_last(1)
    project(1, 0)
    swap(0).wait()
    keys_values(0)
    rest3x(1)
    project(1, 1)
    rest3y(1)
    project(1, 2)
    swap(1).start()
    swap(1).wait()
    keys_values(1)

    probs, dsc, at_ = R["probs"], R["dsc"], R["at"]

    @pl.loop(0, 8, unroll=8)
    def _(n):
        lanes = pl.ds(pl.multiple_of(n * 256, 256), 256)
        dotn = dot_[n]
        s = mm(kv[0], qt[n]) * (SCALE * LOG2E)
        s = (s.reshape(8, 4, 16, 256) + bias[...][None]).reshape(512, 256)
        m = jnp.max(s, axis=0, keepdims=True)
        e = jnp.exp2(s - m)
        prob = e * (1.0 / jnp.sum(e, axis=0, keepdims=True))
        pb16 = prob.astype(BF16)
        probs[:, lanes] = pb16
        at = mm(kvt[1], pb16).astype(BF16)
        at_[n] = at
        dp = mm(kv[1], dotn)
        delta = jnp.sum(at.astype(F32) * dotn.astype(F32), axis=0, keepdims=True)
        dsc[:, lanes] = (prob * (dp - delta)).astype(BF16)

    dkv, dkv_in = R["dkv"], R["dkv_in"]

    def key_grads(r):
        rows = ROWS[r]
        kp = part_in[rows, :HD]
        inv = lax.rsqrt(jnp.mean(kp * kp, axis=-1, keepdims=True) + EPS)
        dk = mm(dsc[rows, :], q[...].reshape(2048, HD)) * SCALE
        dv = mm(probs[rows, :], do[...].reshape(2048, HD))
        dkp = inv * dk - kp * (inv * inv * inv * jnp.mean(kp * dk, axis=-1, keepdims=True))
        dkv[rows, :HD] = dkp.astype(BF16)
        dkv[rows, HD:] = dv.astype(BF16)

    def swap2(r):
        rows = pl.ds(r * 256, 256)
        return rdma(dkv.at[rows], dkv_in.at[rows], R["ss4"].at[2 + r], R["rs4"].at[2 + r], partner)

    def heads_out(lo, hi):
        @pl.loop(lo, hi, unroll=2)
        def _(n):
            lanes = pl.ds(pl.multiple_of(n * HD, HD), HD)
            dqt = mm(kvt[0], dsc[:, pl.ds(pl.multiple_of(n * 256, 256), 256)]) * SCALE
            R["dq_v"][:, lanes] = dqt.T.astype(BF16)
            R["att_v"][:, lanes] = at_[n].astype(F32).T.astype(BF16)

    def both(r):
        swap2(r).wait()
        rows = ROWS[r]
        dkv[rows, :] = (dkv[rows, :].astype(F32) + dkv_in[rows, :].astype(F32)).astype(BF16)

    def back(r, route):
        for k in range(2):
            for l in range(2):
                base = (k * 2 + l) * 1024 + (0, XO, YO)[route]
                n = (ZW, XW, YW)[route]
                zs = slice(l * 4, l * 4 + 4)
                wtb = wt[:, base : base + n]
                v = mm(dkv[ROWS[r], :], wtb).astype(BF16)
                if route == 2:
                    py[r, k * 4 : k * 4 + 4, zs] = v.reshape(4, 4, 16, YW)
                    continue
                for xx in range(4):
                    b = v[xx * 64 : (xx + 1) * 64].reshape(4, 16, n)
                    if route == 0:
                        pz[r, zs, k, xx] = b
                    else:
                        px[r, xx * 2 + k, zs] = b

    rz1 = R["rz1"]

    def rz(r, d, s):
        side = 1 - 2 * d
        at = zind(zo(side * (4 - s)))
        src = pz.at[r, at, d] if s == 0 else pz.at[r, at]
        dst = rz1.at[r, d, 0, d] if s == 0 else rz1.at[r, d, s]
        return rdma(src, dst, R["ssrz1"].at[r], R["rsrz1"].at[r, s * 2 + d if s < 3 else 6], dev(x, y, zo(side), c))

    def rz_arrived(r, d, s):
        arrived(rz1.at[r, d, 0, d] if s == 0 else rz1.at[r, d, s], R["rsrz1"].at[r, s * 2 + d])

    def rzstep(r, s):
        for d in range(2):
            if s > 0:
                rz_arrived(r, d, s - 1)
                at = zind(zo((1 - 2 * d) * (4 - s)))
                if s == 1:
                    pz[r, at, d] = (pz[r, at, d].astype(F32) + rz1[r, d, 0, d].astype(F32)).astype(BF16)
                else:
                    pz[r, at] = (pz[r, at].astype(F32) + rz1[r, d, s - 1].astype(F32)).astype(BF16)
            rz(r, d, s).start()

    def rzy_to(r, k):
        return rdma(
            pz.at[r, zi, k], R["rzy"].at[r, y], R["ssrz2"].at[r], R["rsrz2"].at[r], dev(x, 2 * c + k, z, c)
        )

    def rz_sum(r):
        arrived(rz1.at[r, 0, pl.ds(2, 2)], R["rsrz1"].at[r, 6])
        pz[r, zi] = (pz[r, zi].astype(F32) + rz1[r, 0, 3].astype(F32) + rz1[r, 1, 3].astype(F32)).astype(BF16)
        for k in range(2):
            @pl.when(role != k)
            def _():
                rzy_to(r, k).start()

    def rzx_to(r, d):
        return rdma(
            R["tz"].at[r, xo(d)], R["rzx"].at[x], R["ssrz3"].at[r], R["rsrz3"].at[0], dev(xo(d), y, z, r)
        )

    def rzx_all(r, act):
        for d in (2, 1, 3):
            act(rzx_to(r, d))

        @pl.when(c != r)
        def _():
            act(rzx_to(r, 0))

    def rz_rows(r):
        @pl.when(home)
        def _():
            arrived(R["rzy"].at[r, pl.ds(0, 3)], R["rsrz2"].at[r])
            v = pz[r, zi, yp].astype(F32)
            for d in range(1, 4):
                v += R["rzy"][r, yo(d)].astype(F32)
            R["tz"][r] = v.astype(BF16)
            rzx_all(r, begin)

            @pl.when(c == r)
            def _():
                pltpu.make_async_copy(R["tz"].at[r, x], R["rzx"].at[x], R["rsrz3"].at[0]).start()

    def r1x_opp(r, d):
        return rdma(
            px.at[r, xo(2) * 2 + d], R["r1o"].at[r, d], R["ssr1"].at[r, 0], R["rsr1x"].at[r, d],
            dev(xo(1 - 2 * d), y, z, c),
        )

    def r1x_free(r, d):
        return rdma(
            px.at[r, xo(1 - 2 * d) * 2 + 1 - d], R["r1n"].at[r, d, 1 - d], R["ssr1"].at[r, 0],
            R["rsr1x"].at[r, 2], dev(xo(1 - 2 * d), y, z, c),
        )

    def r1x_dep(r, d):
        return rdma(
            px.at[r, xo(1 - 2 * d) * 2 + d], R["r1n"].at[r, d, d], R["ssr1"].at[r, 0],
            R["rsr1x"].at[r, 2], dev(xo(1 - 2 * d), y, z, c),
        )

    y_opp = {2: ((1, 0, 0), (0, 0, 1)), 3: ((0, 1, 0), (1, 1, 1))}
    y_free = {0: (0, 1, 1), 1: (1, 0, 1), 2: (1, 1, 0), 3: (0, 0, 0)}
    y_dep = {0: (0, 1, 0), 1: (1, 0, 0), 2: (1, 1, 1), 3: (0, 0, 1)}

    def r1y_opp(r, o, i):
        d, k, j = y_opp[o][i]
        return rdma(
            py.at[r, half_y(k, j)], R["r1yo"].at[r], R["ssr1"].at[r, 1], R["rsr1y"].at[r, 0],
            dev(x, yo(1 - 2 * d), z, c),
        )

    def r1y_next(r, o, dep):
        d, k, j = (y_dep if dep else y_free)[o]
        side = 0 if o >= 2 else 1
        return rdma(
            py.at[r, half_y(k, j)], R["r1yn"].at[r, side, pl.ds(j * 2, 2)], R["ssr1"].at[r, 1],
            R["rsr1y"].at[r, 1], dev(x, yo(1 - 2 * d), z, c),
        )

    def opp_x(r):
        for d in range(2):
            r1x_opp(r, d).start()

    def free_x(r):
        for d in range(2):
            r1x_free(r, d).start()

    def opp_y(r):
        for o in (2, 3):
            @pl.when(role == o)
            def _():
                for i in range(2):
                    r1y_opp(r, o, i).start()

    def free_y(r):
        for o in range(4):
            @pl.when(role == o)
            def _():
                r1y_next(r, o, 0).start()

    r1o, r1yo, r1n, r1yn = (R[n] for n in ("r1o", "r1yo", "r1n", "r1yn"))

    def dep_x(r):
        for d in range(2):
            arrived(r1o.at[r, d], R["rsr1x"].at[r, d])
            to = xo(1 - 2 * d) * 2 + d

            @pl.loop(0, 8, unroll=2)
            def _(i):
                px[r, to, i] = (px[r, to, i].astype(F32) + r1o[r, d, i].astype(F32)).astype(BF16)

            r1x_dep(r, d).start()
    def dep_y(r):
        arrived(r1yo.at[r], R["rsr1y"].at[r, 0])
        for o in range(4):
            @pl.when(role == o)
            def _():
                _d, k, j = y_dep[o]

                @pl.loop(0, 8)
                def _(i):
                    for xx in range(2):
                        at = k * 4 + j * 2 + xx
                        py[r, at, i] = (py[r, at, i].astype(F32) + r1yo[r, xx, i].astype(F32)).astype(BF16)

                r1y_next(r, o, 1).start()

    sx, sy, r2x, r2y, tx, ty = (R[n] for n in ("sx", "sy", "r2x", "r2y", "tx", "ty"))

    def r2x_to(r, k):
        return rdma(
            sx.at[r, k], r2x.at[r, y], R["ssr2"].at[r, 0], R["rsr2x"].at[r], dev(x, 2 * c + k, z, c)
        )

    def r2y_to(r, d):
        return rdma(
            sy.at[r, xo(d)], r2y.at[r, x], R["ssr2"].at[r, 1], R["rsr2y"].at[r], dev(xo(d), y, z, c)
        )

    def rs2x(r):
        arrived(r1n.at[r], R["rsr1x"].at[r, 2])

        @pl.loop(0, 8)
        def _(b):
            for k in range(2):
                sx[r, k, b] = (
                    px[r, x * 2 + k, b].astype(F32) + r1n[r, 0, k, b].astype(F32) + r1n[r, 1, k, b].astype(F32)
                ).astype(BF16)

        for k in range(2):
            @pl.when(role != k)
            def _():
                r2x_to(r, k).start()

    def rs2y(r):
        @pl.when(home)
        def _():
            arrived(r1yn.at[r], R["rsr1y"].at[r, 1])

            @pl.loop(0, 8)
            def _(b):
                for k in range(4):
                    sy[r, k, b] = (
                        py[r, yp * 4 + k, b].astype(F32) + r1yn[r, 0, k, b].astype(F32) + r1yn[r, 1, k, b].astype(F32)
                    ).astype(BF16)

            for d in (2, 1, 3):
                r2y_to(r, d).start()

    def r3_to(r, route, d):
        t, dst = ((tx, R["r3x"]), (ty, R["r3y"]))[route]
        zz = zo(d)
        return rdma(
            t.at[r, zind(zz)], dst.at[zi], R["ssr3"].at[r, route], R["rsr3"].at[route], dev(x, y, zz, r)
        )

    def r3_all(r, route, act):
        for d in (4, 3, 5, 2, 6, 1, 7):
            act(r3_to(r, route, d))

        @pl.when(c != r)
        def _():
            act(r3_to(r, route, 0))

    def r3_own(r, route):
        t, dst = ((tx, R["r3x"]), (ty, R["r3y"]))[route]

        @pl.when(c == r)
        def _():
            pltpu.make_async_copy(t.at[r, zi], dst.at[zi], R["rsr3"].at[route]).start()

    def rs3x(r):
        @pl.when(home)
        def _():
            arrived(r2x.at[r, pl.ds(0, 3)], R["rsr2x"].at[r])

            @pl.loop(0, 8, unroll=2)
            def _(b):
                v = sx[r, yp, b].astype(F32)
                for d in range(1, 4):
                    v += r2x[r, yo(d), b].astype(F32)
                tx[r, b] = v.astype(BF16)

            r3_all(r, 0, begin)
            r3_own(r, 0)

    def rs3y(r):
        @pl.when(home)
        def _():
            arrived(r2y.at[r, pl.ds(0, 3)], R["rsr2y"].at[r])

            @pl.loop(0, 8, unroll=2)
            def _(b):
                v = sy[r, x, b].astype(F32)
                for d in range(1, 4):
                    v += r2y[r, xo(d), b].astype(F32)
                ty[r, b] = v.astype(BF16)

            r3_all(r, 1, begin)
            r3_own(r, 1)

    def finish(route):
        src, n, o = ((R["r3x"], XW, XO), (R["r3y"], YW, YO))[route]
        arrived(src, R["rsr3"].at[route])
        total = src[0].astype(F32)
        for b in range(1, 8):
            total += src[b].astype(F32)
        R["gv_v"][:, o : o + n] = total

    def finish_z():
        arrived(R["rzx"], R["rsrz3"].at[0])
        total = R["rzx"][0].astype(F32)
        for b in range(1, 4):
            total += R["rzx"][b].astype(F32)
        R["gv_v"][:, :ZW] = total

    outs = [
        pltpu.make_async_copy(R["att_v"], att_o.at[0], R["osem"].at[0]),
        pltpu.make_async_copy(R["dq_v"], dq_o.at[0], R["osem"].at[1]),
        pltpu.make_async_copy(R["gv_v"], gv_o, R["osem"].at[2]),
    ]

    key_grads(0)
    swap2(0).start()
    key_grads(1)
    swap2(1).start()
    both(0)
    back(0, 1)
    opp_x(0)
    free_x(0)
    back(0, 0)
    for d in range(2):
        rz(0, d, 0).start()
    back(0, 2)
    opp_y(0)
    free_y(0)
    both(1)
    back(1, 1)
    opp_x(1)
    back(1, 2)
    opp_y(1)
    back(1, 0)
    for d in range(2):
        rz(1, d, 0).start()
    dep_x(0)
    free_x(1)
    dep_y(0)
    free_y(1)
    rzstep(0, 1)
    rzstep(1, 1)
    heads_out(0, 4)
    dep_x(1)
    dep_y(1)
    rzstep(0, 2)
    rzstep(1, 2)
    heads_out(4, 8)
    for cp in outs[:2]:
        cp.start()
    rs2x(0)
    rs2y(0)
    rzstep(0, 3)
    rzstep(1, 3)
    rs2x(1)
    rs2y(1)
    rs3x(0)
    rs3y(0)
    rz_sum(0)
    rz_sum(1)
    rz_rows(0)
    rz_rows(1)
    rs3x(1)
    rs3y(1)
    finish_z()
    finish(0)
    finish(1)
    outs[2].start()

    by_home(
        lambda: sent(gz.at[0, 0, 0, pl.ds(0, 3)], R["ssz1"].at[0]),
        lambda: sent(gz.at[0, 0, 0], R["ssz1"].at[0]),
    )
    for i, ref in enumerate((gx, gy)):
        by_home(
            lambda: sent(ref.at[0, 0, pl.ds(0, 7)], R["ss1"].at[i]),
            lambda: sent(ref.at[0, 0], R["ss1"].at[i]),
        )
    for r in range(2):
        sent(gz.at[r, pl.ds(0, 7)], R["ssz3"].at[r])
        sent(pz.at[r, pl.ds(0, 7)], R["ssrz1"].at[r])
        sent(gx.at[r, pl.ds(0, 6)], R["ss3"].at[r, 0])
        sent(px.at[r, pl.ds(0, 6)], R["ssr1"].at[r, 0])

        @pl.when(home)
        def _():
            sent(R["rzy"].at[r, pl.ds(0, 3)], R["ssz2"].at[r])
            sent(gx.at[r, pl.ds(0, 3)], R["ss2"].at[r, 0])
            sent(gy.at[r, pl.ds(0, 3)], R["ss2"].at[r, 1])
            sent(sy.at[r, pl.ds(0, 3)], R["ssr2"].at[r, 1])
            sent(gy.at[:, pl.ds(0, 5)], R["ss3"].at[r, 1])

            @pl.when(c == r)
            def _():
                sent(tx.at[r, pl.ds(0, 7)], R["ssr3"].at[r, 0])
                sent(ty.at[r, pl.ds(0, 7)], R["ssr3"].at[r, 1])
                sent(R["tz"].at[r, pl.ds(0, 3)], R["ssrz3"].at[r])

            @pl.when(c != r)
            def _():
                sent(tx.at[r], R["ssr3"].at[r, 0])
                sent(ty.at[r], R["ssr3"].at[r, 1])
                sent(R["tz"].at[r], R["ssrz3"].at[r])

        by_home(
            lambda: sent(py.at[r, pl.ds(0, 4)], R["ssr1"].at[r, 1]),
            lambda: sent(py.at[r], R["ssr1"].at[r, 1]),
        )
        by_home(
            lambda: sent(sx.at[r, 0], R["ssr2"].at[r, 0]),
            lambda: sent(sx.at[r], R["ssr2"].at[r, 0]),
        )
        by_home(
            lambda: sent(pz.at[r, 0, 0], R["ssrz2"].at[r]),
            lambda: sent(pz.at[r, 0], R["ssrz2"].at[r]),
        )

        @pl.when(c == 1 - h)
        def _():
            sent(gy.at[r, pl.ds(0, 2)], R["ss3"].at[r, 1])

    for cp in outs:
        cp.wait()


def copy_out(a, b, d, ao, bo, do, av, bv, dv, sems):
    moves = ((a, av, ao), (b, bv, bo), (d, dv, do))
    loads = [pltpu.make_async_copy(s, v, sems.at[0, i]) for i, (s, v, _) in enumerate(moves)]
    stores = [pltpu.make_async_copy(v, t, sems.at[1, i]) for i, (_, v, t) in enumerate(moves)]
    for cp in loads:
        cp.start()
    for load, store in zip(loads, stores):
        load.wait()
        store.start()
    for cp in stores:
        cp.wait()


def on_device(queries, grad_attended, vision, key_weight, value_weight, tile_limit):
    vmem = pl.BlockSpec(memory_space=pltpu.VMEM)
    hbm = pl.BlockSpec(memory_space=pl.ANY)
    shapes = (
        jax.ShapeDtypeStruct(queries.shape, BF16),
        jax.ShapeDtypeStruct(queries.shape, BF16),
        jax.ShapeDtypeStruct(vision.shape, F32),
    )
    outs = pl.pallas_call(
        kernel,
        out_shape=shapes,
        in_specs=[hbm, hbm, hbm, hbm, hbm, vmem],
        out_specs=(hbm, hbm, hbm),
        scratch_shapes=list(scratch().values()),
        compiler_params=pltpu.CompilerParams(
            collective_id=0, has_side_effects=True, vmem_limit_bytes=60 * 2**20
        ),
        cost_estimate=pl.CostEstimate(flops=6_000_000_000, bytes_accessed=6_000_000, transcendentals=1_000_000),
    )(vision, key_weight, value_weight, queries, grad_attended, tile_limit)
    return pl.pallas_call(
        copy_out,
        out_shape=shapes,
        in_specs=[hbm, hbm, hbm],
        out_specs=(hbm, hbm, hbm),
        scratch_shapes=[pltpu.VMEM(s.shape, s.dtype) for s in shapes] + [pltpu.SemaphoreType.DMA((2, 3))],
    )(*outs)


def solution(mesh):
    return jax.shard_map(
        on_device,
        mesh=mesh,
        in_specs=(
            P("segment", None, "tensor"),
            P("segment", None, "tensor"),
            P("segment", "tensor"),
            P("segment", None, "tensor"),
            P("segment", None, "tensor"),
            P(),
        ),
        out_specs=(
            P("segment", None, "tensor"),
            P("segment", None, "tensor"),
            P("segment", "tensor"),
        ),
        check_vma=False,
    )
```

```python
import jax
import jax.numpy as jnp
from jax import lax
from jax.experimental import pallas as pl
from jax.experimental.pallas import tpu as pltpu
from jax.sharding import PartitionSpec as P

HD = 128
EPS = 1e-05
SCALE = HD ** (-0.5)
LOG2E = 1.4426950408889634
F32 = jnp.float32
BF16 = jnp.bfloat16
MESH = pl.DeviceIdType.MESH

ZW, XW, YW = 256, 384, 384
XO, YO = ZW, ZW + XW


def scratch():
    v, dma = pltpu.VMEM, pltpu.SemaphoreType.DMA
    s = {
        "vis": v((16, 1024), BF16),
        "q": v((8, 256, 128), BF16), "do": v((8, 256, 128), BF16),
        "w": v((4096, 256), BF16), "wt": v((256, 4096), BF16),
        "qt": v((8, 128, 256), BF16), "dot": v((8, 128, 256), BF16),
        "bias": v((4, 16, 256), F32),
        "part": v((512, 256), F32), "part_in": v((512, 256), F32),
        "kv": v((2, 512, 128), BF16), "kvt": v((2, 128, 512), BF16),
        "probs": v((512, 2048), BF16), "dsc": v((512, 2048), BF16), "at": v((8, 128, 256), BF16),
        "dkv": v((512, 256), BF16), "dkv_in": v((512, 256), BF16),
        "att_v": v((256, 1024), BF16), "dq_v": v((256, 1024), BF16), "gv_v": v((16, 1024), F32),
        "gz": v((2, 8, 2, 4, 16, ZW), BF16), "pz": v((2, 8, 2, 4, 16, ZW), BF16),
        "rz1": v((2, 2, 4, 2, 4, 16, ZW), BF16), "rzy": v((2, 4, 4, 16, ZW), BF16),
        "tz": v((2, 4, 16, ZW), BF16), "rzx": v((4, 16, ZW), BF16),
        "gx": v((2, 8, 8, 16, XW), BF16), "gy": v((2, 8, 8, 16, YW), BF16),
        "px": v((2, 8, 8, 16, XW), BF16), "py": v((2, 8, 8, 16, YW), BF16),
        "r1o": v((2, 2, 8, 16, XW), BF16), "r1n": v((2, 2, 2, 8, 16, XW), BF16),
        "r1yo": v((2, 2, 8, 16, YW), BF16), "r1yn": v((2, 2, 4, 8, 16, YW), BF16),
        "sx": v((2, 2, 8, 16, XW), BF16), "sy": v((2, 4, 8, 16, YW), BF16),
        "r2x": v((2, 4, 8, 16, XW), BF16), "r2y": v((2, 4, 8, 16, YW), BF16),
        "tx": v((2, 8, 16, XW), BF16), "ty": v((2, 8, 16, YW), BF16),
        "r3x": v((8, 16, XW), BF16), "r3y": v((8, 16, YW), BF16),
        "lsem": dma((5,)), "osem": dma((3,)), "ss4": dma((4,)), "rs4": dma((4,)),
        "ssz1": dma((1,)), "ss1": dma((2,)), "ssz2": dma((2,)), "ss2": dma((2, 2)), "ss3": dma((2, 2)),
        "ssz3": dma((2,)), "ssrz1": dma((2,)), "ssr1": dma((2, 2)), "ssr2": dma((2, 2)), "ssr3": dma((2, 2)),
        "ssrz2": dma((2,)), "ssrz3": dma((2,)),
        "rsz1": dma((2,)), "rs1": dma((2, 2)), "rsz2": dma((2,)), "rs2x": dma((2,)), "rs2y": dma((2,)),
        "rs3x": dma((2, 3)), "rs3y": dma((2, 2)), "rsz3": dma((2, 7)),
        "rsrz1": dma((2, 7)), "rsr1x": dma((2, 3)), "rsr1y": dma((2, 2)), "rsr2x": dma((2,)), "rsr2y": dma((2,)),
        "rsr3": dma((2,)), "rsrz2": dma((2,)), "rsrz3": dma((1,)),
    }
    return s


NAMES = tuple(scratch())


def mm(a, b):
    return jnp.dot(a, b, preferred_element_type=F32)


def kernel(vis_in, wk, wv, q_in, do_in, lim, att_o, dq_o, gv_o, *rest):
    R = dict(zip(NAMES, rest, strict=True))
    vis, q, do, w, wt = R["vis"], R["q"], R["do"], R["w"], R["wt"]
    gx, gy, gz, px, py, pz = (R[n] for n in ("gx", "gy", "gz", "px", "py", "pz"))

    seg, ten = lax.axis_index("segment"), lax.axis_index("tensor")
    zh, x, c = lax.div(seg, 8), lax.rem(lax.div(seg, 2), 4), lax.rem(seg, 2)
    y, zl = lax.div(ten, 2), lax.rem(ten, 2)
    z = zh * 2 + zl
    zi = zl * 4 + zh
    h, yp = lax.div(y, 2), lax.rem(y, 2)
    role = lax.rem(y + 4 - 2 * c, 4)
    home = c == h

    def dev(xx, yy, zz, cc):
        return (lax.div(zz, 2) * 8 + xx * 2 + cc, yy * 2 + lax.rem(zz, 2))

    def zind(zz):
        return lax.rem(zz, 2) * 4 + lax.div(zz, 2)

    def xo(d):
        return lax.rem(x + d + 4, 4)

    def yo(d):
        return lax.rem(y + d + 4, 4)

    def zo(d):
        return lax.rem(z + d + 8, 8)

    partner = dev(x, y, z, 1 - c)

    def rdma(src, dst, ss, rs, to):
        return pltpu.make_async_remote_copy(
            src_ref=src, dst_ref=dst, send_sem=ss, recv_sem=rs, device_id=to, device_id_type=MESH
        )

    def arrived(dst, rs):
        rdma(dst, dst, R["ss4"].at[0], rs, partner).wait_recv()

    def begin(cp):
        cp.start()

    def sent(ref, ss):
        rdma(ref, ref, ss, R["rs4"].at[0], partner).wait_send()

    lsem = R["lsem"]
    wcopies = [
        pltpu.make_async_copy(wk.at[0], w.at[:, pl.ds(0, HD)], lsem.at[0]),
        pltpu.make_async_copy(wv.at[0], w.at[:, pl.ds(HD, HD)], lsem.at[1]),
    ]

    barrier = pltpu.get_barrier_semaphore()
    greet = [dev(x, y, zo(d), cc) for d in range(1, 8) for cc in (0, 1)]
    greet += [dev(xo(d), y, z, cc) for d in range(1, 4) for cc in (0, 1)]
    greet += [dev(x, yo(d), z, c) for d in range(1, 4)] + [partner]
    shard = pltpu.make_async_copy(vis_in, vis, lsem.at[4])
    shard.start()
    for other in greet:
        pl.semaphore_signal(barrier, inc=1, device_id=other, device_id_type=MESH)
    for cp in wcopies:
        cp.start()
    loads = [
        pltpu.make_async_copy(q_in.at[0], R["att_v"], lsem.at[2]),
        pltpu.make_async_copy(do_in.at[0], R["dq_v"], lsem.at[3]),
    ]
    for cp in loads:
        cp.start()
    shard.wait()
    pl.semaphore_wait(barrier, len(greet))

    def z1(d):
        return rdma(vis.at[:, pl.ds(0, ZW)], gz.at[c, zi, yp, x], R["ssz1"].at[0], R["rsz1"].at[c], dev(xo(d), y, z, h))

    def z1_all(act):
        for d in (2, 1, 3):
            act(z1(d))

        @pl.when(c == 1 - h)
        def _():
            act(z1(0))

    def g1(route, d):
        src, dst = (
            (vis.at[:, pl.ds(XO, XW)], gx.at[c, x * 2 + yp, zi]),
            (vis.at[:, pl.ds(YO, YW)], gy.at[c, yp * 4 + x, zi]),
        )[route]
        return rdma(src, dst, R["ss1"].at[route], R["rs1"].at[c, route], dev(x, y, zo(d), h))

    def g1_all(route, act):
        for d in (4, 3, 5, 2, 6, 1, 7):
            act(g1(route, d))

        @pl.when(c == 1 - h)
        def _():
            act(g1(route, 0))

    z1_all(begin)
    for route in range(2):
        g1_all(route, begin)

    @pl.when(home)
    def _():
        pltpu.make_async_copy(vis.at[:, pl.ds(0, ZW)], gz.at[c, zi, yp, x], R["rsz1"].at[c]).start()
        pltpu.make_async_copy(vis.at[:, pl.ds(XO, XW)], gx.at[c, x * 2 + yp, zi], R["rs1"].at[c, 0]).start()
        pltpu.make_async_copy(vis.at[:, pl.ds(YO, YW)], gy.at[c, yp * 4 + x, zi], R["rs1"].at[c, 1]).start()

    for cp in loads:
        cp.wait()
    qt, dot_, bias = R["qt"], R["dot"], R["bias"]

    @pl.loop(0, 8)
    def _(n):
        lanes = pl.ds(pl.multiple_of(n * HD, HD), HD)
        qn = R["att_v"][:, lanes]
        dn = R["dq_v"][:, lanes]
        q[n] = qn
        do[n] = dn
        qt[n] = qn.astype(F32).T.astype(BF16)
        dot_[n] = dn.astype(F32).T.astype(BF16)

    def z2(r, d):
        blk = gz.at[r, zi, yp]
        return rdma(blk, blk, R["ssz2"].at[r], R["rsz2"].at[r], dev(x, yo(d), z, c))

    @pl.when(home)
    def _():
        for r in range(2):
            arrived(gz.at[r, zi, yp], R["rsz1"].at[r])
            for d in (2, 1, 3):
                z2(r, d).start()

    def g2x(r, d):
        blk = gx.at[r, x * 2 + yp]
        return rdma(blk, blk, R["ss2"].at[r, 0], R["rs2x"].at[r], dev(x, yo(d), z, c))

    def g2y(r, d):
        blk = gy.at[r, yp * 4 + x]
        return rdma(blk, blk, R["ss2"].at[r, 1], R["rs2y"].at[r], dev(xo(d), y, z, c))

    def step2x(r):
        @pl.when(home)
        def _():
            arrived(gx.at[r, x * 2 + yp], R["rs1"].at[r, 0])
            for d in (2, 1, 3):
                g2x(r, d).start()

    def step2y(r):
        @pl.when(home)
        def _():
            arrived(gy.at[r, yp * 4 + x], R["rs1"].at[r, 1])
            for d in (2, 1, 3):
                g2y(r, d).start()

    def by_home(few, many):
        @pl.when(home)
        def _():
            few()

        @pl.when(c == 1 - h)
        def _():
            many()

    def z3(r, d, s):
        side = 1 - 2 * d
        at = zind(zo(-side * s))
        blk = gz.at[r, at] if s < 3 else gz.at[r, at, d]
        return rdma(blk, blk, R["ssz3"].at[r], R["rsz3"].at[r, s * 2 + d if s < 3 else 6], dev(x, y, zo(side), c))

    def z3_arrived(r, d, s):
        arrived(gz.at[r, zind(zo(-(1 - 2 * d) * (s + 1)))], R["rsz3"].at[r, s * 2 + d])

    def z3_last(r):
        arrived(gz.at[r, zind(zo(4))], R["rsz3"].at[r, 6])

    def zstep(r, s):
        if s == 0:
            by_home(
                lambda: arrived(gz.at[r, zi, 1 - yp], R["rsz2"].at[r]),
                lambda: arrived(gz.at[r, zi], R["rsz2"].at[r]),
            )
        for d in range(2):
            if s > 0:
                z3_arrived(r, d, s - 1)
            z3(r, d, s).start()

    def g3x(r, d, half):
        blk = gx.at[r, x * 2 + half]
        return rdma(blk, blk, R["ss3"].at[r, 0], R["rs3x"].at[r, d if half == d else 2], dev(xo(1 - 2 * d), y, z, c))

    def g3xf(r, d):
        blk = gx.at[r, xo(2 * d - 1) * 2 + d]
        return rdma(blk, blk, R["ss3"].at[r, 0], R["rs3x"].at[r, 2], dev(xo(1 - 2 * d), y, z, c))

    def half_y(k, j):
        return pl.ds(k * 4 + j * 2, 2)

    passed = ((1, 0, 1), (0, 0, 0), (1, 1, 0), (0, 1, 1))

    def g3y(r, o, k, j, d):
        blk = gy.at[r, half_y(k, j)]
        first = passed[(o + 1 - 2 * d) % 4][:2] == (k, j)
        return rdma(blk, blk, R["ss3"].at[r, 1], R["rs3y"].at[r, 0 if first else 1], dev(x, yo(1 - 2 * d), z, c))

    def g3y_role(r, o):
        order = ((0, 0, 0), (0, 1, 1), (0, 1, 0), (0, 0, 1)) if o == 0 else ((1, 0, 1), (1, 1, 0), (1, 1, 1), (1, 0, 0))
        return [g3y(r, o, k, j, d) for k, j, d in order]

    def g3yf(r, o):
        k, j, d = passed[o]
        return g3y(r, o, k, j, d)

    def step3x(r):
        by_home(
            lambda: arrived(gx.at[r, x * 2 + 1 - yp], R["rs2x"].at[r]),
            lambda: arrived(gx.at[r, pl.ds(x * 2, 2)], R["rs2x"].at[r]),
        )
        for d, half in ((0, 0), (1, 1), (0, 1), (1, 0)):
            g3x(r, d, half).start()

    def step3y(r):
        for o in (0, 1):
            @pl.when(role == o)
            def _():
                arrived(gy.at[r, pl.ds(o * 4, 3)], R["rs2y"].at[r])
                for cp in g3y_role(r, o):
                    cp.start()

    def forward3x(r):
        for d in range(2):
            arrived(gx.at[r, xo(2 * d - 1) * 2 + d], R["rs3x"].at[r, d])
            g3xf(r, d).start()

    def forward3y(r):
        for o in range(4):
            @pl.when(role == o)
            def _():
                arrived(gy.at[r, half_y(*passed[o][:2])], R["rs3y"].at[r, 0])
                g3yf(r, o).start()

    def rest3x(r):
        arrived(gx.at[r, pl.ds(0, 4)], R["rs3x"].at[r, 2])

    def rest3y(r):
        by_home(
            lambda: arrived(gy.at[r, pl.ds(0, 2)], R["rs3y"].at[r, 1]),
            lambda: arrived(gy.at[r, pl.ds(0, 6)], R["rs3y"].at[r, 1]),
        )

    part, part_in = R["part"], R["part_in"]
    ROWS = (slice(0, 256), slice(256, 512))

    def project(r, route):
        total = part[ROWS[r], :] if route != (1, 0)[r] else jnp.zeros((256, 256), F32)
        for k in range(2):
            for l in range(2):
                base = (k * 2 + l) * 1024
                zs = slice(l * 4, l * 4 + 4)
                if route == 0:
                    a = jnp.concatenate([gz[r, zs, k, xx].reshape(64, ZW) for xx in range(4)], axis=0)
                    total += mm(a, w[base : base + ZW, :])
                elif route == 1:
                    a = jnp.concatenate([gx[r, xx * 2 + k, zs].reshape(64, XW) for xx in range(4)], axis=0)
                    total += mm(a, w[base + XO : base + XO + XW, :])
                else:
                    a = gy[r, k * 4 : k * 4 + 4, zs].reshape(256, YW)
                    total += mm(a, w[base + YO : base + YO + YW, :])
        part[ROWS[r], :] = total

    def swap(r):
        rows = pl.ds(r * 256, 256)
        return rdma(part.at[rows], part_in.at[rows], R["ss4"].at[r], R["rs4"].at[r], partner)

    kv, kvt = R["kv"], R["kvt"]

    def keys_values(r):
        rows = ROWS[r]
        pre = part[rows, :] + part_in[rows, :]
        part_in[rows, :] = pre
        kp = pre[:, :HD]
        inv = lax.rsqrt(jnp.mean(kp * kp, axis=-1, keepdims=True) + EPS)
        keys = (kp * inv).astype(BF16)
        vals = pre[:, HD:].astype(BF16)
        kv[0, rows] = keys
        kv[1, rows] = vals
        kvt[0, :, rows] = keys.astype(F32).T.astype(BF16)
        kvt[1, :, rows] = vals.astype(F32).T.astype(BF16)

    def transpose_weights(lo, hi):
        @pl.loop(lo, hi)
        def _(n):
            rows = pl.ds(pl.multiple_of(n * 256, 256), 256)
            wt[:, rows] = w[rows, :].astype(F32).T.astype(BF16)

    step2x(0)
    step2x(1)
    step2y(0)
    step2y(1)
    zstep(0, 0)
    zstep(1, 0)
    for cp in wcopies:
        cp.wait()
    step3x(0)
    step3y(0)
    step3x(1)
    step3y(1)
    transpose_weights(0, 8)
    zstep(0, 1)
    zstep(1, 1)
    transpose_weights(8, 16)
    limits = lim[...].reshape(1, 512)
    limit = (1 - c) * limits[:, :256] + c * limits[:, 256:]
    for t in range(4):
        bias[t] = jnp.broadcast_to(jnp.where(t < limit, 0.0, -1e30), (16, 256))
    forward3x(0)
    forward3y(0)
    zstep(0, 2)
    zstep(1, 2)
    forward3x(1)
    forward3y(1)
    zstep(0, 3)
    zstep(1, 3)
    rest3x(0)
    project(0, 1)
    rest3y(0)
    project(0, 2)
    z3_last(0)
    project(0, 0)
    swap(0).start()
    z3_last(1)
    project(1, 0)
    swap(0).wait()
    keys_values(0)
    rest3x(1)
    project(1, 1)
    rest3y(1)
    project(1, 2)
    swap(1).start()
    swap(1).wait()
    keys_values(1)

    probs, dsc, at_ = R["probs"], R["dsc"], R["at"]

    @pl.loop(0, 8, unroll=8)
    def _(n):
        lanes = pl.ds(pl.multiple_of(n * 256, 256), 256)
        dotn = dot_[n]
        s = mm(kv[0], qt[n]) * (SCALE * LOG2E)
        s = (s.reshape(8, 4, 16, 256) + bias[...][None]).reshape(512, 256)
        m = jnp.max(s, axis=0, keepdims=True)
        e = jnp.exp2(s - m)
        prob = e * (1.0 / jnp.sum(e, axis=0, keepdims=True))
        pb16 = prob.astype(BF16)
        probs[:, lanes] = pb16
        at = mm(kvt[1], pb16).astype(BF16)
        at_[n] = at
        dp = mm(kv[1], dotn)
        delta = jnp.sum(at.astype(F32) * dotn.astype(F32), axis=0, keepdims=True)
        dsc[:, lanes] = (prob * (dp - delta)).astype(BF16)

    dkv, dkv_in = R["dkv"], R["dkv_in"]

    def key_grads(r):
        rows = ROWS[r]
        kp = part_in[rows, :HD]
        inv = lax.rsqrt(jnp.mean(kp * kp, axis=-1, keepdims=True) + EPS)
        dk = mm(dsc[rows, :], q[...].reshape(2048, HD)) * SCALE
        dv = mm(probs[rows, :], do[...].reshape(2048, HD))
        dkp = inv * dk - kp * (inv * inv * inv * jnp.mean(kp * dk, axis=-1, keepdims=True))
        dkv[rows, :HD] = dkp.astype(BF16)
        dkv[rows, HD:] = dv.astype(BF16)

    def swap2(r):
        rows = pl.ds(r * 256, 256)
        return rdma(dkv.at[rows], dkv_in.at[rows], R["ss4"].at[2 + r], R["rs4"].at[2 + r], partner)

    def heads_out(lo, hi):
        @pl.loop(lo, hi, unroll=2)
        def _(n):
            lanes = pl.ds(pl.multiple_of(n * HD, HD), HD)
            dqt = mm(kvt[0], dsc[:, pl.ds(pl.multiple_of(n * 256, 256), 256)]) * SCALE
            R["dq_v"][:, lanes] = dqt.T.astype(BF16)
            R["att_v"][:, lanes] = at_[n].astype(F32).T.astype(BF16)

    def both(r):
        swap2(r).wait()
        rows = ROWS[r]
        dkv[rows, :] = (dkv[rows, :].astype(F32) + dkv_in[rows, :].astype(F32)).astype(BF16)

    def back(r, route):
        for k in range(2):
            for l in range(2):
                base = (k * 2 + l) * 1024 + (0, XO, YO)[route]
                n = (ZW, XW, YW)[route]
                zs = slice(l * 4, l * 4 + 4)
                wtb = wt[:, base : base + n]
                v = mm(dkv[ROWS[r], :], wtb).astype(BF16)
                if route == 2:
                    py[r, k * 4 : k * 4 + 4, zs] = v.reshape(4, 4, 16, YW)
                    continue
                for xx in range(4):
                    b = v[xx * 64 : (xx + 1) * 64].reshape(4, 16, n)
                    if route == 0:
                        pz[r, zs, k, xx] = b
                    else:
                        px[r, xx * 2 + k, zs] = b

    rz1 = R["rz1"]

    def rz(r, d, s):
        side = 1 - 2 * d
        at = zind(zo(side * (4 - s)))
        src = pz.at[r, at, d] if s == 0 else pz.at[r, at]
        dst = rz1.at[r, d, 0, d] if s == 0 else rz1.at[r, d, s]
        return rdma(src, dst, R["ssrz1"].at[r], R["rsrz1"].at[r, s * 2 + d if s < 3 else 6], dev(x, y, zo(side), c))

    def rz_arrived(r, d, s):
        arrived(rz1.at[r, d, 0, d] if s == 0 else rz1.at[r, d, s], R["rsrz1"].at[r, s * 2 + d])

    def rzstep(r, s):
        for d in range(2):
            if s > 0:
                rz_arrived(r, d, s - 1)
                at = zind(zo((1 - 2 * d) * (4 - s)))
                if s == 1:
                    pz[r, at, d] = (pz[r, at, d].astype(F32) + rz1[r, d, 0, d].astype(F32)).astype(BF16)
                else:
                    pz[r, at] = (pz[r, at].astype(F32) + rz1[r, d, s - 1].astype(F32)).astype(BF16)
            rz(r, d, s).start()

    def rzy_to(r, k):
        return rdma(
            pz.at[r, zi, k], R["rzy"].at[r, y], R["ssrz2"].at[r], R["rsrz2"].at[r], dev(x, 2 * c + k, z, c)
        )

    def rz_sum(r):
        arrived(rz1.at[r, 0, pl.ds(2, 2)], R["rsrz1"].at[r, 6])
        pz[r, zi] = (pz[r, zi].astype(F32) + rz1[r, 0, 3].astype(F32) + rz1[r, 1, 3].astype(F32)).astype(BF16)
        for k in range(2):
            @pl.when(role != k)
            def _():
                rzy_to(r, k).start()

    def rzx_to(r, d):
        return rdma(
            R["tz"].at[r, xo(d)], R["rzx"].at[x], R["ssrz3"].at[r], R["rsrz3"].at[0], dev(xo(d), y, z, r)
        )

    def rzx_all(r, act):
        for d in (2, 1, 3):
            act(rzx_to(r, d))

        @pl.when(c != r)
        def _():
            act(rzx_to(r, 0))

    def rz_rows(r):
        @pl.when(home)
        def _():
            arrived(R["rzy"].at[r, pl.ds(0, 3)], R["rsrz2"].at[r])
            v = pz[r, zi, yp].astype(F32)
            for d in range(1, 4):
                v += R["rzy"][r, yo(d)].astype(F32)
            R["tz"][r] = v.astype(BF16)
            rzx_all(r, begin)

            @pl.when(c == r)
            def _():
                pltpu.make_async_copy(R["tz"].at[r, x], R["rzx"].at[x], R["rsrz3"].at[0]).start()

    def r1x_opp(r, d):
        return rdma(
            px.at[r, xo(2) * 2 + d], R["r1o"].at[r, d], R["ssr1"].at[r, 0], R["rsr1x"].at[r, d],
            dev(xo(1 - 2 * d), y, z, c),
        )

    def r1x_free(r, d):
        return rdma(
            px.at[r, xo(1 - 2 * d) * 2 + 1 - d], R["r1n"].at[r, d, 1 - d], R["ssr1"].at[r, 0],
            R["rsr1x"].at[r, 2], dev(xo(1 - 2 * d), y, z, c),
        )

    def r1x_dep(r, d):
        return rdma(
            px.at[r, xo(1 - 2 * d) * 2 + d], R["r1n"].at[r, d, d], R["ssr1"].at[r, 0],
            R["rsr1x"].at[r, 2], dev(xo(1 - 2 * d), y, z, c),
        )

    y_opp = {2: ((1, 0, 0), (0, 0, 1)), 3: ((0, 1, 0), (1, 1, 1))}
    y_free = {0: (0, 1, 1), 1: (1, 0, 1), 2: (1, 1, 0), 3: (0, 0, 0)}
    y_dep = {0: (0, 1, 0), 1: (1, 0, 0), 2: (1, 1, 1), 3: (0, 0, 1)}

    def r1y_opp(r, o, i):
        d, k, j = y_opp[o][i]
        return rdma(
            py.at[r, half_y(k, j)], R["r1yo"].at[r], R["ssr1"].at[r, 1], R["rsr1y"].at[r, 0],
            dev(x, yo(1 - 2 * d), z, c),
        )

    def r1y_next(r, o, dep):
        d, k, j = (y_dep if dep else y_free)[o]
        side = 0 if o >= 2 else 1
        return rdma(
            py.at[r, half_y(k, j)], R["r1yn"].at[r, side, pl.ds(j * 2, 2)], R["ssr1"].at[r, 1],
            R["rsr1y"].at[r, 1], dev(x, yo(1 - 2 * d), z, c),
        )

    def opp_x(r):
        for d in range(2):
            r1x_opp(r, d).start()

    def free_x(r):
        for d in range(2):
            r1x_free(r, d).start()

    def opp_y(r):
        for o in (2, 3):
            @pl.when(role == o)
            def _():
                for i in range(2):
                    r1y_opp(r, o, i).start()

    def free_y(r):
        for o in range(4):
            @pl.when(role == o)
            def _():
                r1y_next(r, o, 0).start()

    r1o, r1yo, r1n, r1yn = (R[n] for n in ("r1o", "r1yo", "r1n", "r1yn"))

    def dep_x(r):
        for d in range(2):
            arrived(r1o.at[r, d], R["rsr1x"].at[r, d])
            to = xo(1 - 2 * d) * 2 + d

            @pl.loop(0, 8, unroll=2)
            def _(i):
                px[r, to, i] = (px[r, to, i].astype(F32) + r1o[r, d, i].astype(F32)).astype(BF16)

            r1x_dep(r, d).start()
    def dep_y(r):
        arrived(r1yo.at[r], R["rsr1y"].at[r, 0])
        for o in range(4):
            @pl.when(role == o)
            def _():
                _d, k, j = y_dep[o]

                @pl.loop(0, 8)
                def _(i):
                    for xx in range(2):
                        at = k * 4 + j * 2 + xx
                        py[r, at, i] = (py[r, at, i].astype(F32) + r1yo[r, xx, i].astype(F32)).astype(BF16)

                r1y_next(r, o, 1).start()

    sx, sy, r2x, r2y, tx, ty = (R[n] for n in ("sx", "sy", "r2x", "r2y", "tx", "ty"))

    def r2x_to(r, k):
        return rdma(
            sx.at[r, k], r2x.at[r, y], R["ssr2"].at[r, 0], R["rsr2x"].at[r], dev(x, 2 * c + k, z, c)
        )

    def r2y_to(r, d):
        return rdma(
            sy.at[r, xo(d)], r2y.at[r, x], R["ssr2"].at[r, 1], R["rsr2y"].at[r], dev(xo(d), y, z, c)
        )

    def rs2x(r):
        arrived(r1n.at[r], R["rsr1x"].at[r, 2])

        @pl.loop(0, 8)
        def _(b):
            for k in range(2):
                sx[r, k, b] = (
                    px[r, x * 2 + k, b].astype(F32) + r1n[r, 0, k, b].astype(F32) + r1n[r, 1, k, b].astype(F32)
                ).astype(BF16)

        for k in range(2):
            @pl.when(role != k)
            def _():
                r2x_to(r, k).start()

    def rs2y(r):
        @pl.when(home)
        def _():
            arrived(r1yn.at[r], R["rsr1y"].at[r, 1])

            @pl.loop(0, 8)
            def _(b):
                for k in range(4):
                    sy[r, k, b] = (
                        py[r, yp * 4 + k, b].astype(F32) + r1yn[r, 0, k, b].astype(F32) + r1yn[r, 1, k, b].astype(F32)
                    ).astype(BF16)

            for d in (2, 1, 3):
                r2y_to(r, d).start()

    def r3_to(r, route, d):
        t, dst = ((tx, R["r3x"]), (ty, R["r3y"]))[route]
        zz = zo(d)
        return rdma(
            t.at[r, zind(zz)], dst.at[zi], R["ssr3"].at[r, route], R["rsr3"].at[route], dev(x, y, zz, r)
        )

    def r3_all(r, route, act):
        for d in (4, 3, 5, 2, 6, 1, 7):
            act(r3_to(r, route, d))

        @pl.when(c != r)
        def _():
            act(r3_to(r, route, 0))

    def r3_own(r, route):
        t, dst = ((tx, R["r3x"]), (ty, R["r3y"]))[route]

        @pl.when(c == r)
        def _():
            pltpu.make_async_copy(t.at[r, zi], dst.at[zi], R["rsr3"].at[route]).start()

    def rs3x(r):
        @pl.when(home)
        def _():
            arrived(r2x.at[r, pl.ds(0, 3)], R["rsr2x"].at[r])

            @pl.loop(0, 8, unroll=2)
            def _(b):
                v = sx[r, yp, b].astype(F32)
                for d in range(1, 4):
                    v += r2x[r, yo(d), b].astype(F32)
                tx[r, b] = v.astype(BF16)

            r3_all(r, 0, begin)
            r3_own(r, 0)

    def rs3y(r):
        @pl.when(home)
        def _():
            arrived(r2y.at[r, pl.ds(0, 3)], R["rsr2y"].at[r])

            @pl.loop(0, 8, unroll=2)
            def _(b):
                v = sy[r, x, b].astype(F32)
                for d in range(1, 4):
                    v += r2y[r, xo(d), b].astype(F32)
                ty[r, b] = v.astype(BF16)

            r3_all(r, 1, begin)
            r3_own(r, 1)

    def finish(route):
        src, n, o = ((R["r3x"], XW, XO), (R["r3y"], YW, YO))[route]
        arrived(src, R["rsr3"].at[route])
        total = src[0].astype(F32)
        for b in range(1, 8):
            total += src[b].astype(F32)
        R["gv_v"][:, o : o + n] = total

    def finish_z():
        arrived(R["rzx"], R["rsrz3"].at[0])
        total = R["rzx"][0].astype(F32)
        for b in range(1, 4):
            total += R["rzx"][b].astype(F32)
        R["gv_v"][:, :ZW] = total

    outs = [
        pltpu.make_async_copy(R["att_v"], att_o.at[0], R["osem"].at[0]),
        pltpu.make_async_copy(R["dq_v"], dq_o.at[0], R["osem"].at[1]),
        pltpu.make_async_copy(R["gv_v"], gv_o, R["osem"].at[2]),
    ]

    key_grads(0)
    swap2(0).start()
    key_grads(1)
    swap2(1).start()
    both(0)
    back(0, 1)
    opp_x(0)
    free_x(0)
    back(0, 0)
    for d in range(2):
        rz(0, d, 0).start()
    back(0, 2)
    opp_y(0)
    free_y(0)
    both(1)
    back(1, 1)
    opp_x(1)
    back(1, 2)
    opp_y(1)
    back(1, 0)
    for d in range(2):
        rz(1, d, 0).start()
    dep_x(0)
    free_x(1)
    dep_y(0)
    free_y(1)
    rzstep(0, 1)
    rzstep(1, 1)
    heads_out(0, 4)
    dep_x(1)
    dep_y(1)
    rzstep(0, 2)
    rzstep(1, 2)
    heads_out(4, 8)
    for cp in outs[:2]:
        cp.start()
    rs2x(0)
    rs2y(0)
    rzstep(0, 3)
    rzstep(1, 3)
    rs2x(1)
    rs2y(1)
    rs3x(0)
    rs3y(0)
    rz_sum(0)
    rz_sum(1)
    rs3x(1)
    rs3y(1)
    rz_rows(0)
    rz_rows(1)
    finish_z()
    finish(0)
    finish(1)
    outs[2].start()

    by_home(
        lambda: sent(gz.at[0, 0, 0, pl.ds(0, 3)], R["ssz1"].at[0]),
        lambda: sent(gz.at[0, 0, 0], R["ssz1"].at[0]),
    )
    for i, ref in enumerate((gx, gy)):
        by_home(
            lambda: sent(ref.at[0, 0, pl.ds(0, 7)], R["ss1"].at[i]),
            lambda: sent(ref.at[0, 0], R["ss1"].at[i]),
        )
    for r in range(2):
        sent(gz.at[r, pl.ds(0, 7)], R["ssz3"].at[r])
        sent(pz.at[r, pl.ds(0, 7)], R["ssrz1"].at[r])
        sent(gx.at[r, pl.ds(0, 6)], R["ss3"].at[r, 0])
        sent(px.at[r, pl.ds(0, 6)], R["ssr1"].at[r, 0])

        @pl.when(home)
        def _():
            sent(R["rzy"].at[r, pl.ds(0, 3)], R["ssz2"].at[r])
            sent(gx.at[r, pl.ds(0, 3)], R["ss2"].at[r, 0])
            sent(gy.at[r, pl.ds(0, 3)], R["ss2"].at[r, 1])
            sent(sy.at[r, pl.ds(0, 3)], R["ssr2"].at[r, 1])
            sent(gy.at[:, pl.ds(0, 5)], R["ss3"].at[r, 1])

            @pl.when(c == r)
            def _():
                sent(tx.at[r, pl.ds(0, 7)], R["ssr3"].at[r, 0])
                sent(ty.at[r, pl.ds(0, 7)], R["ssr3"].at[r, 1])
                sent(R["tz"].at[r, pl.ds(0, 3)], R["ssrz3"].at[r])

            @pl.when(c != r)
            def _():
                sent(tx.at[r], R["ssr3"].at[r, 0])
                sent(ty.at[r], R["ssr3"].at[r, 1])
                sent(R["tz"].at[r], R["ssrz3"].at[r])

        by_home(
            lambda: sent(py.at[r, pl.ds(0, 4)], R["ssr1"].at[r, 1]),
            lambda: sent(py.at[r], R["ssr1"].at[r, 1]),
        )
        by_home(
            lambda: sent(sx.at[r, 0], R["ssr2"].at[r, 0]),
            lambda: sent(sx.at[r], R["ssr2"].at[r, 0]),
        )
        by_home(
            lambda: sent(pz.at[r, 0, 0], R["ssrz2"].at[r]),
            lambda: sent(pz.at[r, 0], R["ssrz2"].at[r]),
        )

        @pl.when(c == 1 - h)
        def _():
            sent(gy.at[r, pl.ds(0, 2)], R["ss3"].at[r, 1])

    for cp in outs:
        cp.wait()


def copy_out(a, b, d, ao, bo, do, av, bv, dv, sems):
    moves = ((a, av, ao), (b, bv, bo), (d, dv, do))
    loads = [pltpu.make_async_copy(s, v, sems.at[0, i]) for i, (s, v, _) in enumerate(moves)]
    stores = [pltpu.make_async_copy(v, t, sems.at[1, i]) for i, (_, v, t) in enumerate(moves)]
    for cp in loads:
        cp.start()
    for load, store in zip(loads, stores):
        load.wait()
        store.start()
    for cp in stores:
        cp.wait()


def on_device(queries, grad_attended, vision, key_weight, value_weight, tile_limit):
    vmem = pl.BlockSpec(memory_space=pltpu.VMEM)
    hbm = pl.BlockSpec(memory_space=pl.ANY)
    shapes = (
        jax.ShapeDtypeStruct(queries.shape, BF16),
        jax.ShapeDtypeStruct(queries.shape, BF16),
        jax.ShapeDtypeStruct(vision.shape, F32),
    )
    outs = pl.pallas_call(
        kernel,
        out_shape=shapes,
        in_specs=[hbm, hbm, hbm, hbm, hbm, vmem],
        out_specs=(hbm, hbm, hbm),
        scratch_shapes=list(scratch().values()),
        compiler_params=pltpu.CompilerParams(
            collective_id=0, has_side_effects=True, vmem_limit_bytes=60 * 2**20
        ),
        cost_estimate=pl.CostEstimate(flops=6_000_000_000, bytes_accessed=6_000_000, transcendentals=1_000_000),
    )(vision, key_weight, value_weight, queries, grad_attended, tile_limit)
    return pl.pallas_call(
        copy_out,
        out_shape=shapes,
        in_specs=[hbm, hbm, hbm],
        out_specs=(hbm, hbm, hbm),
        scratch_shapes=[pltpu.VMEM(s.shape, s.dtype) for s in shapes] + [pltpu.SemaphoreType.DMA((2, 3))],
    )(*outs)


def solution(mesh):
    return jax.shard_map(
        on_device,
        mesh=mesh,
        in_specs=(
            P("segment", None, "tensor"),
            P("segment", None, "tensor"),
            P("segment", "tensor"),
            P("segment", None, "tensor"),
            P("segment", None, "tensor"),
            P(),
        ),
        out_specs=(
            P("segment", None, "tensor"),
            P("segment", None, "tensor"),
            P("segment", "tensor"),
        ),
        check_vma=False,
    )
```

```python
import jax
import jax.numpy as jnp
from jax import lax
from jax.experimental import pallas as pl
from jax.experimental.pallas import tpu as pltpu
from jax.sharding import PartitionSpec as P

HD = 128
EPS = 1e-05
SCALE = HD ** (-0.5)
LOG2E = 1.4426950408889634
F32 = jnp.float32
BF16 = jnp.bfloat16
MESH = pl.DeviceIdType.MESH

ZW, XW, YW = 256, 384, 384
XO, YO = ZW, ZW + XW


def scratch():
    v, dma = pltpu.VMEM, pltpu.SemaphoreType.DMA
    s = {
        "vis": v((16, 1024), BF16),
        "q": v((8, 256, 128), BF16), "do": v((8, 256, 128), BF16),
        "w": v((4096, 256), BF16), "wt": v((256, 4096), BF16),
        "qt": v((8, 128, 256), BF16), "dot": v((8, 128, 256), BF16),
        "bias": v((4, 16, 256), F32),
        "part": v((512, 256), F32), "part_in": v((512, 256), F32),
        "kv": v((2, 512, 128), BF16), "kvt": v((2, 128, 512), BF16),
        "probs": v((512, 2048), BF16), "dsc": v((512, 2048), BF16), "at": v((8, 128, 256), BF16),
        "dkv": v((512, 256), BF16), "dkv_in": v((512, 256), BF16),
        "att_v": v((256, 1024), BF16), "dq_v": v((256, 1024), BF16), "gv_v": v((16, 1024), F32),
        "gz": v((2, 8, 2, 4, 16, ZW), BF16), "pz": v((2, 8, 2, 4, 16, ZW), BF16),
        "rz1": v((2, 2, 4, 2, 4, 16, ZW), BF16), "rzy": v((2, 4, 4, 16, ZW), BF16),
        "tz": v((2, 4, 16, ZW), BF16), "rzx": v((4, 16, ZW), BF16),
        "gx": v((2, 8, 8, 16, XW), BF16), "gy": v((2, 8, 8, 16, YW), BF16),
        "px": v((2, 8, 8, 16, XW), BF16), "py": v((2, 8, 8, 16, YW), BF16),
        "r1o": v((2, 2, 8, 16, XW), BF16), "r1n": v((2, 2, 2, 8, 16, XW), BF16),
        "r1yo": v((2, 2, 8, 16, YW), BF16), "r1yn": v((2, 2, 4, 8, 16, YW), BF16),
        "sx": v((2, 2, 8, 16, XW), BF16), "sy": v((2, 4, 8, 16, YW), BF16),
        "r2x": v((2, 4, 8, 16, XW), BF16), "r2y": v((2, 4, 8, 16, YW), BF16),
        "tx": v((2, 8, 16, XW), BF16), "ty": v((2, 8, 16, YW), BF16),
        "r3x": v((8, 16, XW), BF16), "r3y": v((8, 16, YW), BF16),
        "lsem": dma((5,)), "osem": dma((3,)), "ss4": dma((4,)), "rs4": dma((4,)),
        "ssz1": dma((1,)), "ss1": dma((2,)), "ssz2": dma((2,)), "ss2": dma((2, 2)), "ss3": dma((2, 2)),
        "ssz3": dma((2,)), "ssrz1": dma((2,)), "ssr1": dma((2, 2)), "ssr2": dma((2, 2)), "ssr3": dma((2, 2)),
        "ssrz2": dma((2,)), "ssrz3": dma((2,)),
        "rsz1": dma((2,)), "rs1": dma((2, 2)), "rsz2": dma((2,)), "rs2x": dma((2,)), "rs2y": dma((2,)),
        "rs3x": dma((2, 3)), "rs3y": dma((2, 2)), "rsz3": dma((2, 7)),
        "rsrz1": dma((2, 7)), "rsr1x": dma((2, 3)), "rsr1y": dma((2, 2)), "rsr2x": dma((2,)), "rsr2y": dma((2,)),
        "rsr3": dma((2,)), "rsrz2": dma((2,)), "rsrz3": dma((1,)),
    }
    return s


NAMES = tuple(scratch())


def mm(a, b):
    return jnp.dot(a, b, preferred_element_type=F32)


def kernel(vis_in, wk, wv, q_in, do_in, lim, att_o, dq_o, gv_o, *rest):
    R = dict(zip(NAMES, rest, strict=True))
    vis, q, do, w, wt = R["vis"], R["q"], R["do"], R["w"], R["wt"]
    gx, gy, gz, px, py, pz = (R[n] for n in ("gx", "gy", "gz", "px", "py", "pz"))

    seg, ten = lax.axis_index("segment"), lax.axis_index("tensor")
    zh, x, c = lax.div(seg, 8), lax.rem(lax.div(seg, 2), 4), lax.rem(seg, 2)
    y, zl = lax.div(ten, 2), lax.rem(ten, 2)
    z = zh * 2 + zl
    zi = zl * 4 + zh
    h, yp = lax.div(y, 2), lax.rem(y, 2)
    role = lax.rem(y + 4 - 2 * c, 4)
    home = c == h

    def dev(xx, yy, zz, cc):
        return (lax.div(zz, 2) * 8 + xx * 2 + cc, yy * 2 + lax.rem(zz, 2))

    def zind(zz):
        return lax.rem(zz, 2) * 4 + lax.div(zz, 2)

    def xo(d):
        return lax.rem(x + d + 4, 4)

    def yo(d):
        return lax.rem(y + d + 4, 4)

    def zo(d):
        return lax.rem(z + d + 8, 8)

    partner = dev(x, y, z, 1 - c)

    def rdma(src, dst, ss, rs, to):
        return pltpu.make_async_remote_copy(
            src_ref=src, dst_ref=dst, send_sem=ss, recv_sem=rs, device_id=to, device_id_type=MESH
        )

    def arrived(dst, rs):
        rdma(dst, dst, R["ss4"].at[0], rs, partner).wait_recv()

    def begin(cp):
        cp.start()

    def sent(ref, ss):
        rdma(ref, ref, ss, R["rs4"].at[0], partner).wait_send()

    lsem = R["lsem"]
    wcopies = [
        pltpu.make_async_copy(wk.at[0], w.at[:, pl.ds(0, HD)], lsem.at[0]),
        pltpu.make_async_copy(wv.at[0], w.at[:, pl.ds(HD, HD)], lsem.at[1]),
    ]

    barrier = pltpu.get_barrier_semaphore()
    greet = [dev(x, y, zo(d), cc) for d in range(1, 8) for cc in (0, 1)]
    greet += [dev(xo(d), y, z, cc) for d in range(1, 4) for cc in (0, 1)]
    greet += [dev(x, yo(d), z, c) for d in range(1, 4)] + [partner]
    shard = pltpu.make_async_copy(vis_in, vis, lsem.at[4])
    shard.start()
    for other in greet:
        pl.semaphore_signal(barrier, inc=1, device_id=other, device_id_type=MESH)
    for cp in wcopies:
        cp.start()
    loads = [
        pltpu.make_async_copy(q_in.at[0], R["att_v"], lsem.at[2]),
        pltpu.make_async_copy(do_in.at[0], R["dq_v"], lsem.at[3]),
    ]
    for cp in loads:
        cp.start()
    shard.wait()
    pl.semaphore_wait(barrier, len(greet))

    def z1(d):
        return rdma(vis.at[:, pl.ds(0, ZW)], gz.at[c, zi, yp, x], R["ssz1"].at[0], R["rsz1"].at[c], dev(xo(d), y, z, h))

    def z1_all(act):
        for d in (2, 1, 3):
            act(z1(d))

        @pl.when(c == 1 - h)
        def _():
            act(z1(0))

    def g1(route, d):
        src, dst = (
            (vis.at[:, pl.ds(XO, XW)], gx.at[c, x * 2 + yp, zi]),
            (vis.at[:, pl.ds(YO, YW)], gy.at[c, yp * 4 + x, zi]),
        )[route]
        return rdma(src, dst, R["ss1"].at[route], R["rs1"].at[c, route], dev(x, y, zo(d), h))

    def g1_all(route, act):
        for d in (4, 3, 5, 2, 6, 1, 7):
            act(g1(route, d))

        @pl.when(c == 1 - h)
        def _():
            act(g1(route, 0))

    z1_all(begin)
    for route in range(2):
        g1_all(route, begin)

    @pl.when(home)
    def _():
        pltpu.make_async_copy(vis.at[:, pl.ds(0, ZW)], gz.at[c, zi, yp, x], R["rsz1"].at[c]).start()
        pltpu.make_async_copy(vis.at[:, pl.ds(XO, XW)], gx.at[c, x * 2 + yp, zi], R["rs1"].at[c, 0]).start()
        pltpu.make_async_copy(vis.at[:, pl.ds(YO, YW)], gy.at[c, yp * 4 + x, zi], R["rs1"].at[c, 1]).start()

    for cp in loads:
        cp.wait()
    qt, dot_, bias = R["qt"], R["dot"], R["bias"]

    @pl.loop(0, 8)
    def _(n):
        lanes = pl.ds(pl.multiple_of(n * HD, HD), HD)
        qn = R["att_v"][:, lanes]
        dn = R["dq_v"][:, lanes]
        q[n] = qn
        do[n] = dn
        qt[n] = qn.astype(F32).T.astype(BF16)
        dot_[n] = dn.astype(F32).T.astype(BF16)

    def z2(r, d):
        blk = gz.at[r, zi, yp]
        return rdma(blk, blk, R["ssz2"].at[r], R["rsz2"].at[r], dev(x, yo(d), z, c))

    @pl.when(home)
    def _():
        for r in range(2):
            arrived(gz.at[r, zi, yp], R["rsz1"].at[r])
            for d in (2, 1, 3):
                z2(r, d).start()

    def g2x(r, d):
        blk = gx.at[r, x * 2 + yp]
        return rdma(blk, blk, R["ss2"].at[r, 0], R["rs2x"].at[r], dev(x, yo(d), z, c))

    def g2y(r, d):
        blk = gy.at[r, yp * 4 + x]
        return rdma(blk, blk, R["ss2"].at[r, 1], R["rs2y"].at[r], dev(xo(d), y, z, c))

    def step2x(r):
        @pl.when(home)
        def _():
            arrived(gx.at[r, x * 2 + yp], R["rs1"].at[r, 0])
            for d in (2, 1, 3):
                g2x(r, d).start()

    def step2y(r):
        @pl.when(home)
        def _():
            arrived(gy.at[r, yp * 4 + x], R["rs1"].at[r, 1])
            for d in (2, 1, 3):
                g2y(r, d).start()

    def by_home(few, many):
        @pl.when(home)
        def _():
            few()

        @pl.when(c == 1 - h)
        def _():
            many()

    def z3(r, d, s):
        side = 1 - 2 * d
        at = zind(zo(-side * s))
        blk = gz.at[r, at] if s < 3 else gz.at[r, at, d]
        return rdma(blk, blk, R["ssz3"].at[r], R["rsz3"].at[r, s * 2 + d if s < 3 else 6], dev(x, y, zo(side), c))

    def z3_arrived(r, d, s):
        arrived(gz.at[r, zind(zo(-(1 - 2 * d) * (s + 1)))], R["rsz3"].at[r, s * 2 + d])

    def z3_last(r):
        arrived(gz.at[r, zind(zo(4))], R["rsz3"].at[r, 6])

    def zstep(r, s):
        if s == 0:
            by_home(
                lambda: arrived(gz.at[r, zi, 1 - yp], R["rsz2"].at[r]),
                lambda: arrived(gz.at[r, zi], R["rsz2"].at[r]),
            )
        for d in range(2):
            if s > 0:
                z3_arrived(r, d, s - 1)
            z3(r, d, s).start()

    def g3x(r, d, half):
        blk = gx.at[r, x * 2 + half]
        return rdma(blk, blk, R["ss3"].at[r, 0], R["rs3x"].at[r, d if half == d else 2], dev(xo(1 - 2 * d), y, z, c))

    def g3xf(r, d):
        blk = gx.at[r, xo(2 * d - 1) * 2 + d]
        return rdma(blk, blk, R["ss3"].at[r, 0], R["rs3x"].at[r, 2], dev(xo(1 - 2 * d), y, z, c))

    def half_y(k, j):
        return pl.ds(k * 4 + j * 2, 2)

    passed = ((1, 0, 1), (0, 0, 0), (1, 1, 0), (0, 1, 1))

    def g3y(r, o, k, j, d):
        blk = gy.at[r, half_y(k, j)]
        first = passed[(o + 1 - 2 * d) % 4][:2] == (k, j)
        return rdma(blk, blk, R["ss3"].at[r, 1], R["rs3y"].at[r, 0 if first else 1], dev(x, yo(1 - 2 * d), z, c))

    def g3y_role(r, o):
        order = ((0, 0, 0), (0, 1, 1), (0, 1, 0), (0, 0, 1)) if o == 0 else ((1, 0, 1), (1, 1, 0), (1, 1, 1), (1, 0, 0))
        return [g3y(r, o, k, j, d) for k, j, d in order]

    def g3yf(r, o):
        k, j, d = passed[o]
        return g3y(r, o, k, j, d)

    def step3x(r):
        by_home(
            lambda: arrived(gx.at[r, x * 2 + 1 - yp], R["rs2x"].at[r]),
            lambda: arrived(gx.at[r, pl.ds(x * 2, 2)], R["rs2x"].at[r]),
        )
        for d, half in ((0, 0), (1, 1), (0, 1), (1, 0)):
            g3x(r, d, half).start()

    def step3y(r):
        for o in (0, 1):
            @pl.when(role == o)
            def _():
                arrived(gy.at[r, pl.ds(o * 4, 3)], R["rs2y"].at[r])
                for cp in g3y_role(r, o):
                    cp.start()

    def forward3x(r):
        for d in range(2):
            arrived(gx.at[r, xo(2 * d - 1) * 2 + d], R["rs3x"].at[r, d])
            g3xf(r, d).start()

    def forward3y(r):
        for o in range(4):
            @pl.when(role == o)
            def _():
                arrived(gy.at[r, half_y(*passed[o][:2])], R["rs3y"].at[r, 0])
                g3yf(r, o).start()

    def rest3x(r):
        arrived(gx.at[r, pl.ds(0, 4)], R["rs3x"].at[r, 2])

    def rest3y(r):
        by_home(
            lambda: arrived(gy.at[r, pl.ds(0, 2)], R["rs3y"].at[r, 1]),
            lambda: arrived(gy.at[r, pl.ds(0, 6)], R["rs3y"].at[r, 1]),
        )

    part, part_in = R["part"], R["part_in"]
    ROWS = (slice(0, 256), slice(256, 512))

    def project(r, route):
        total = part[ROWS[r], :] if route != (1, 0)[r] else jnp.zeros((256, 256), F32)
        for k in range(2):
            for l in range(2):
                base = (k * 2 + l) * 1024
                zs = slice(l * 4, l * 4 + 4)
                if route == 0:
                    a = jnp.concatenate([gz[r, zs, k, xx].reshape(64, ZW) for xx in range(4)], axis=0)
                    total += mm(a, w[base : base + ZW, :])
                elif route == 1:
                    a = jnp.concatenate([gx[r, xx * 2 + k, zs].reshape(64, XW) for xx in range(4)], axis=0)
                    total += mm(a, w[base + XO : base + XO + XW, :])
                else:
                    a = gy[r, k * 4 : k * 4 + 4, zs].reshape(256, YW)
                    total += mm(a, w[base + YO : base + YO + YW, :])
        part[ROWS[r], :] = total

    def swap(r):
        rows = pl.ds(r * 256, 256)
        return rdma(part.at[rows], part_in.at[rows], R["ss4"].at[r], R["rs4"].at[r], partner)

    kv, kvt = R["kv"], R["kvt"]

    def keys_values(r):
        rows = ROWS[r]
        pre = part[rows, :] + part_in[rows, :]
        part_in[rows, :] = pre
        kp = pre[:, :HD]
        inv = lax.rsqrt(jnp.mean(kp * kp, axis=-1, keepdims=True) + EPS)
        keys = (kp * inv).astype(BF16)
        vals = pre[:, HD:].astype(BF16)
        kv[0, rows] = keys
        kv[1, rows] = vals
        kvt[0, :, rows] = keys.astype(F32).T.astype(BF16)
        kvt[1, :, rows] = vals.astype(F32).T.astype(BF16)

    def transpose_weights(lo, hi):
        @pl.loop(lo, hi)
        def _(n):
            rows = pl.ds(pl.multiple_of(n * 256, 256), 256)
            wt[:, rows] = w[rows, :].astype(F32).T.astype(BF16)

    step2x(0)
    step2x(1)
    step2y(0)
    step2y(1)
    zstep(0, 0)
    zstep(1, 0)
    for cp in wcopies:
        cp.wait()
    step3x(0)
    step3y(0)
    step3x(1)
    step3y(1)
    transpose_weights(0, 8)
    zstep(0, 1)
    zstep(1, 1)
    transpose_weights(8, 16)
    limits = lim[...].reshape(1, 512)
    limit = (1 - c) * limits[:, :256] + c * limits[:, 256:]
    for t in range(4):
        bias[t] = jnp.broadcast_to(jnp.where(t < limit, 0.0, -1e30), (16, 256))
    forward3x(0)
    forward3y(0)
    zstep(0, 2)
    zstep(1, 2)
    forward3x(1)
    forward3y(1)
    zstep(0, 3)
    zstep(1, 3)
    rest3x(0)
    project(0, 1)
    rest3y(0)
    project(0, 2)
    z3_last(0)
    project(0, 0)
    swap(0).start()
    z3_last(1)
    project(1, 0)
    swap(0).wait()
    keys_values(0)
    rest3x(1)
    project(1, 1)
    rest3y(1)
    project(1, 2)
    swap(1).start()
    swap(1).wait()
    keys_values(1)

    probs, dsc, at_ = R["probs"], R["dsc"], R["at"]

    @pl.loop(0, 8, unroll=8)
    def _(n):
        lanes = pl.ds(pl.multiple_of(n * 256, 256), 256)
        dotn = dot_[n]
        s = mm(kv[0], qt[n]) * (SCALE * LOG2E)
        s = (s.reshape(8, 4, 16, 256) + bias[...][None]).reshape(512, 256)
        m = jnp.max(s, axis=0, keepdims=True)
        e = jnp.exp2(s - m)
        prob = e * (1.0 / jnp.sum(e, axis=0, keepdims=True))
        pb16 = prob.astype(BF16)
        probs[:, lanes] = pb16
        at = mm(kvt[1], pb16).astype(BF16)
        at_[n] = at
        dp = mm(kv[1], dotn)
        delta = jnp.sum(at.astype(F32) * dotn.astype(F32), axis=0, keepdims=True)
        dsc[:, lanes] = (prob * (dp - delta)).astype(BF16)

    dkv, dkv_in = R["dkv"], R["dkv_in"]

    def key_grads(r):
        rows = ROWS[r]
        kp = part_in[rows, :HD]
        inv = lax.rsqrt(jnp.mean(kp * kp, axis=-1, keepdims=True) + EPS)
        dk = mm(dsc[rows, :], q[...].reshape(2048, HD)) * SCALE
        dv = mm(probs[rows, :], do[...].reshape(2048, HD))
        dkp = inv * dk - kp * (inv * inv * inv * jnp.mean(kp * dk, axis=-1, keepdims=True))
        dkv[rows, :HD] = dkp.astype(BF16)
        dkv[rows, HD:] = dv.astype(BF16)

    def swap2(r):
        rows = pl.ds(r * 256, 256)
        return rdma(dkv.at[rows], dkv_in.at[rows], R["ss4"].at[2 + r], R["rs4"].at[2 + r], partner)

    def heads_out(lo, hi):
        @pl.loop(lo, hi, unroll=2)
        def _(n):
            lanes = pl.ds(pl.multiple_of(n * HD, HD), HD)
            dqt = mm(kvt[0], dsc[:, pl.ds(pl.multiple_of(n * 256, 256), 256)]) * SCALE
            R["dq_v"][:, lanes] = dqt.T.astype(BF16)
            R["att_v"][:, lanes] = at_[n].astype(F32).T.astype(BF16)

    def both(r):
        swap2(r).wait()
        rows = ROWS[r]
        dkv[rows, :] = (dkv[rows, :].astype(F32) + dkv_in[rows, :].astype(F32)).astype(BF16)

    def back(r, route):
        for k in range(2):
            for l in range(2):
                base = (k * 2 + l) * 1024 + (0, XO, YO)[route]
                n = (ZW, XW, YW)[route]
                zs = slice(l * 4, l * 4 + 4)
                wtb = wt[:, base : base + n]
                v = mm(dkv[ROWS[r], :], wtb).astype(BF16)
                if route == 2:
                    py[r, k * 4 : k * 4 + 4, zs] = v.reshape(4, 4, 16, YW)
                    continue
                for xx in range(4):
                    b = v[xx * 64 : (xx + 1) * 64].reshape(4, 16, n)
                    if route == 0:
                        pz[r, zs, k, xx] = b
                    else:
                        px[r, xx * 2 + k, zs] = b

    rz1 = R["rz1"]

    def rz(r, d, s):
        side = 1 - 2 * d
        at = zind(zo(side * (4 - s)))
        src = pz.at[r, at, d] if s == 0 else pz.at[r, at]
        dst = rz1.at[r, d, 0, d] if s == 0 else rz1.at[r, d, s]
        return rdma(src, dst, R["ssrz1"].at[r], R["rsrz1"].at[r, s * 2 + d if s < 3 else 6], dev(x, y, zo(side), c))

    def rz_arrived(r, d, s):
        arrived(rz1.at[r, d, 0, d] if s == 0 else rz1.at[r, d, s], R["rsrz1"].at[r, s * 2 + d])

    def rzstep(r, s):
        for d in range(2):
            if s > 0:
                rz_arrived(r, d, s - 1)
                at = zind(zo((1 - 2 * d) * (4 - s)))
                if s == 1:
                    pz[r, at, d] = (pz[r, at, d].astype(F32) + rz1[r, d, 0, d].astype(F32)).astype(BF16)
                else:
                    pz[r, at] = (pz[r, at].astype(F32) + rz1[r, d, s - 1].astype(F32)).astype(BF16)
            rz(r, d, s).start()

    def rzy_to(r, k):
        return rdma(
            pz.at[r, zi, k], R["rzy"].at[r, y], R["ssrz2"].at[r], R["rsrz2"].at[r], dev(x, 2 * c + k, z, c)
        )

    def rz_sum(r):
        arrived(rz1.at[r, 0, pl.ds(2, 2)], R["rsrz1"].at[r, 6])
        pz[r, zi] = (pz[r, zi].astype(F32) + rz1[r, 0, 3].astype(F32) + rz1[r, 1, 3].astype(F32)).astype(BF16)
        for k in range(2):
            @pl.when(role != k)
            def _():
                rzy_to(r, k).start()

    def rzx_to(r, d):
        return rdma(
            R["tz"].at[r, xo(d)], R["rzx"].at[x], R["ssrz3"].at[r], R["rsrz3"].at[0], dev(xo(d), y, z, r)
        )

    def rzx_all(r, act):
        for d in (2, 1, 3):
            act(rzx_to(r, d))

        @pl.when(c != r)
        def _():
            act(rzx_to(r, 0))

    def rz_rows(r):
        @pl.when(home)
        def _():
            arrived(R["rzy"].at[r, pl.ds(0, 3)], R["rsrz2"].at[r])
            v = pz[r, zi, yp].astype(F32)
            for d in range(1, 4):
                v += R["rzy"][r, yo(d)].astype(F32)
            R["tz"][r] = v.astype(BF16)
            rzx_all(r, begin)

            @pl.when(c == r)
            def _():
                pltpu.make_async_copy(R["tz"].at[r, x], R["rzx"].at[x], R["rsrz3"].at[0]).start()

    def r1x_opp(r, d):
        return rdma(
            px.at[r, xo(2) * 2 + d], R["r1o"].at[r, d], R["ssr1"].at[r, 0], R["rsr1x"].at[r, d],
            dev(xo(1 - 2 * d), y, z, c),
        )

    def r1x_free(r, d):
        return rdma(
            px.at[r, xo(1 - 2 * d) * 2 + 1 - d], R["r1n"].at[r, d, 1 - d], R["ssr1"].at[r, 0],
            R["rsr1x"].at[r, 2], dev(xo(1 - 2 * d), y, z, c),
        )

    def r1x_dep(r, d):
        return rdma(
            px.at[r, xo(1 - 2 * d) * 2 + d], R["r1n"].at[r, d, d], R["ssr1"].at[r, 0],
            R["rsr1x"].at[r, 2], dev(xo(1 - 2 * d), y, z, c),
        )

    y_opp = {2: ((1, 0, 0), (0, 0, 1)), 3: ((0, 1, 0), (1, 1, 1))}
    y_free = {0: (0, 1, 1), 1: (1, 0, 1), 2: (1, 1, 0), 3: (0, 0, 0)}
    y_dep = {0: (0, 1, 0), 1: (1, 0, 0), 2: (1, 1, 1), 3: (0, 0, 1)}

    def r1y_opp(r, o, i):
        d, k, j = y_opp[o][i]
        return rdma(
            py.at[r, half_y(k, j)], R["r1yo"].at[r], R["ssr1"].at[r, 1], R["rsr1y"].at[r, 0],
            dev(x, yo(1 - 2 * d), z, c),
        )

    def r1y_next(r, o, dep):
        d, k, j = (y_dep if dep else y_free)[o]
        side = 0 if o >= 2 else 1
        return rdma(
            py.at[r, half_y(k, j)], R["r1yn"].at[r, side, pl.ds(j * 2, 2)], R["ssr1"].at[r, 1],
            R["rsr1y"].at[r, 1], dev(x, yo(1 - 2 * d), z, c),
        )

    def opp_x(r):
        for d in range(2):
            r1x_opp(r, d).start()

    def free_x(r):
        for d in range(2):
            r1x_free(r, d).start()

    def opp_y(r):
        for o in (2, 3):
            @pl.when(role == o)
            def _():
                for i in range(2):
                    r1y_opp(r, o, i).start()

    def free_y(r):
        for o in range(4):
            @pl.when(role == o)
            def _():
                r1y_next(r, o, 0).start()

    r1o, r1yo, r1n, r1yn = (R[n] for n in ("r1o", "r1yo", "r1n", "r1yn"))

    def dep_x(r):
        for d in range(2):
            arrived(r1o.at[r, d], R["rsr1x"].at[r, d])
            to = xo(1 - 2 * d) * 2 + d

            @pl.loop(0, 8, unroll=2)
            def _(i):
                px[r, to, i] = (px[r, to, i].astype(F32) + r1o[r, d, i].astype(F32)).astype(BF16)

            r1x_dep(r, d).start()
    def dep_y(r):
        arrived(r1yo.at[r], R["rsr1y"].at[r, 0])
        for o in range(4):
            @pl.when(role == o)
            def _():
                _d, k, j = y_dep[o]

                @pl.loop(0, 8)
                def _(i):
                    for xx in range(2):
                        at = k * 4 + j * 2 + xx
                        py[r, at, i] = (py[r, at, i].astype(F32) + r1yo[r, xx, i].astype(F32)).astype(BF16)

                r1y_next(r, o, 1).start()

    sx, sy, r2x, r2y, tx, ty = (R[n] for n in ("sx", "sy", "r2x", "r2y", "tx", "ty"))

    def r2x_to(r, k):
        return rdma(
            sx.at[r, k], r2x.at[r, y], R["ssr2"].at[r, 0], R["rsr2x"].at[r], dev(x, 2 * c + k, z, c)
        )

    def r2y_to(r, d):
        return rdma(
            sy.at[r, xo(d)], r2y.at[r, x], R["ssr2"].at[r, 1], R["rsr2y"].at[r], dev(xo(d), y, z, c)
        )

    def rs2x(r):
        arrived(r1n.at[r], R["rsr1x"].at[r, 2])

        @pl.loop(0, 8)
        def _(b):
            for k in range(2):
                sx[r, k, b] = (
                    px[r, x * 2 + k, b].astype(F32) + r1n[r, 0, k, b].astype(F32) + r1n[r, 1, k, b].astype(F32)
                ).astype(BF16)

        for k in range(2):
            @pl.when(role != k)
            def _():
                r2x_to(r, k).start()

    def rs2y(r):
        @pl.when(home)
        def _():
            arrived(r1yn.at[r], R["rsr1y"].at[r, 1])

            @pl.loop(0, 8)
            def _(b):
                for k in range(4):
                    sy[r, k, b] = (
                        py[r, yp * 4 + k, b].astype(F32) + r1yn[r, 0, k, b].astype(F32) + r1yn[r, 1, k, b].astype(F32)
                    ).astype(BF16)

            for d in (2, 1, 3):
                r2y_to(r, d).start()

    def r3_to(r, route, d):
        t, dst = ((tx, R["r3x"]), (ty, R["r3y"]))[route]
        zz = zo(d)
        return rdma(
            t.at[r, zind(zz)], dst.at[zi], R["ssr3"].at[r, route], R["rsr3"].at[route], dev(x, y, zz, r)
        )

    def r3_all(r, route, act):
        for d in (4, 3, 5, 2, 6, 1, 7):
            act(r3_to(r, route, d))

        @pl.when(c != r)
        def _():
            act(r3_to(r, route, 0))

    def r3_own(r, route):
        t, dst = ((tx, R["r3x"]), (ty, R["r3y"]))[route]

        @pl.when(c == r)
        def _():
            pltpu.make_async_copy(t.at[r, zi], dst.at[zi], R["rsr3"].at[route]).start()

    def rs3x(r):
        @pl.when(home)
        def _():
            arrived(r2x.at[r, pl.ds(0, 3)], R["rsr2x"].at[r])

            @pl.loop(0, 8, unroll=2)
            def _(b):
                v = sx[r, yp, b].astype(F32)
                for d in range(1, 4):
                    v += r2x[r, yo(d), b].astype(F32)
                tx[r, b] = v.astype(BF16)

            r3_all(r, 0, begin)
            r3_own(r, 0)

    def rs3y(r):
        @pl.when(home)
        def _():
            arrived(r2y.at[r, pl.ds(0, 3)], R["rsr2y"].at[r])

            @pl.loop(0, 8, unroll=2)
            def _(b):
                v = sy[r, x, b].astype(F32)
                for d in range(1, 4):
                    v += r2y[r, xo(d), b].astype(F32)
                ty[r, b] = v.astype(BF16)

            r3_all(r, 1, begin)
            r3_own(r, 1)

    def finish(route):
        src, n, o = ((R["r3x"], XW, XO), (R["r3y"], YW, YO))[route]
        arrived(src, R["rsr3"].at[route])
        total = src[0].astype(F32)
        for b in range(1, 8):
            total += src[b].astype(F32)
        R["gv_v"][:, o : o + n] = total

    def finish_z():
        arrived(R["rzx"], R["rsrz3"].at[0])
        total = R["rzx"][0].astype(F32)
        for b in range(1, 4):
            total += R["rzx"][b].astype(F32)
        R["gv_v"][:, :ZW] = total

    outs = [
        pltpu.make_async_copy(R["att_v"], att_o.at[0], R["osem"].at[0]),
        pltpu.make_async_copy(R["dq_v"], dq_o.at[0], R["osem"].at[1]),
        pltpu.make_async_copy(R["gv_v"], gv_o, R["osem"].at[2]),
    ]

    key_grads(0)
    swap2(0).start()
    key_grads(1)
    swap2(1).start()
    both(0)
    back(0, 1)
    opp_x(0)
    free_x(0)
    back(0, 2)
    opp_y(0)
    free_y(0)
    back(0, 0)
    for d in range(2):
        rz(0, d, 0).start()
    both(1)
    back(1, 1)
    opp_x(1)
    back(1, 2)
    opp_y(1)
    back(1, 0)
    for d in range(2):
        rz(1, d, 0).start()
    dep_x(0)
    free_x(1)
    dep_y(0)
    free_y(1)
    rzstep(0, 1)
    rzstep(1, 1)
    heads_out(0, 4)
    dep_x(1)
    dep_y(1)
    rzstep(0, 2)
    rzstep(1, 2)
    heads_out(4, 8)
    for cp in outs[:2]:
        cp.start()
    rs2x(0)
    rs2y(0)
    rzstep(0, 3)
    rzstep(1, 3)
    rs2x(1)
    rs2y(1)
    rs3x(0)
    rs3y(0)
    rz_sum(0)
    rz_sum(1)
    rs3x(1)
    rs3y(1)
    rz_rows(0)
    rz_rows(1)
    finish_z()
    finish(0)
    finish(1)
    outs[2].start()

    by_home(
        lambda: sent(gz.at[0, 0, 0, pl.ds(0, 3)], R["ssz1"].at[0]),
        lambda: sent(gz.at[0, 0, 0], R["ssz1"].at[0]),
    )
    for i, ref in enumerate((gx, gy)):
        by_home(
            lambda: sent(ref.at[0, 0, pl.ds(0, 7)], R["ss1"].at[i]),
            lambda: sent(ref.at[0, 0], R["ss1"].at[i]),
        )
    for r in range(2):
        sent(gz.at[r, pl.ds(0, 7)], R["ssz3"].at[r])
        sent(pz.at[r, pl.ds(0, 7)], R["ssrz1"].at[r])
        sent(gx.at[r, pl.ds(0, 6)], R["ss3"].at[r, 0])
        sent(px.at[r, pl.ds(0, 6)], R["ssr1"].at[r, 0])

        @pl.when(home)
        def _():
            sent(R["rzy"].at[r, pl.ds(0, 3)], R["ssz2"].at[r])
            sent(gx.at[r, pl.ds(0, 3)], R["ss2"].at[r, 0])
            sent(gy.at[r, pl.ds(0, 3)], R["ss2"].at[r, 1])
            sent(sy.at[r, pl.ds(0, 3)], R["ssr2"].at[r, 1])
            sent(gy.at[:, pl.ds(0, 5)], R["ss3"].at[r, 1])

            @pl.when(c == r)
            def _():
                sent(tx.at[r, pl.ds(0, 7)], R["ssr3"].at[r, 0])
                sent(ty.at[r, pl.ds(0, 7)], R["ssr3"].at[r, 1])
                sent(R["tz"].at[r, pl.ds(0, 3)], R["ssrz3"].at[r])

            @pl.when(c != r)
            def _():
                sent(tx.at[r], R["ssr3"].at[r, 0])
                sent(ty.at[r], R["ssr3"].at[r, 1])
                sent(R["tz"].at[r], R["ssrz3"].at[r])

        by_home(
            lambda: sent(py.at[r, pl.ds(0, 4)], R["ssr1"].at[r, 1]),
            lambda: sent(py.at[r], R["ssr1"].at[r, 1]),
        )
        by_home(
            lambda: sent(sx.at[r, 0], R["ssr2"].at[r, 0]),
            lambda: sent(sx.at[r], R["ssr2"].at[r, 0]),
        )
        by_home(
            lambda: sent(pz.at[r, 0, 0], R["ssrz2"].at[r]),
            lambda: sent(pz.at[r, 0], R["ssrz2"].at[r]),
        )

        @pl.when(c == 1 - h)
        def _():
            sent(gy.at[r, pl.ds(0, 2)], R["ss3"].at[r, 1])

    for cp in outs:
        cp.wait()


def copy_out(a, b, d, ao, bo, do, av, bv, dv, sems):
    moves = ((a, av, ao), (b, bv, bo), (d, dv, do))
    loads = [pltpu.make_async_copy(s, v, sems.at[0, i]) for i, (s, v, _) in enumerate(moves)]
    stores = [pltpu.make_async_copy(v, t, sems.at[1, i]) for i, (_, v, t) in enumerate(moves)]
    for cp in loads:
        cp.start()
    for load, store in zip(loads, stores):
        load.wait()
        store.start()
    for cp in stores:
        cp.wait()


def on_device(queries, grad_attended, vision, key_weight, value_weight, tile_limit):
    vmem = pl.BlockSpec(memory_space=pltpu.VMEM)
    hbm = pl.BlockSpec(memory_space=pl.ANY)
    shapes = (
        jax.ShapeDtypeStruct(queries.shape, BF16),
        jax.ShapeDtypeStruct(queries.shape, BF16),
        jax.ShapeDtypeStruct(vision.shape, F32),
    )
    outs = pl.pallas_call(
        kernel,
        out_shape=shapes,
        in_specs=[hbm, hbm, hbm, hbm, hbm, vmem],
        out_specs=(hbm, hbm, hbm),
        scratch_shapes=list(scratch().values()),
        compiler_params=pltpu.CompilerParams(
            collective_id=0, has_side_effects=True, vmem_limit_bytes=60 * 2**20
        ),
        cost_estimate=pl.CostEstimate(flops=6_000_000_000, bytes_accessed=6_000_000, transcendentals=1_000_000),
    )(vision, key_weight, value_weight, queries, grad_attended, tile_limit)
    return pl.pallas_call(
        copy_out,
        out_shape=shapes,
        in_specs=[hbm, hbm, hbm],
        out_specs=(hbm, hbm, hbm),
        scratch_shapes=[pltpu.VMEM(s.shape, s.dtype) for s in shapes] + [pltpu.SemaphoreType.DMA((2, 3))],
    )(*outs)


def solution(mesh):
    return jax.shard_map(
        on_device,
        mesh=mesh,
        in_specs=(
            P("segment", None, "tensor"),
            P("segment", None, "tensor"),
            P("segment", "tensor"),
            P("segment", None, "tensor"),
            P("segment", None, "tensor"),
            P(),
        ),
        out_specs=(
            P("segment", None, "tensor"),
            P("segment", None, "tensor"),
            P("segment", "tensor"),
        ),
        check_vma=False,
    )
```
